32 devices in a mesh: pipe: 2 (over y), batch: 16 (over z, x, core).
Axes of the slice: x: 2, y: 2, z: 4, core: 2. Of those that a mesh axis runs over, the one named last changes fastest.
Arguments:
- inputs: bfloat16 [2, 8192, 768], P(None, 'batch'), may hold values from -6 to 6
- cotangent: bfloat16 [2, 8192, 768], P(None, 'batch'), may hold values from -6 to 6
- lengths: int32 [32], P('batch'), may hold values from 128 to 512, as said below
- assign: int32 [32], P('batch'), may hold values from 0 to 1, as said below
- query_key_value: bfloat16 [2, 768, 2304], P('pipe'), may hold values from -0.3125 to 0.3125
- out_weight: bfloat16 [2, 768, 768], P('pipe'), may hold values from -0.21875 to 0.21875
- up_weight: bfloat16 [2, 768, 3072], P('pipe'), may hold values from -0.21875 to 0.21875
- down_weight: bfloat16 [2, 3072, 768], P('pipe'), may hold values from -0.109375 to 0.109375
- model_gains: float32 [2, 3, 768], P('pipe'), may hold values from 0.5 to 1.5
- model_shifts: float32 [2, 7, 768], P('pipe'), may hold values from -2 to 2
- hidden_gains: float32 [2, 3072], P('pipe'), may hold values from 0.5 to 1.5
- hidden_shifts: float32 [2, 2, 3072], P('pipe'), may hold values from -2 to 2
Outputs:
- section_out: bfloat16 [2, 2, 8192, 768], P('pipe', None, 'batch')
- section_in_grad: bfloat16 [2, 2, 8192, 768], P('pipe', None, 'batch')
- query_key_value_grad: float32 [2, 768, 2304], P('pipe')
- out_weight_grad: float32 [2, 768, 768], P('pipe')
- up_weight_grad: float32 [2, 768, 3072], P('pipe')
- down_weight_grad: float32 [2, 3072, 768], P('pipe')
- model_gains_grad: float32 [2, 3, 768], P('pipe')
- model_shifts_grad: float32 [2, 7, 768], P('pipe')
- hidden_gains_grad: float32 [2, 3072], P('pipe')
- hidden_shifts_grad: float32 [2, 2, 3072], P('pipe')
The draws below stay inside these ranges and needn't reach their ends.
Inputs may be any that keep to these rules, and one draw needn't show every extreme that they name: `lengths`: each device's 2 sequences fit a slot; one sequence of exactly 512 tokens in every draw. `assign`: each device's 2 entries name every micro-batch once.
All inputs are finite; a program needn't handle non-finite values.
Results may differ from the reference program's by a relative error of at most 0.025.
Values may be sent and summed in bfloat16 or wider, within the bound.
A program may use at most 384 MiB of HBM per device.

```python
from functools import partial
import jax
import jax.numpy as jnp
from jax import lax

D = 768
FF = 3072
HEAD = 64
MB = 2
SLOT = 512
MIN_LEN = 128
SEQS = 32
TOKENS = 8192
N_PIPE = 2


def draw_lengths(key, part):
    key = jax.random.fold_in(key, 11)
    first_key, second_key = jax.random.split(key)
    drawn = jax.random.randint(first_key, (SEQS,), MIN_LEN, SLOT + 1)
    longest = jax.random.randint(second_key, (), 0, SEQS)
    return jnp.where(jnp.arange(SEQS) == longest, SLOT, drawn).astype(jnp.int32)


def draw_assign(key, part):
    key = jax.random.fold_in(key, 23)
    ordered = jnp.tile(jnp.arange(MB, dtype=jnp.int32)[None, :], (SEQS // MB, 1))
    shuffled = jax.random.permutation(key, ordered, axis=1, independent=True)
    return shuffled.reshape(SEQS).astype(jnp.int32)


def levels(key, extent, pieces, smallest, largest):
    factor_of = 1.0
    for axis_at, blocks in pieces:
        draws = jax.random.uniform(jax.random.fold_in(jax.random.fold_in(key, 6), axis_at), (blocks,), jnp.float32, smallest / len(pieces), largest / len(pieces))
        factor_of = factor_of * jnp.repeat(jnp.exp(draws), extent[axis_at] // blocks).reshape((-1,) + (1,) * (len(extent) - 1 - axis_at))
    return factor_of


def noise(rng, shape, width, bound, cuts=(), held_as=jnp.bfloat16):
    result = jax.random.normal(rng, shape, jnp.float32) * width
    if len(cuts) > 0:
        result = levels(rng, shape, cuts, -0.22, 0.18) * result
    return jnp.clip(result, min=-bound, max=bound).astype(held_as)


def setup_inputs(seed: int = 0) -> dict:
    seeds = jax.random.split(jax.random.key(seed), 13)
    return {
        "inputs": noise(seeds[0], (MB, TOKENS, D), 1.0, 6.0, ((1, 16),)),
        "cotangent": noise(seeds[1], (MB, TOKENS, D), 1.0, 6.0, ((1, 16),)),
        "lengths": draw_lengths(jax.random.fold_in(seeds[12], 71), 0),
        "assign": draw_assign(jax.random.fold_in(seeds[12], 71), 0),
        "query_key_value": noise(seeds[4], (N_PIPE, D, 3 * D), (D // 2) ** -0.5, 0.3125, ((0, 2),)),
        "out_weight": noise(seeds[5], (N_PIPE, D, D), D ** -0.5, 0.21875, ((0, 2),)),
        "up_weight": noise(seeds[6], (N_PIPE, D, FF), D ** -0.5, 0.21875, ((0, 2),)),
        "down_weight": noise(seeds[7], (N_PIPE, FF, D), FF ** -0.5, 0.109375, ((0, 2),)),
        "model_gains": jnp.clip(1.0 + 0.1 * jax.random.normal(seeds[8], (N_PIPE, 3, D), jnp.float32), 0.5, 1.5),
        "model_shifts": noise(seeds[9], (N_PIPE, 7, D), 0.5, 2.0, ((0, 2),), jnp.float32),
        "hidden_gains": jnp.clip(1.0 + 0.1 * jax.random.normal(seeds[10], (N_PIPE, FF), jnp.float32), 0.5, 1.5),
        "hidden_shifts": noise(seeds[11], (N_PIPE, 2, FF), 0.5, 2.0, ((0, 2),), jnp.float32),
    }


@jax.custom_vjp
def low(v):
    return lax.optimization_barrier(v.astype(jnp.bfloat16)).astype(jnp.float32)

@jax.custom_vjp
def low_back(v):
    return v

def low_keep(v):
    return (low(v), None)

def low_pass(kept, grad):
    return (grad,)

def back_keep(v):
    return (v, None)

def back_low(kept, grad):
    return (low(grad),)
low.defvjp(low_keep, low_pass)
low_back.defvjp(back_keep, back_low)
EPSILON = 1e-05
SCALE = 0.125
HIGHEST = lax.Precision.HIGHEST

def product(left, right):
    return jnp.dot(left, right, precision=HIGHEST)

def normalize(values_in, gain, shift):
    centred = values_in - lax.optimization_barrier(jnp.mean(values_in, axis=-1, keepdims=True))
    variance = lax.optimization_barrier(jnp.mean(centred * centred, axis=-1, keepdims=True))
    return centred * lax.rsqrt(variance + EPSILON) * gain + shift

def gelu_exact(values_in):
    return 0.5 * values_in * (1.0 + lax.erf(values_in * 0.7071067811865476))

def visible_mask(start, block_rows, row_count, length):
    query_pos = start + jnp.arange(block_rows, dtype=jnp.int32)[:, None]
    key_pos = jnp.arange(row_count, dtype=jnp.int32)[None, :]
    return (key_pos <= query_pos) & ((key_pos < length) | (key_pos == query_pos))

def attend(queries, key_part, value_part, length):
    row_count = queries.shape[0]
    head_count = queries.shape[1] // HEAD
    block_rows = min(512, row_count)
    key_heads = key_part.reshape(row_count, head_count, HEAD)
    value_heads = value_part.reshape(row_count, head_count, HEAD)

    def one_block(start):
        query_block = lax.dynamic_slice_in_dim(queries, start, block_rows, 0).reshape(block_rows, head_count, HEAD)
        scores = jnp.einsum('qhd,khd->hqk', query_block, key_heads, precision=HIGHEST) * SCALE
        allowed = visible_mask(start, block_rows, row_count, length)
        scores = low_back(jnp.where(allowed[None], scores, -1e+30))
        row_max = lax.optimization_barrier(jnp.max(scores, axis=-1, keepdims=True))
        exps = jnp.exp(scores - row_max)
        probabilities = low(exps / lax.optimization_barrier(jnp.sum(exps, axis=-1, keepdims=True)))
        attended = jnp.einsum('hqk,khd->qhd', probabilities, value_heads, precision=HIGHEST)
        return attended.reshape(block_rows, head_count * HEAD)
    starts = jnp.arange(row_count // block_rows, dtype=jnp.int32) * block_rows
    return lax.map(jax.checkpoint(one_block), starts).reshape(row_count, head_count * HEAD)

def one_layer(features, qkv_weight, out_matrix, up_matrix, down_matrix, gains_model, shifts_model, gains_hidden, shifts_hidden, length):
    model_width = features.shape[1]
    normed_in = low(normalize(features, gains_model[0], shifts_model[0]))
    input_bias = jnp.concatenate([shifts_model[1], jnp.zeros_like(shifts_model[1]), shifts_model[2]])
    projected = low_back(low(product(normed_in, qkv_weight) + input_bias))
    attended = low_back(attend(projected[:, :model_width], projected[:, model_width:2 * model_width], projected[:, 2 * model_width:], length))
    normed_mix = low(normalize(attended, gains_model[1], shifts_model[3]))
    residual = features + low_back(product(normed_mix, out_matrix) + shifts_model[4])
    normed_ffn = low(normalize(residual, gains_model[2], shifts_model[5]))
    pre_act = low_back(product(normed_ffn, up_matrix) + shifts_hidden[0])
    normed_hidden = low(normalize(gelu_exact(pre_act), gains_hidden, shifts_hidden[1]))
    return residual + low_back(product(normed_hidden, down_matrix) + shifts_model[6])

def network(features, zero_pad, params, length):
    lower_out = one_layer(features, *[item[0] for item in params], length)
    middle = low_back(low(lower_out)) + zero_pad
    upper_out = one_layer(middle, *[item[1] for item in params], length)
    return (lower_out, upper_out)

def reference(inputs, cotangent, lengths, assign, query_key_value, out_weight, up_weight, down_weight, model_gains, model_shifts, hidden_gains, hidden_shifts):
    micro_count = inputs.shape[0]
    model_width = inputs.shape[2]
    device_count = lengths.shape[0] // micro_count
    seq_len = lengths.reshape(device_count, micro_count)
    seq_micro = assign.reshape(device_count, micro_count)
    owners = seq_micro[:, :, None] == jnp.arange(micro_count, dtype=jnp.int32)[None, None, :]
    slot_len = lax.optimization_barrier(jnp.sum(jnp.where(owners, seq_len[:, :, None], 0), axis=1))
    slot_len = slot_len.T.reshape(micro_count * device_count).astype(jnp.int32)
    slot_inputs = inputs.reshape(micro_count * device_count, SLOT, model_width)
    slot_grads = cotangent.reshape(micro_count * device_count, SLOT, model_width)
    weights = tuple((item.astype(jnp.float32) for item in (query_key_value, out_weight, up_weight, down_weight, model_gains, model_shifts, hidden_gains, hidden_shifts)))

    def slot_step(totals, slot_items):
        features, upstream, length = slot_items
        features = features.astype(jnp.float32)
        zero_pad = jnp.zeros_like(features)
        (lower_out, upper_out), pullback = jax.vjp(partial(network, length=length), features, zero_pad, weights)
        live_rows = (jnp.arange(SLOT, dtype=jnp.int32) < length).astype(jnp.float32)[:, None]
        d_input, d_middle, d_params = pullback((jnp.zeros_like(lower_out), upstream.astype(jnp.float32) * live_rows))
        totals = tuple((left + right for left, right in zip(totals, d_params)))
        return (totals, (lower_out.astype(jnp.bfloat16), upper_out.astype(jnp.bfloat16), d_input.astype(jnp.bfloat16), d_middle.astype(jnp.bfloat16)))
    initial = tuple((jnp.zeros_like(item) for item in weights))
    totals, (lower_all, upper_all, input_grads, middle_grads) = lax.scan(slot_step, initial, (slot_inputs, slot_grads, slot_len))
    out_shape = (micro_count, device_count * SLOT, model_width)
    section_out = jnp.stack([lower_all.reshape(out_shape), upper_all.reshape(out_shape)])
    section_in_grad = jnp.stack([input_grads.reshape(out_shape), middle_grads.reshape(out_shape)])
    return (section_out, section_in_grad, totals[0], totals[1], totals[2], totals[3], totals[4], totals[5], totals[6], totals[7])
```

```python
import functools

import jax
import jax.numpy as jnp
from jax import lax
from jax.experimental import pallas as pl
from jax.experimental.pallas import tpu as pltpu
from jax.sharding import PartitionSpec as P

HEAD = 64
PAIR = 2 * HEAD
EPSILON = 1e-05
SCALE = 0.125
HIDDEN_NEG = -1e30
CHUNK = 512
SUM_ROWS = 32
TILE = 16
VMEM_BYTES = 56 * 1024 * 1024
MESH_IDS = pl.DeviceIdType.MESH


def dot_nn(left, right):
    return jnp.dot(left, right, preferred_element_type=jnp.float32)


def dot_nt(left, right):
    return lax.dot_general(
        left, right, (((1,), (1,)), ((), ())), preferred_element_type=jnp.float32
    )


def dot_tn(left, right):
    return lax.dot_general(
        left, right, (((0,), (0,)), ((), ())), preferred_element_type=jnp.float32
    )


def standardize(values_in):
    centred = values_in - jnp.mean(values_in, axis=-1, keepdims=True)
    scale = lax.rsqrt(jnp.mean(centred * centred, axis=-1, keepdims=True) + EPSILON)
    return centred * scale, scale


def row_blocks(total, size, body):
    def one(index, carry):
        body(pl.ds(pl.multiple_of(index * size, size), size))
        return carry

    lax.fori_loop(0, total // size, one, 0)


FWD_STATE = ("normed_in", "projected", "log_total", "attended", "normed_mix", "residual",
             "normed_ffn", "normed_hidden", "slope", "spread")


def state_shapes(rows, width, hidden):
    bf, f = jnp.bfloat16, jnp.float32
    return {
        "normed_in": ((rows, width), bf),
        "projected": ((rows, 3 * width), bf),
        "log_total": ((PAIR, rows), f),
        "attended": ((rows, width), f),
        "normed_mix": ((rows, width), bf),
        "residual": ((rows, width), f),
        "normed_ffn": ((rows, width), bf),
        "normed_hidden": ((rows, hidden), bf),
        "slope": ((rows, hidden), bf),
        "spread": ((rows, PAIR), f),
    }


def forward_kernel(
    aliased, flag_ref, length_ref, x_hbm, wq_hbm, wo_hbm, wu_hbm, wd_hbm, gm, sm, gh, sh, *refs
):
    count = 1 + len(FWD_STATE)
    if aliased:
        refs = refs[count:]
    outs, scratch = refs[:count], refs[count:]
    y_hbm, state_hbm = outs[0], dict(zip(FWD_STATE, outs[1:]))
    (x_s, wq, wo, wu, wd, y_s) = scratch[:6]
    held = dict(zip(FWD_STATE, scratch[6 : 6 + len(FWD_STATE)]))
    (act_s, bias_s, in_sem, out_sem) = scratch[6 + len(FWD_STATE) :]
    rows, width = x_s.shape
    hidden = wu.shape[1]
    heads = width // HEAD

    @pl.when(flag_ref[0] == 1)
    def _():
        loads = [
            pltpu.make_async_copy(source, target, in_sem.at[at])
            for at, (source, target) in enumerate(
                [(x_hbm, x_s), (wq_hbm, wq), (wo_hbm, wo), (wu_hbm, wu), (wd_hbm, wd)]
            )
        ]
        for item in loads:
            item.start()
        stores = {
            name: pltpu.make_async_copy(held[name], state_hbm[name], out_sem.at[at])
            for at, name in enumerate(FWD_STATE)
        }
        store_y = pltpu.make_async_copy(y_s, y_hbm, out_sem.at[len(FWD_STATE)])

        length = length_ref[0]
        query = lax.broadcasted_iota(jnp.int32, (rows, rows), 0)
        key = lax.broadcasted_iota(jnp.int32, (rows, rows), 1)
        visible = (key <= query) & ((key < length) | (key == query))
        bias_s[...] = jnp.where(visible, 0.0, HIDDEN_NEG)

        loads[0].wait()
        loads[1].wait()

        def project(at):
            unit, unused = standardize(x_s[at, :].astype(jnp.float32))
            normed = (unit * gm[0:1, :] + sm[0:1, :]).astype(jnp.bfloat16)
            held["normed_in"][at, :] = normed
            for block in range(3):
                cols = pl.ds(block * width, width)
                out = dot_nn(normed, wq[:, cols])
                if block != 1:
                    out = out + sm[1 + block // 2 : 2 + block // 2, :]
                held["projected"][at, cols] = out.astype(jnp.bfloat16)

        project(slice(None))
        stores["normed_in"].start()
        stores["projected"].start()

        half = rows // 2
        lane = lax.broadcasted_iota(jnp.int32, (half, PAIR), 1)

        def attend(pair, totals):
            first = pl.multiple_of(pair * PAIR, PAIR)
            new_totals = []
            for block in range(2):
                at = pl.ds(block * half, half)
                reach = (block + 1) * half
                q = held["projected"][at, pl.ds(first, PAIR)] * jnp.bfloat16(SCALE)
                k = held["projected"][0:reach, pl.ds(width + first, PAIR)]
                v = held["projected"][0:reach, pl.ds(2 * width + first, PAIR)]
                mixed = []
                total = totals[block]
                for which in range(2):
                    mine = (lane >= HEAD) if which else (lane < HEAD)
                    scores = dot_nt(jnp.where(mine, q, jnp.zeros_like(q)), k)
                    scores = scores + bias_s[at, 0:reach]
                    top = jnp.max(scores, axis=-1, keepdims=True)
                    exps = jnp.exp(scores - top)
                    row_sum = jnp.sum(exps, axis=-1, keepdims=True)
                    out = dot_nn(exps.astype(jnp.bfloat16), v)
                    mixed.append(out * (1.0 / row_sum))
                    total = jnp.where(lane == 2 * pair + which, top + jnp.log(row_sum), total)
                held["attended"][at, pl.ds(first, PAIR)] = jnp.where(
                    lane < HEAD, mixed[0], mixed[1]
                )
                new_totals.append(total)
            return tuple(new_totals)

        zero = jnp.zeros((half, PAIR), jnp.float32)
        totals = lax.fori_loop(0, heads // 2, attend, (zero, zero))
        for block in range(2):
            held["log_total"][:, block * half : (block + 1) * half] = totals[block].T
        stores["log_total"].start()
        stores["attended"].start()

        loads[2].wait()

        unit, unused = standardize(held["attended"][...])
        normed_mix = (unit * gm[1:2, :] + sm[3:4, :]).astype(jnp.bfloat16)
        held["normed_mix"][...] = normed_mix
        stores["normed_mix"].start()
        residual = x_s[...].astype(jnp.float32) + dot_nn(normed_mix, wo[...]) + sm[4:5, :]
        held["residual"][...] = residual
        stores["residual"].start()
        unit, unused = standardize(residual)
        normed_ffn = (unit * gm[2:3, :] + sm[5:6, :]).astype(jnp.bfloat16)
        held["normed_ffn"][...] = normed_ffn
        stores["normed_ffn"].start()
        loads[3].wait()
        total = jnp.zeros((rows, 1), jnp.float32)
        for first in range(0, hidden, CHUNK):
            cols = slice(first, first + CHUNK)
            pre = dot_nn(held["normed_ffn"][...], wu[:, cols]) + sh[0:1, cols]
            share = 0.5 + 0.5 * lax.erf(pre * 0.7071067811865476)
            density = 0.3989422804014327 * jnp.exp(-0.5 * pre * pre)
            act = pre * share
            held["slope"][:, cols] = (share + pre * density).astype(jnp.bfloat16)
            act_s[:, cols] = act
            total = total + jnp.sum(act, axis=-1, keepdims=True)
        stores["slope"].start()
        mean = total * (1.0 / hidden)
        square = jnp.zeros((rows, 1), jnp.float32)
        for first in range(0, hidden, CHUNK):
            centred = act_s[:, first : first + CHUNK] - mean
            square = square + jnp.sum(centred * centred, axis=-1, keepdims=True)
        scale = lax.rsqrt(square * (1.0 / hidden) + EPSILON)
        held["spread"][...] = jnp.broadcast_to(scale, (rows, PAIR))
        stores["spread"].start()
        for first in range(0, hidden, CHUNK):
            cols = slice(first, first + CHUNK)
            unit = (act_s[:, cols] - mean) * scale
            held["normed_hidden"][:, cols] = (
                unit * gh[0:1, cols] + sh[1:2, cols]
            ).astype(jnp.bfloat16)
        stores["normed_hidden"].start()
        loads[4].wait()
        out = held["residual"][...] + dot_nn(held["normed_hidden"][...], wd[...]) + sm[6:7, :]
        y_s[...] = out.astype(jnp.bfloat16)
        store_y.start()
        for name in FWD_STATE:
            stores[name].wait()
        store_y.wait()


def forward_call(flag, length, x, weights, previous=None):
    wq, wo, wu, wd, gm, sm, gh, sh = weights
    rows, width = x.shape
    hidden = wu.shape[1]
    shapes = state_shapes(rows, width, hidden)
    out_shape = [jax.ShapeDtypeStruct((rows, width), jnp.bfloat16)]
    out_shape += [jax.ShapeDtypeStruct(*shapes[name]) for name in FWD_STATE]
    any_spec = pl.BlockSpec(memory_space=pl.ANY)
    vmem_spec = pl.BlockSpec(memory_space=pltpu.VMEM)
    smem_spec = pl.BlockSpec(memory_space=pltpu.SMEM)
    in_specs = [smem_spec] * 2 + [any_spec] * 5 + [vmem_spec] * 4
    args = [flag, length, x, wq, wo, wu, wd, gm, sm, gh, sh]
    aliases = {}
    if previous is not None:
        aliases = {len(args) + at: at for at in range(len(previous))}
        in_specs += [any_spec] * len(previous)
        args += list(previous)
    bf = jnp.bfloat16
    scratch = [pltpu.VMEM(item.shape, bf) for item in (x, wq, wo, wu, wd, x)]
    scratch += [pltpu.VMEM(*shapes[name]) for name in FWD_STATE]
    scratch += [
        pltpu.VMEM((rows, hidden), jnp.float32),
        pltpu.VMEM((rows, rows), jnp.float32),
        pltpu.SemaphoreType.DMA((5,)),
        pltpu.SemaphoreType.DMA((len(FWD_STATE) + 1,)),
    ]
    return pl.pallas_call(
        functools.partial(forward_kernel, previous is not None),
        out_shape=out_shape,
        in_specs=in_specs,
        out_specs=[any_spec] * len(out_shape),
        input_output_aliases=aliases,
        scratch_shapes=scratch,
        compiler_params=pltpu.CompilerParams(vmem_limit_bytes=VMEM_BYTES),
        cost_estimate=pl.CostEstimate(
            flops=2 * rows * width * (3 * width + width + 2 * hidden),
            bytes_accessed=40_000_000,
            transcendentals=0,
        ),
    )(*args)


BWD_STATE = ("d_down", "d_pre", "d_branch", "d_proj", "sums")


def backward_shapes(rows, width, hidden):
    bf = jnp.bfloat16
    return {
        "d_down": ((rows, width), bf),
        "d_pre": ((rows, hidden), bf),
        "d_branch": ((rows, width), bf),
        "d_proj": ((rows, 3 * width), bf),
        "sums": ((SUM_ROWS, width), jnp.float32),
    }


def unit_backward(grad, unit, scale, gain):
    scaled = grad * gain
    first = jnp.mean(scaled, axis=-1, keepdims=True)
    second = jnp.mean(scaled * unit, axis=-1, keepdims=True)
    return (
        scale * (scaled - first - unit * second),
        jnp.sum(grad * unit, axis=0, keepdims=True),
        jnp.sum(grad, axis=0, keepdims=True),
    )


def column_sum(values):
    return jnp.sum(values.astype(jnp.float32), axis=0, keepdims=True)


def backward_kernel(
    aliased, masked, flag_ref, length_ref, dy_hbm, x_hbm, wq_hbm, wo_hbm, wu_hbm, wd_hbm, gm, sm,
    gh, sh, projected_hbm, log_total_hbm, attended_hbm, residual_hbm, normed_hidden_hbm, slope_hbm,
    spread_hbm, *refs
):
    count = 1 + len(BWD_STATE)
    if aliased:
        refs = refs[count:]
    outs, scratch = refs[:count], refs[count:]
    dx_hbm, out_hbm = outs[0], dict(zip(BWD_STATE, outs[1:]))
    (dy_s, x_s, wq, wo, wu, wd, projected, log_total, attended, residual, normed_hidden, slope,
     spread, dx_s) = scratch[:14]
    held = dict(zip(BWD_STATE, scratch[14 : 14 + len(BWD_STATE)]))
    (e_s, d_residual, d_attended, delta_s, bias_s, in_sem, out_sem) = scratch[14 + len(BWD_STATE) :]
    rows, width = dx_s.shape
    hidden = wu.shape[1]
    heads = width // HEAD
    wide = hidden // width

    @pl.when(flag_ref[0] == 1)
    def _():
        order = [
            (dy_hbm, dy_s), (wd_hbm, wd), (normed_hidden_hbm, normed_hidden),
            (slope_hbm, slope), (spread_hbm, spread), (wu_hbm, wu), (residual_hbm, residual),
            (wo_hbm, wo), (attended_hbm, attended), (projected_hbm, projected),
            (log_total_hbm, log_total), (wq_hbm, wq), (x_hbm, x_s),
        ]
        loads = [
            pltpu.make_async_copy(source, target, in_sem.at[at])
            for at, (source, target) in enumerate(order)
        ]
        for item in loads:
            item.start()
        stores = {
            name: pltpu.make_async_copy(held[name], out_hbm[name], out_sem.at[at])
            for at, name in enumerate(BWD_STATE)
        }
        store_dx = pltpu.make_async_copy(dx_s, dx_hbm, out_sem.at[len(BWD_STATE)])
        sums = held["sums"]
        sums[...] = jnp.zeros_like(sums)

        length = length_ref[0]
        query = lax.broadcasted_iota(jnp.int32, (rows, rows), 1)
        key = lax.broadcasted_iota(jnp.int32, (rows, rows), 0)
        visible = (key <= query) & ((key < length) | (key == query))
        bias_s[...] = jnp.where(visible, 0.0, HIDDEN_NEG)

        loads[0].wait()
        if masked:
            live = lax.broadcasted_iota(jnp.int32, (rows, 1), 0) < length
            dy_s[...] = jnp.where(live, dy_s[...].astype(jnp.float32), 0.0).astype(jnp.bfloat16)
        held["d_down"][...] = dy_s[...]
        stores["d_down"].start()
        sums[9:10, :] = column_sum(dy_s[...])
        for item in loads[1:5]:
            item.wait()

        scale = spread[:, 0:1]
        first_total = jnp.zeros((rows, 1), jnp.float32)
        second_total = jnp.zeros((rows, 1), jnp.float32)
        for block in range(wide):
            cols = slice(block * width, (block + 1) * width)
            grad = dot_nt(dy_s[...], wd[cols, :])
            unit = (normed_hidden[:, cols].astype(jnp.float32) - sh[1:2, cols]) * gh[1:2, cols]
            sums[10 + block : 11 + block, :] = jnp.sum(grad * unit, axis=0, keepdims=True)
            sums[18 + block : 19 + block, :] = jnp.sum(grad, axis=0, keepdims=True)
            scaled = grad * gh[0:1, cols]
            e_s[:, cols] = scaled
            first_total = first_total + jnp.sum(scaled, axis=-1, keepdims=True)
            second_total = second_total + jnp.sum(scaled * unit, axis=-1, keepdims=True)
        first_mean = first_total * (1.0 / hidden)
        second_mean = second_total * (1.0 / hidden)
        for block in range(wide):
            cols = slice(block * width, (block + 1) * width)
            unit = (normed_hidden[:, cols].astype(jnp.float32) - sh[1:2, cols]) * gh[1:2, cols]
            d_act = scale * (e_s[:, cols] - first_mean - unit * second_mean)
            d_pre = (d_act * slope[:, cols].astype(jnp.float32)).astype(jnp.bfloat16)
            held["d_pre"][:, cols] = d_pre
            sums[14 + block : 15 + block, :] = column_sum(d_pre)
        stores["d_pre"].start()

        loads[5].wait()
        loads[6].wait()
        d_ffn = dot_nt(held["d_pre"][...], wu[...])
        unit, scale = standardize(residual[...])
        through, gain_sum, shift_sum = unit_backward(d_ffn, unit, scale, gm[2:3, :])
        sums[2:3, :] = gain_sum
        sums[8:9, :] = shift_sum
        through = through + dy_s[...].astype(jnp.float32)
        d_residual[...] = through
        held["d_branch"][...] = through.astype(jnp.bfloat16)
        stores["d_branch"].start()
        sums[7:8, :] = column_sum(held["d_branch"][...])

        loads[7].wait()
        loads[8].wait()
        d_mix = dot_nt(held["d_branch"][...], wo[...])
        unit, scale = standardize(attended[...])
        through, gain_sum, shift_sum = unit_backward(d_mix, unit, scale, gm[1:2, :])
        sums[1:2, :] = gain_sum
        sums[6:7, :] = shift_sum
        d_attended[...] = through.astype(jnp.bfloat16)
        product = d_attended[...].astype(jnp.float32) * attended[...]
        upper = product.astype(jnp.bfloat16)
        lower = (product - upper.astype(jnp.float32)).astype(jnp.bfloat16)
        head_row = lax.broadcasted_iota(jnp.int32, (16, width), 0)
        head_col = lax.broadcasted_iota(jnp.int32, (16, width), 1) // HEAD
        chooser = jnp.where(head_row == head_col, 1.0, 0.0).astype(jnp.bfloat16)
        delta_s[...] = dot_nt(chooser, upper) + dot_nt(chooser, lower)

        loads[9].wait()
        loads[10].wait()
        half = rows // 2
        lane = lax.broadcasted_iota(jnp.int32, (half, PAIR), 1)
        spot = lax.broadcasted_iota(jnp.int32, (PAIR, rows), 0)

        def attend(pair, carry):
            first = pl.multiple_of(pair * PAIR, PAIR)
            k_all = projected[:, pl.ds(width + first, PAIR)]
            v_all = projected[:, pl.ds(2 * width + first, PAIR)]
            k_turned = k_all.T
            dk = [None, None]
            dv = [None, None]
            for block in range(2):
                at = slice(block * half, (block + 1) * half)
                reach = (block + 1) * half
                q = projected[at, pl.ds(first, PAIR)] * jnp.bfloat16(SCALE)
                grad = d_attended[at, pl.ds(first, PAIR)]
                dq_turned = None
                for which in range(2):
                    mine = (lane >= HEAD) if which else (lane < HEAD)
                    own = (spot >= HEAD) if which else (spot < HEAD)
                    q_own = jnp.where(mine, q, jnp.zeros_like(q))
                    grad_own = jnp.where(mine, grad, jnp.zeros_like(grad))
                    scores = dot_nt(k_all[0:reach], q_own) + bias_s[0:reach, at]
                    head = pl.ds(2 * pair + which, 1)
                    probs = jnp.exp(scores - log_total[head, at])
                    d_probs = dot_nt(v_all[0:reach], grad_own)
                    d_scores = (probs * (d_probs - delta_s[head, at])).astype(jnp.bfloat16)
                    more_v = dot_nn(probs.astype(jnp.bfloat16), grad_own)
                    more_k = dot_nn(d_scores, q_own)
                    for part in range(block + 1):
                        piece = slice(part * half, (part + 1) * half)
                        dv[part] = more_v[piece] if dv[part] is None else dv[part] + more_v[piece]
                        dk[part] = more_k[piece] if dk[part] is None else dk[part] + more_k[piece]
                    k_own = jnp.where(own, k_turned, jnp.zeros_like(k_turned))[:, 0:reach]
                    more_q = dot_nn(k_own, d_scores)
                    dq_turned = more_q if dq_turned is None else dq_turned + more_q
                held["d_proj"][at, pl.ds(first, PAIR)] = (dq_turned.T * SCALE).astype(jnp.bfloat16)
            for part in range(2):
                at = slice(part * half, (part + 1) * half)
                held["d_proj"][at, pl.ds(width + first, PAIR)] = dk[part].astype(jnp.bfloat16)
                held["d_proj"][at, pl.ds(2 * width + first, PAIR)] = dv[part].astype(jnp.bfloat16)
            return carry

        lax.fori_loop(0, heads // 2, attend, 0)
        stores["d_proj"].start()

        loads[11].wait()
        loads[12].wait()
        d_norm = dot_nt(held["d_proj"][...], wq[...])
        sums[4:5, :] = column_sum(held["d_proj"][:, 0:width])
        sums[5:6, :] = column_sum(held["d_proj"][:, 2 * width :])
        unit, scale = standardize(x_s[...].astype(jnp.float32))
        through, gain_sum, shift_sum = unit_backward(d_norm, unit, scale, gm[0:1, :])
        sums[0:1, :] = gain_sum
        sums[3:4, :] = shift_sum
        dx_s[...] = (through + d_residual[...]).astype(jnp.bfloat16)
        store_dx.start()
        stores["sums"].start()
        for name in BWD_STATE:
            stores[name].wait()
        store_dx.wait()


def backward_call(flag, length, dy, x, weights, state, masked, previous=None):
    wq, wo, wu, wd, gm, sm, gh, sh = weights
    rows, width = x.shape
    hidden = wu.shape[1]
    shapes = backward_shapes(rows, width, hidden)
    bf = jnp.bfloat16
    out_shape = [jax.ShapeDtypeStruct((rows, width), bf)]
    out_shape += [jax.ShapeDtypeStruct(*shapes[name]) for name in BWD_STATE]
    any_spec = pl.BlockSpec(memory_space=pl.ANY)
    vmem_spec = pl.BlockSpec(memory_space=pltpu.VMEM)
    smem_spec = pl.BlockSpec(memory_space=pltpu.SMEM)
    kept = [state[name] for name in ("projected", "log_total", "attended", "residual",
                                     "normed_hidden", "slope", "spread")]
    in_specs = [smem_spec] * 2 + [any_spec] * 6 + [vmem_spec] * 4 + [any_spec] * len(kept)
    args = [flag, length, dy, x, wq, wo, wu, wd, gm, sm, gh, sh] + kept
    aliases = {}
    if previous is not None:
        aliases = {len(args) + at: at for at in range(len(previous))}
        in_specs += [any_spec] * len(previous)
        args += list(previous)
    scratch = [pltpu.VMEM(item.shape, item.dtype) for item in [dy, x, wq, wo, wu, wd] + kept + [x]]
    scratch += [pltpu.VMEM(*shapes[name]) for name in BWD_STATE]
    scratch += [
        pltpu.VMEM((rows, hidden), jnp.float32),
        pltpu.VMEM((rows, width), jnp.float32),
        pltpu.VMEM((rows, width), bf),
        pltpu.VMEM((16, rows), jnp.float32),
        pltpu.VMEM((rows, rows), jnp.float32),
        pltpu.SemaphoreType.DMA((13,)),
        pltpu.SemaphoreType.DMA((len(BWD_STATE) + 1,)),
    ]
    return pl.pallas_call(
        functools.partial(backward_kernel, previous is not None, masked),
        out_shape=out_shape,
        in_specs=in_specs,
        out_specs=[any_spec] * len(out_shape),
        input_output_aliases=aliases,
        scratch_shapes=scratch,
        compiler_params=pltpu.CompilerParams(vmem_limit_bytes=VMEM_BYTES),
        cost_estimate=pl.CostEstimate(
            flops=2 * rows * width * (3 * width + width + 2 * hidden),
            bytes_accessed=40_000_000,
            transcendentals=0,
        ),
    )(*args)


LEFT = ("normed_hidden", "normed_ffn", "normed_mix", "normed_in")
RIGHT = ("d_down", "d_pre", "d_branch", "d_proj")


def weight_grad_kernel(micro_count, *refs):
    parts = len(LEFT)
    sources = [refs[slot * 9 : slot * 9 + 9] for slot in range(micro_count)]
    out_hbm = refs[micro_count * 9]
    scratch = refs[micro_count * 9 + 1 :]
    left, right = scratch[0:parts], scratch[parts : 2 * parts]
    sums, out_s, turned, in_sem, out_sem = scratch[2 * parts :]
    tokens, width = left[3].shape
    rows = tokens // micro_count
    hidden = left[0].shape[1]
    wide = hidden // width
    loads = []
    for part in range(parts):
        for slot in range(micro_count):
            at = pl.ds(slot * rows, rows)
            for side, target in ((0, left[part]), (parts, right[part])):
                loads.append(
                    pltpu.make_async_copy(
                        sources[slot][side + part], target.at[at], in_sem.at[len(loads)]
                    )
                )
    for slot in range(micro_count):
        loads.append(
            pltpu.make_async_copy(sources[slot][2 * parts], sums.at[slot], in_sem.at[len(loads)])
        )
    for item in loads:
        item.start()
    starts = {"normed_in": 0, "normed_mix": 3, "normed_ffn": 4, "normed_hidden": 4 + wide}
    stores = []

    def store(first, count):
        at = pl.ds(first, count)
        stores.append(pltpu.make_async_copy(out_s.at[at], out_hbm.at[at], out_sem.at[len(stores)]))
        stores[-1].start()

    for part, name in enumerate(LEFT):
        for item in loads[2 * micro_count * part : 2 * micro_count * (part + 1)]:
            item.wait()
        first = starts[name] * width
        if name == "normed_hidden":

            def one(block, carry):
                cols = pl.ds(pl.multiple_of(block * width, width), width)
                turned[...] = left[part][:, cols].T
                at = pl.ds(pl.multiple_of(first + block * width, width), width)
                out_s[at, :] = dot_nn(turned[...], right[part][...]).astype(jnp.bfloat16)
                return carry

            lax.fori_loop(0, wide, one, 0)
            store(first, wide * width)
        else:
            turned[...] = left[part][...].T
            blocks = right[part].shape[1] // width

            def one(block, carry):
                cols = pl.ds(pl.multiple_of(block * width, width), width)
                at = pl.ds(pl.multiple_of(first + block * width, width), width)
                out_s[at, :] = dot_nn(turned[...], right[part][:, cols]).astype(jnp.bfloat16)
                return carry

            lax.fori_loop(0, blocks, one, 0)
            store(first, blocks * width)
    for item in loads[2 * micro_count * parts :]:
        item.wait()
    total = sums[0]
    for slot in range(1, micro_count):
        total = total + sums[slot]
    first = (4 + 2 * wide) * width
    out_s[first : first + SUM_ROWS, :] = total.astype(jnp.bfloat16)
    rest = out_s.shape[0] - first - SUM_ROWS
    if rest:
        out_s[first + SUM_ROWS :, :] = jnp.zeros((rest, width), jnp.bfloat16)
    store(first, SUM_ROWS + rest)
    for item in stores:
        item.wait()


def weight_grads(forward_states, backward_states, devices):
    micro_count = len(forward_states)
    args = []
    for kept, grads in zip(forward_states, backward_states):
        args += [kept[name] for name in LEFT] + [grads[name] for name in RIGHT] + [grads["sums"]]
    rows, width = forward_states[0]["normed_in"].shape
    hidden = forward_states[0]["normed_hidden"].shape[1]
    used = (4 + 2 * hidden // width) * width + SUM_ROWS
    unit = TILE * devices
    total_rows = used + -used % unit
    bf = jnp.bfloat16
    any_spec = pl.BlockSpec(memory_space=pl.ANY)
    scratch = [pltpu.VMEM((micro_count * rows, item.shape[1]), bf) for item in args[:8]]
    scratch += [
        pltpu.VMEM((micro_count, SUM_ROWS, width), jnp.float32),
        pltpu.VMEM((total_rows, width), bf),
        pltpu.VMEM((width, micro_count * rows), bf),
        pltpu.SemaphoreType.DMA((len(args),)),
        pltpu.SemaphoreType.DMA((5,)),
    ]
    return pl.pallas_call(
        functools.partial(weight_grad_kernel, micro_count),
        out_shape=jax.ShapeDtypeStruct((total_rows, width), bf),
        in_specs=[any_spec] * len(args),
        out_specs=any_spec,
        scratch_shapes=scratch,
        compiler_params=pltpu.CompilerParams(vmem_limit_bytes=VMEM_BYTES),
        cost_estimate=pl.CostEstimate(
            flops=2 * micro_count * rows * used * width,
            bytes_accessed=40_000_000,
            transcendentals=0,
        ),
    )(*args)


def ring_sum_kernel(
    chips,
    lanes,
    part_ref,
    sum_ref,
    held,
    from_core,
    arriving,
    final,
    load_sem,
    core_send,
    core_recv,
    ring_send,
    ring_recv,
    spread_send,
    spread_recv,
    cross_send,
    cross_recv,
    store_sem,
):
    line_len = chips // 2
    pipe = lax.axis_index("pipe")
    batch = lax.axis_index("batch")
    core = batch % 2
    side = (batch // 2) % 2
    line = batch // 4
    place = line * (1 - side) + (chips - 1 - line) * side

    def chip_at(spot):
        far = spot // line_len
        along = spot * (1 - far) + (chips - 1 - spot) * far
        return (pipe, (along * 2 + far) * 2 + core)

    onward = chip_at((place + 1) % chips)
    backward = chip_at((place + chips - 1) % chips)
    twin = (pipe, batch + 1 - 2 * core)

    barrier = pltpu.get_barrier_semaphore()
    for other in (onward, backward, twin):
        pl.semaphore_signal(barrier, inc=1, device_id=other, device_id_type=MESH_IDS)

    def chunk_of(rank):
        half_up = (rank + 1) // 2
        sign = 1 - 2 * (rank % 2)
        return (place + chips + sign * half_up) % chips

    def load(rank):
        chunk = chunk_of(rank)
        return pltpu.make_async_copy(part_ref.at[core, chunk], held.at[chunk], load_sem.at[rank])

    def swap(rank):
        chunk = chunk_of(rank)
        return pltpu.make_async_remote_copy(
            src_ref=part_ref.at[1 - core, chunk],
            dst_ref=from_core.at[chunk],
            send_sem=core_send.at[rank],
            recv_sem=core_recv.at[rank],
            device_id=twin,
            device_id_type=MESH_IDS,
        )

    for rank in range(chips):
        load(rank).start()
    pl.semaphore_wait(barrier, 3)
    for rank in range(chips):
        swap(rank).start()

    def add_rows(chunk, first, count, source):
        def one(index, carry):
            rows = pl.ds(pl.multiple_of(first + index * TILE, TILE), TILE)
            held[chunk, rows, :] = (
                held[chunk, rows, :].astype(jnp.float32) + source[rows, :].astype(jnp.float32)
            ).astype(jnp.bfloat16)
            return carry

        lax.fori_loop(0, count // TILE, one, 0, unroll=False)

    def prepare(rank):
        chunk = chunk_of(rank)
        load(rank).wait()
        swap(rank).wait_recv()
        add_rows(chunk, 0, held.shape[1], from_core.at[chunk])

    def ring_chunk(lane, step):
        return (place + (chips - 1) * chips - lanes[lane][0] * step) % chips

    def ring_copy(lane, step):
        sign, first, count = lanes[lane]
        chunk = ring_chunk(lane, step)
        rows = pl.ds(first, count)
        return pltpu.make_async_remote_copy(
            src_ref=held.at[chunk, rows],
            dst_ref=arriving.at[step, rows],
            send_sem=ring_send.at[lane, step],
            recv_sem=ring_recv.at[lane, step],
            device_id=onward if sign > 0 else backward,
            device_id_type=MESH_IDS,
        )

    def take(lane, step):
        sign, first, count = lanes[lane]
        chunk = ring_chunk(lane, step)
        ring_copy(lane, step - 1).wait_recv()
        add_rows(chunk, first, count, arriving.at[step - 1])

    prepare(0)
    for lane in range(len(lanes)):
        ring_copy(lane, 0).start()

    def early_step(step, carry):
        prepare(2 * step - 1)

        @pl.when(2 * step < chips)
        def _():
            prepare(2 * step)

        for lane in range(len(lanes)):
            take(lane, step)
            ring_copy(lane, step).start()
        return carry

    def late_step(step, carry):
        for lane in range(len(lanes)):
            take(lane, step)
            ring_copy(lane, step).start()
        return carry

    lax.fori_loop(1, chips // 2 + 1, early_step, 0)
    lax.fori_loop(chips // 2 + 1, chips - 1, late_step, 0)

    def spread_parts(lane, step):
        sign, first, count = lanes[lane]
        chunk = (place + (chips + 1) * chips + sign * (1 - step)) % chips
        return sign, chunk, pl.ds(first, count)

    def spread_copy(lane, step, source):
        sign, chunk, rows = spread_parts(lane, step)
        return pltpu.make_async_remote_copy(
            src_ref=source.at[chunk, rows],
            dst_ref=final.at[chunk, rows],
            send_sem=spread_send.at[lane, step],
            recv_sem=spread_recv.at[lane, step],
            device_id=onward if sign > 0 else backward,
            device_id_type=MESH_IDS,
        )

    def cross_copy(lane, step, source):
        sign, chunk, rows = spread_parts(lane, step)
        return pltpu.make_async_remote_copy(
            src_ref=source.at[chunk, rows],
            dst_ref=sum_ref.at[core, chunk, rows],
            send_sem=cross_send.at[lane, step],
            recv_sem=cross_recv.at[lane, step],
            device_id=twin,
            device_id_type=MESH_IDS,
        )

    def store_copy(lane, step, source):
        sign, chunk, rows = spread_parts(lane, step)
        return pltpu.make_async_copy(
            source.at[chunk, rows], sum_ref.at[core, chunk, rows], store_sem.at[lane, step]
        )

    for lane in range(len(lanes)):
        take(lane, chips - 1)
        spread_copy(lane, 0, held).start()
        cross_copy(lane, 0, held).start()
        store_copy(lane, 0, held).start()

    def spread_step(step, carry):
        for lane in range(len(lanes)):
            spread_copy(lane, step - 1, final).wait_recv()
            spread_copy(lane, step, final).start()
            cross_copy(lane, step, final).start()
            store_copy(lane, step, final).start()
        return carry

    lax.fori_loop(1, chips - 1, spread_step, 0)
    for lane in range(len(lanes)):
        spread_copy(lane, chips - 2, final).wait_recv()
        cross_copy(lane, chips - 1, final).start()
        store_copy(lane, chips - 1, final).start()

    def settle_swap(rank, carry):
        swap(rank).wait_send()
        return carry

    def settle_ring(step, carry):
        for lane in range(len(lanes)):
            ring_copy(lane, step).wait_send()
            spread_copy(lane, step, final).wait_send()
        return carry

    def settle_out(step, carry):
        for lane in range(len(lanes)):
            cross_copy(lane, step, final).wait()
            store_copy(lane, step, final).wait()
        return carry

    lax.fori_loop(0, chips, settle_swap, 0)
    lax.fori_loop(0, chips - 1, settle_ring, 0)
    lax.fori_loop(0, chips, settle_out, 0)


def ring_sum(parts, devices):
    total_rows, columns = parts.shape
    chips = devices // 2
    chunk_rows = total_rows // devices
    tiles = chunk_rows // TILE
    counts = [tiles // 4 + (1 if spot < tiles % 4 else 0) for spot in range(4)]
    lanes = []
    first = 0
    for sign, count in zip((1, -1, 1, -1), counts):
        lanes.append((sign, first * TILE, count * TILE))
        first += count
    block = (chips, chunk_rows, columns)
    dma = pltpu.SemaphoreType.DMA
    summed = pl.pallas_call(
        functools.partial(ring_sum_kernel, chips, tuple(lanes)),
        out_shape=jax.ShapeDtypeStruct((2,) + block, jnp.bfloat16),
        in_specs=[pl.BlockSpec(memory_space=pl.ANY)],
        out_specs=pl.BlockSpec(memory_space=pl.ANY),
        scratch_shapes=[
            pltpu.VMEM(block, jnp.bfloat16),
            pltpu.VMEM(block, jnp.bfloat16),
            pltpu.VMEM(block, jnp.bfloat16),
            pltpu.VMEM(block, jnp.bfloat16),
            dma((chips,)),
            dma((chips,)),
            dma((chips,)),
            dma((4, chips)),
            dma((4, chips)),
            dma((4, chips)),
            dma((4, chips)),
            dma((4, chips)),
            dma((4, chips)),
            dma((4, chips)),
        ],
        compiler_params=pltpu.CompilerParams(
            collective_id=0, has_side_effects=True, vmem_limit_bytes=56 * 1024 * 1024
        ),
    )(parts.reshape((2,) + block))
    return summed.reshape(total_rows, columns)


def widen_kernel(rows_ref, out_ref):
    out_ref[...] = rows_ref[...].astype(jnp.float32)


def widen(rows, first, shape):
    height, columns = shape
    width = rows.shape[1]
    size = width // 2
    steps = height // size
    return pl.pallas_call(
        widen_kernel,
        out_shape=jax.ShapeDtypeStruct(shape, jnp.float32),
        grid=(columns // width, steps),
        in_specs=[pl.BlockSpec((size, width), lambda j, i: (first // size + j * steps + i, 0))],
        out_specs=pl.BlockSpec((size, width), lambda j, i: (i, j)),
        cost_estimate=pl.CostEstimate(
            flops=0, bytes_accessed=6 * height * columns, transcendentals=0
        ),
    )(rows)


def passed_along(block, axis, distance):
    devices = range(lax.axis_size(axis))
    route = [(i - distance, i) for i in devices if i - distance in devices]
    return lax.ppermute(block, axis, route)


def shards(
    inputs,
    cotangent,
    lengths,
    assign,
    query_key_value,
    out_weight,
    up_weight,
    down_weight,
    model_gains,
    model_shifts,
    hidden_gains,
    hidden_shifts,
):
    pipe_rank = lax.axis_index("pipe")
    micro_count = inputs.shape[0]
    width = inputs.shape[2]
    hidden = up_weight.shape[2]
    slots = range(micro_count)
    owners = assign[:, None] == jnp.arange(micro_count, dtype=jnp.int32)[None, :]
    slot_len = jnp.sum(jnp.where(owners, lengths[:, None], 0), axis=0).astype(jnp.int32)
    length = [slot_len[slot : slot + 1] for slot in slots]
    weights = (
        query_key_value[0],
        out_weight[0],
        up_weight[0],
        down_weight[0],
        model_gains[0],
        model_shifts[0],
        jnp.concatenate([hidden_gains, 1.0 / hidden_gains], axis=0),
        hidden_shifts[0],
    )
    lower = (pipe_rank == 0).astype(jnp.int32)[None]
    upper = (pipe_rank == 1).astype(jnp.int32)[None]

    forward = [forward_call(lower, length[slot], inputs[slot], weights) for slot in slots]
    middle = [passed_along(forward[slot][0], "pipe", 1) for slot in slots]
    forward = [
        forward_call(upper, length[slot], middle[slot], weights, forward[slot]) for slot in slots
    ]
    kept = [dict(zip(FWD_STATE, forward[slot][1:])) for slot in slots]
    backward = [
        backward_call(
            upper, length[slot], cotangent[slot], middle[slot], weights, kept[slot], True
        )
        for slot in slots
    ]
    returned = [passed_along(backward[slot][0], "pipe", -1) for slot in slots]
    backward = [
        backward_call(
            lower, length[slot], returned[slot], inputs[slot], weights, kept[slot], False,
            backward[slot],
        )
        for slot in slots
    ]
    grads = [dict(zip(BWD_STATE, backward[slot][1:])) for slot in slots]
    devices = lax.axis_size("batch")
    rows = ring_sum(weight_grads(kept, grads, devices), devices)
    blocks = 4 + hidden // width
    ends = (blocks + hidden // width) * width
    vectors = rows[ends : ends + SUM_ROWS].astype(jnp.float32)
    wide = hidden // width
    return (
        jnp.stack([forward[slot][0] for slot in slots])[None],
        jnp.stack([backward[slot][0] for slot in slots])[None],
        widen(rows, 0, (width, 3 * width))[None],
        widen(rows, 3 * width, (width, width))[None],
        widen(rows, 4 * width, (width, hidden))[None],
        widen(rows, blocks * width, (hidden, width))[None],
        vectors[None, 0:3],
        vectors[None, 3:10],
        vectors[10 : 10 + wide].reshape(1, hidden),
        vectors[10 + wide : 10 + 3 * wide].reshape(1, 2, hidden),
    )


def solution(mesh):
    return jax.shard_map(
        shards,
        mesh=mesh,
        in_specs=(
            P(None, "batch", None),
            P(None, "batch", None),
            P("batch"),
            P("batch"),
            P("pipe", None, None),
            P("pipe", None, None),
            P("pipe", None, None),
            P("pipe", None, None),
            P("pipe", None, None),
            P("pipe", None, None),
            P("pipe", None),
            P("pipe", None, None),
        ),
        out_specs=(
            P("pipe", None, "batch", None),
            P("pipe", None, "batch", None),
            P("pipe", None, None),
            P("pipe", None, None),
            P("pipe", None, None),
            P("pipe", None, None),
            P("pipe", None, None),
            P("pipe", None, None),
            P("pipe", None),
            P("pipe", None, None),
        ),
        check_vma=False,
    )
```

```python
import functools
import types

import jax
import jax.numpy as jnp
from jax import lax
from jax.experimental import pallas as pl
from jax.experimental.pallas import tpu as pltpu
from jax.sharding import PartitionSpec as P

HEAD = 64
PAIR = 2 * HEAD
EPSILON = 1e-05
SCALE = 0.125
HIDDEN_NEG = -1e30
CHUNK = 512
SUM_ROWS = 32
DEPTH = 3
HEAD_ROWS = 16

TILE = 16
VMEM_BYTES = 60 * 1024 * 1024
MESH_IDS = pl.DeviceIdType.MESH


def named(**given):
    return types.SimpleNamespace(**{name: name for name in given})


N = named(
    x=0,
    dy=0,
    y=0,
    dx=0,
    wq=0,
    wo=0,
    wu=0,
    wd=0,
    normed_in=0,
    projected=0,
    log_total=0,
    attended=0,
    normed_mix=0,
    residual=0,
    normed_ffn=0,
    normed_hidden=0,
    slope=0,
    spread=0,
    d_down=0,
    d_pre=0,
    d_branch=0,
    d_proj=0,
    sums=0,
    wide_scratch=0,
    d_residual=0,
    d_attended=0,
    delta=0,
    bias=0,
    bias_back=0,
    forward=0,
    backward=0,
)


def dot_nn(left, right):
    return jnp.dot(left, right, preferred_element_type=jnp.float32)


def dot_nt(left, right):
    return lax.dot_general(
        left, right, (((1,), (1,)), ((), ())), preferred_element_type=jnp.float32
    )


def standardize(values_in):
    centred = values_in - jnp.mean(values_in, axis=-1, keepdims=True)
    scale = lax.rsqrt(jnp.mean(centred * centred, axis=-1, keepdims=True) + EPSILON)
    return centred * scale, scale


def unit_backward(grad, unit, scale, gain):
    scaled = grad * gain
    first = jnp.mean(scaled, axis=-1, keepdims=True)
    second = jnp.mean(scaled * unit, axis=-1, keepdims=True)
    return (
        scale * (scaled - first - unit * second),
        jnp.sum(grad * unit, axis=0, keepdims=True),
        jnp.sum(grad, axis=0, keepdims=True),
    )


def column_sum(values):
    return jnp.sum(values.astype(jnp.float32), axis=0, keepdims=True)


def hiding_bias(rows, length, query_dim):
    query = lax.broadcasted_iota(jnp.int32, (rows, rows), query_dim)
    key = lax.broadcasted_iota(jnp.int32, (rows, rows), 1 - query_dim)
    visible = (key <= query) & ((key < length) | (key == query))
    return jnp.where(visible, 0.0, HIDDEN_NEG)


def own_lanes(values, which):
    lane = lax.broadcasted_iota(jnp.int32, values.shape, 1)
    mine = (lane >= HEAD) if which else (lane < HEAD)
    return jnp.where(mine, values, jnp.zeros_like(values))


def attend_forward(projected, attended, log_total, bias):
    rows, width = attended.shape
    half = rows // 2
    lane = lax.broadcasted_iota(jnp.int32, (half, PAIR), 1)

    def one_pair(pair, totals):
        first = pl.multiple_of(pair * PAIR, PAIR)
        items = []
        for block in range(2):
            at = slice(block * half, (block + 1) * half)
            reach = (block + 1) * half
            q = projected[at, pl.ds(first, PAIR)] * jnp.bfloat16(SCALE)
            k = projected[0:reach, pl.ds(width + first, PAIR)]
            v = projected[0:reach, pl.ds(2 * width + first, PAIR)]
            items += [(at, reach, own_lanes(q, which), k, v) for which in range(2)]
        scores = [dot_nt(q, k) + bias[at, 0:reach] for at, reach, q, k, v in items]
        softened = []
        for item in scores:
            top = jnp.max(item, axis=-1, keepdims=True)
            exps = jnp.exp(item - top)
            softened.append((exps, jnp.sum(exps, axis=-1, keepdims=True), top))
        mixed = [
            dot_nn(exps.astype(jnp.bfloat16), item[4]) * (1.0 / total)
            for item, (exps, total, top) in zip(items, softened)
        ]
        new_totals = []
        for block in range(2):
            at = items[2 * block][0]
            attended[at, pl.ds(first, PAIR)] = jnp.where(
                lane < HEAD, mixed[2 * block], mixed[2 * block + 1]
            )
            logs = totals[block]
            for which in range(2):
                exps, total, top = softened[2 * block + which]
                logs = jnp.where(lane == 2 * pair + which, top + jnp.log(total), logs)
            new_totals.append(logs)
        return tuple(new_totals)

    zero = jnp.zeros((half, PAIR), jnp.float32)
    totals = lax.fori_loop(0, width // PAIR, one_pair, (zero, zero), unroll=2)
    for block in range(2):
        log_total[:, block * half : (block + 1) * half] = totals[block].T[0:HEAD_ROWS]


def attend_backward(projected, d_attended, log_total, delta, bias, d_proj):
    rows, width = d_attended.shape
    half = rows // 2

    def one_pair(pair, carry):
        first = pl.multiple_of(pair * PAIR, PAIR)
        k_all = projected[:, pl.ds(width + first, PAIR)]
        v_all = projected[:, pl.ds(2 * width + first, PAIR)]
        k_turned = k_all.T
        items = []
        for block in range(2):
            at = slice(block * half, (block + 1) * half)
            q = projected[at, pl.ds(first, PAIR)] * jnp.bfloat16(SCALE)
            grad = d_attended[at, pl.ds(first, PAIR)]
            for which in range(2):
                items.append((block, which, at, own_lanes(q, which), own_lanes(grad, which)))
        raw = []
        for block, which, at, q, grad in items:
            reach = (block + 1) * half
            raw.append((dot_nt(k_all[0:reach], q), dot_nt(v_all[0:reach], grad)))
        shaped = []
        for (block, which, at, q, grad), (scores, d_probs) in zip(items, raw):
            reach = (block + 1) * half
            head = pl.ds(2 * pair + which, 1)
            probs = jnp.exp(scores + bias[0:reach, at] - log_total[head, at])
            d_scores = (probs * (d_probs - delta[head, at])).astype(jnp.bfloat16)
            shaped.append((probs.astype(jnp.bfloat16), d_scores))
        dk = [None, None]
        dv = [None, None]
        dq = []
        for (block, which, at, q, grad), (probs, d_scores) in zip(items, shaped):
            reach = (block + 1) * half
            more_v = dot_nn(probs, grad)
            more_k = dot_nn(d_scores, q)
            dq.append(dot_nn(k_turned[which * HEAD : (which + 1) * HEAD, 0:reach], d_scores))
            for part in range(block + 1):
                piece = slice(part * half, (part + 1) * half)
                dv[part] = more_v[piece] if dv[part] is None else dv[part] + more_v[piece]
                dk[part] = more_k[piece] if dk[part] is None else dk[part] + more_k[piece]
        for block in range(2):
            at = slice(block * half, (block + 1) * half)
            turned = jnp.concatenate(dq[2 * block : 2 * block + 2], axis=0) * SCALE
            d_proj[at, pl.ds(first, PAIR)] = turned.T.astype(jnp.bfloat16)
            d_proj[at, pl.ds(width + first, PAIR)] = dk[block].astype(jnp.bfloat16)
            d_proj[at, pl.ds(2 * width + first, PAIR)] = dv[block].astype(jnp.bfloat16)
        return carry

    lax.fori_loop(0, width // PAIR, one_pair, 0, unroll=2)


KEPT = (N.normed_in, N.projected, N.log_total, N.attended, N.normed_mix, N.residual,
        N.normed_ffn, N.normed_hidden, N.slope, N.spread)
GRADS = (N.d_down, N.d_pre, N.d_branch, N.d_proj, N.sums)


def buffer_shapes(rows, width, hidden):
    bf, f = jnp.bfloat16, jnp.float32
    return {
        N.x: ((rows, width), bf),
        N.dy: ((rows, width), bf),
        N.y: ((rows, width), bf),
        N.dx: ((rows, width), bf),
        N.wq: ((width, 3 * width), bf),
        N.wo: ((width, width), bf),
        N.wu: ((width, hidden), bf),
        N.wd: ((hidden, width), bf),
        N.normed_in: ((rows, width), bf),
        N.projected: ((rows, 3 * width), bf),
        N.log_total: ((HEAD_ROWS, rows), f),
        N.attended: ((rows, width), f),
        N.normed_mix: ((rows, width), bf),
        N.residual: ((rows, width), f),
        N.normed_ffn: ((rows, width), bf),
        N.normed_hidden: ((rows, hidden), bf),
        N.slope: ((rows, hidden), bf),
        N.spread: ((rows, PAIR), f),
        N.d_down: ((rows, width), bf),
        N.d_pre: ((rows, hidden), bf),
        N.d_branch: ((rows, width), bf),
        N.d_proj: ((rows, 3 * width), bf),
        N.sums: ((SUM_ROWS, width), f),
        N.wide_scratch: ((rows, hidden), f),
        N.d_residual: ((rows, width), f),
        N.d_attended: ((rows, width), bf),
        N.delta: ((HEAD_ROWS, rows), f),
        N.bias: ((rows, rows), f),
        N.bias_back: ((rows, rows), f),
    }


def forward_body(held, vectors, length, ready, emit):
    gm, sm, gh, sh = vectors
    gm, sm, sh = gm.at[0], sm.at[0], sh.at[0]
    bf = jnp.bfloat16
    rows, width = held[N.x].shape
    hidden = held[N.wu].shape[1]
    wide_scratch = held[N.wide_scratch]
    held[N.bias][...] = hiding_bias(rows, length, 0)
    ready(N.x)
    unit, unused = standardize(held[N.x][...].astype(jnp.float32))
    held[N.normed_in][...] = (unit * gm[0:1, :] + sm[0:1, :]).astype(bf)
    emit(N.normed_in)
    for block in range(3):
        cols = slice(block * width, (block + 1) * width)
        ready(N.wq)
        out = dot_nn(held[N.normed_in][...], held[N.wq][:, cols])
        if block != 1:
            out = out + sm[1 + block // 2 : 2 + block // 2, :]
        held[N.projected][:, cols] = out.astype(bf)
    emit(N.projected)
    attend_forward(held[N.projected], held[N.attended], held[N.log_total], held[N.bias])
    emit(N.log_total)
    emit(N.attended)

    unit, unused = standardize(held[N.attended][...])
    held[N.normed_mix][...] = (unit * gm[1:2, :] + sm[3:4, :]).astype(bf)
    emit(N.normed_mix)
    ready(N.wo)
    residual = held[N.x][...].astype(jnp.float32) + sm[4:5, :]
    residual = residual + dot_nn(held[N.normed_mix][...], held[N.wo][...])
    held[N.residual][...] = residual
    emit(N.residual)
    unit, unused = standardize(residual)
    held[N.normed_ffn][...] = (unit * gm[2:3, :] + sm[5:6, :]).astype(bf)
    emit(N.normed_ffn)
    ready(N.wu)
    total = jnp.zeros((rows, 1), jnp.float32)
    for first in range(0, hidden, CHUNK):
        cols = slice(first, first + CHUNK)
        pre = dot_nn(held[N.normed_ffn][...], held[N.wu][:, cols]) + sh[0:1, cols]
        share = 0.5 + 0.5 * lax.erf(pre * 0.7071067811865476)
        density = 0.3989422804014327 * jnp.exp(-0.5 * pre * pre)
        act = pre * share
        held[N.slope][:, cols] = (share + pre * density).astype(bf)
        wide_scratch[:, cols] = act
        total = total + jnp.sum(act, axis=-1, keepdims=True)
    emit(N.slope)
    mean = total * (1.0 / hidden)
    square = jnp.zeros((rows, 1), jnp.float32)
    for first in range(0, hidden, CHUNK):
        centred = wide_scratch[:, first : first + CHUNK] - mean
        square = square + jnp.sum(centred * centred, axis=-1, keepdims=True)
    scale = lax.rsqrt(square * (1.0 / hidden) + EPSILON)
    held[N.spread][...] = jnp.broadcast_to(scale, (rows, PAIR))
    emit(N.spread)
    for first in range(0, hidden, CHUNK):
        cols = slice(first, first + CHUNK)
        unit = (wide_scratch[:, cols] - mean) * scale
        held[N.normed_hidden][:, cols] = (unit * gh[0:1, cols] + sh[1:2, cols]).astype(bf)
    emit(N.normed_hidden)
    ready(N.wd)
    out = held[N.residual][...] + dot_nn(held[N.normed_hidden][...], held[N.wd][...])
    held[N.y][...] = (out + sm[6:7, :]).astype(bf)
    emit(N.y)


def backward_body(held, vectors, length, masked, ready, emit):
    gm, sm, gh, sh = vectors
    gm, sm, sh = gm.at[0], sm.at[0], sh.at[0]
    bf = jnp.bfloat16
    rows, width = held[N.x].shape
    hidden = held[N.wu].shape[1]
    wide = hidden // width
    wide_scratch, sums = held[N.wide_scratch], held[N.sums]
    sums[...] = jnp.zeros_like(sums)
    held[N.bias_back][...] = hiding_bias(rows, length, 1)
    ready(N.dy)
    d_down = held[N.dy][...]
    if masked:
        live = lax.broadcasted_iota(jnp.int32, (rows, 1), 0) < length
        d_down = jnp.where(live, d_down.astype(jnp.float32), 0.0).astype(bf)
    held[N.d_down][...] = d_down
    emit(N.d_down)
    sums[9:10, :] = column_sum(d_down)

    first_total = jnp.zeros((rows, 1), jnp.float32)
    second_total = jnp.zeros((rows, 1), jnp.float32)
    for block in range(wide):
        cols = slice(block * width, (block + 1) * width)
        ready(N.wd)
        ready(N.normed_hidden)
        grad = dot_nt(held[N.d_down][...], held[N.wd][cols, :])
        normed = held[N.normed_hidden][:, cols].astype(jnp.float32)
        unit = (normed - sh[1:2, cols]) * (1.0 / gh[0:1, cols])
        sums[10 + block : 11 + block, :] = jnp.sum(grad * unit, axis=0, keepdims=True)
        sums[18 + block : 19 + block, :] = jnp.sum(grad, axis=0, keepdims=True)
        scaled = grad * gh[0:1, cols]
        wide_scratch[:, cols] = scaled
        first_total = first_total + jnp.sum(scaled, axis=-1, keepdims=True)
        second_total = second_total + jnp.sum(scaled * unit, axis=-1, keepdims=True)
    first_mean = first_total * (1.0 / hidden)
    second_mean = second_total * (1.0 / hidden)
    ready(N.spread)
    ready(N.slope)
    scale = held[N.spread][:, 0:1]
    for block in range(wide):
        cols = slice(block * width, (block + 1) * width)
        normed = held[N.normed_hidden][:, cols].astype(jnp.float32)
        unit = (normed - sh[1:2, cols]) * (1.0 / gh[0:1, cols])
        d_act = scale * (wide_scratch[:, cols] - first_mean - unit * second_mean)
        d_pre = (d_act * held[N.slope][:, cols].astype(jnp.float32)).astype(bf)
        held[N.d_pre][:, cols] = d_pre
        sums[14 + block : 15 + block, :] = column_sum(d_pre)
    emit(N.d_pre)

    ready(N.wu)
    d_ffn = dot_nt(held[N.d_pre][...], held[N.wu][...])
    ready(N.residual)
    unit, scale = standardize(held[N.residual][...])
    through, gain_sum, shift_sum = unit_backward(d_ffn, unit, scale, gm[2:3, :])
    sums[2:3, :] = gain_sum
    sums[8:9, :] = shift_sum
    through = through + held[N.d_down][...].astype(jnp.float32)
    held[N.d_residual][...] = through
    held[N.d_branch][...] = through.astype(bf)
    emit(N.d_branch)
    sums[7:8, :] = column_sum(held[N.d_branch][...])

    ready(N.wo)
    d_mix = dot_nt(held[N.d_branch][...], held[N.wo][...])
    ready(N.attended)
    attended = held[N.attended][...]
    unit, scale = standardize(attended)
    through, gain_sum, shift_sum = unit_backward(d_mix, unit, scale, gm[1:2, :])
    sums[1:2, :] = gain_sum
    sums[6:7, :] = shift_sum
    held[N.d_attended][...] = through.astype(bf)
    product = held[N.d_attended][...].astype(jnp.float32) * attended
    upper = product.astype(bf)
    lower = (product - upper.astype(jnp.float32)).astype(bf)
    head_row = lax.broadcasted_iota(jnp.int32, (HEAD_ROWS, width), 0)
    head_col = lax.broadcasted_iota(jnp.int32, (HEAD_ROWS, width), 1) // HEAD
    chooser = jnp.where(head_row == head_col, 1.0, 0.0).astype(bf)
    held[N.delta][...] = dot_nt(chooser, upper) + dot_nt(chooser, lower)

    ready(N.projected)
    ready(N.log_total)
    attend_backward(
        held[N.projected], held[N.d_attended], held[N.log_total], held[N.delta],
        held[N.bias_back], held[N.d_proj],
    )
    emit(N.d_proj)
    ready(N.wq)
    d_norm = dot_nt(held[N.d_proj][...], held[N.wq][...])
    sums[4:5, :] = column_sum(held[N.d_proj][:, 0:width])
    sums[5:6, :] = column_sum(held[N.d_proj][:, 2 * width :])
    ready(N.x)
    unit, scale = standardize(held[N.x][...].astype(jnp.float32))
    through, gain_sum, shift_sum = unit_backward(d_norm, unit, scale, gm[0:1, :])
    sums[0:1, :] = gain_sum
    sums[3:4, :] = shift_sum
    held[N.dx][...] = (through + held[N.d_residual][...]).astype(bf)
    emit(N.dx)
    emit(N.sums)


def slot_length(lengths_ref, assign_ref, slot):
    total = jnp.int32(0)
    for at in range(lengths_ref.shape[0]):
        total = total + jnp.where(assign_ref[at] == slot, lengths_ref[at], 0)
    return total


def layer_kernel(
    steps, plane, slot, groups, stacked, out_names, shared, buffers, lengths_ref, assign_ref, *refs
):
    in_names = sum(groups, ())
    sources = dict(zip(in_names, refs))
    for name in stacked:
        sources[name] = sources[name].at[slot]
    vectors = refs[len(in_names) : len(in_names) + 4]
    refs = refs[len(in_names) + 4 + shared :]
    targets = dict(zip(out_names, refs))
    refs = refs[len(out_names) :]
    held = dict(zip(buffers, refs))
    in_sem, out_sem = refs[len(buffers) :]

    @pl.when(lax.axis_index("pipe") == plane)
    def _():
        loads = {
            name: pltpu.make_async_copy(sources[name], held[name], in_sem.at[at])
            for at, name in enumerate(in_names)
        }
        stores = {
            name: pltpu.make_async_copy(held[name], targets[name], out_sem.at[at])
            for at, name in enumerate(out_names)
        }
        for name in in_names:
            loads[name].start()
        waited = set()

        def ready(name):
            for group in groups:
                if name in group and name not in waited:
                    waited.update(group)
                    for item in group:
                        loads[item].wait()

        def emit(name):
            if name in stores:
                stores[name].start()

        length = slot_length(lengths_ref, assign_ref, slot)
        if N.forward in steps:
            forward_body(held, vectors, length, ready, emit)
        if N.backward in steps:
            backward_body(held, vectors, length, N.forward in steps, ready, emit)
        for name in out_names:
            stores[name].wait()


FORWARD_ONLY = (N.projected, N.log_total, N.attended, N.residual, N.slope, N.spread)


def layer_call(steps, plane, slot, sizes, given, vectors, previous):
    stacked = tuple(name for name in (N.x, N.dy) if name in given and given[name].ndim == 3)
    rows, width = given[N.x].shape[-2:]
    hidden = given[N.wu].shape[1]
    shapes = buffer_shapes(rows, width, hidden)
    if steps == (N.forward,):
        groups = ((N.x, N.wq), (N.wo, N.wu, N.wd))
        out_names = (N.y,) + KEPT
        spare = (N.wide_scratch, N.bias)
    elif steps == (N.backward,):
        groups = ((N.dy, N.wd, N.normed_hidden), (N.spread, N.slope, N.wu, N.residual),
                  (N.wo, N.attended, N.projected, N.log_total), (N.wq, N.x))
        out_names = (N.dx,) + GRADS
        spare = (N.wide_scratch, N.bias_back, N.d_residual, N.d_attended, N.delta)
    else:
        groups = ((N.x, N.wq), (N.wo, N.wu), (N.wd, N.dy))
        out_names = (N.y,) + tuple(name for name in KEPT if name not in FORWARD_ONLY)
        out_names += (N.dx,) + GRADS
        spare = (N.wide_scratch, N.bias, N.bias_back, N.d_residual, N.d_attended, N.delta)
        spare += FORWARD_ONLY
    in_names = sum(groups, ())
    buffers = in_names + tuple(name for name in out_names if name not in in_names) + spare
    any_spec = pl.BlockSpec(memory_space=pl.ANY)
    vmem_spec = pl.BlockSpec(memory_space=pltpu.VMEM)
    smem_spec = pl.BlockSpec(memory_space=pltpu.SMEM)
    in_specs = [smem_spec] * 2 + [any_spec] * len(in_names) + [vmem_spec] * 4
    args = list(sizes) + [given[name] for name in in_names] + list(vectors)
    shared = [name for name in out_names if name in previous]
    aliases = {len(args) + at: out_names.index(name) for at, name in enumerate(shared)}
    in_specs += [any_spec] * len(shared)
    args += [previous[name] for name in shared]
    scratch = [pltpu.VMEM(*shapes[name]) for name in buffers]
    scratch.append(pltpu.SemaphoreType.DMA((len(in_names),)))
    scratch.append(pltpu.SemaphoreType.DMA((len(out_names),)))
    outs = pl.pallas_call(
        functools.partial(
            layer_kernel, steps, plane, slot, groups, stacked, out_names, len(shared), buffers
        ),
        out_shape=[jax.ShapeDtypeStruct(*shapes[name]) for name in out_names],
        in_specs=in_specs,
        out_specs=[any_spec] * len(out_names),
        input_output_aliases=aliases,
        scratch_shapes=scratch,
        compiler_params=pltpu.CompilerParams(vmem_limit_bytes=VMEM_BYTES),
        cost_estimate=pl.CostEstimate(
            flops=len(steps) * 2 * rows * width * (4 * width + 2 * hidden),
            bytes_accessed=40_000_000,
            transcendentals=0,
        ),
    )(*args)
    return dict(zip(out_names, outs))


LEFT = (N.normed_hidden, N.normed_ffn, N.normed_mix, N.normed_in)
RIGHT = (N.d_down, N.d_pre, N.d_branch, N.d_proj)


def weight_grad_kernel(*refs):
    parts = len(LEFT)
    sources, out_hbm, scratch = refs[: 2 * parts], refs[2 * parts], refs[2 * parts + 1 :]
    left, right = scratch[0:parts], scratch[parts : 2 * parts]
    out_s, turned, in_sem, out_sem = scratch[2 * parts :]
    width = left[3].shape[1]
    wide = left[0].shape[1] // width
    loads = [
        pltpu.make_async_copy(source, target, in_sem.at[at])
        for at, (source, target) in enumerate(zip(sources, left + right))
    ]
    for part in range(parts):
        loads[part].start()
        loads[parts + part].start()
    starts = (4 + wide, 4, 3, 0)
    stores = []

    def store(first, count):
        at = pl.ds(first, count)
        stores.append(pltpu.make_async_copy(out_s.at[at], out_hbm.at[at], out_sem.at[len(stores)]))
        stores[-1].start()

    for part in range(parts):
        loads[part].wait()
        loads[parts + part].wait()
        first = starts[part] * width
        if part == 0:

            def one(block, carry):
                cols = pl.ds(pl.multiple_of(block * width, width), width)
                turned[...] = left[part][:, cols].T
                at = pl.ds(pl.multiple_of(first + block * width, width), width)
                out_s[at, :] = dot_nn(turned[...], right[part][...]).astype(jnp.bfloat16)
                return carry

            lax.fori_loop(0, wide, one, 0)
            store(first, wide * width)
        else:
            turned[...] = left[part][...].T
            blocks = right[part].shape[1] // width

            def one(block, carry):
                cols = pl.ds(pl.multiple_of(block * width, width), width)
                at = pl.ds(pl.multiple_of(first + block * width, width), width)
                out_s[at, :] = dot_nn(turned[...], right[part][:, cols]).astype(jnp.bfloat16)
                return carry

            lax.fori_loop(0, blocks, one, 0)
            store(first, blocks * width)
    used = (4 + 2 * wide) * width
    rest = out_s.shape[0] - used
    if rest:
        out_s[used:, :] = jnp.zeros((rest, width), jnp.bfloat16)
        store(used, rest)
    for item in stores:
        item.wait()


def weight_grads(kept, grads, devices):
    args = [kept[name] for name in LEFT] + [grads[name] for name in RIGHT]
    rows, width = kept[N.normed_in].shape
    hidden = kept[N.normed_hidden].shape[1]
    used = (4 + 2 * hidden // width) * width
    total_rows = used + -used % (TILE * devices)
    bf = jnp.bfloat16
    any_spec = pl.BlockSpec(memory_space=pl.ANY)
    scratch = [pltpu.VMEM(item.shape, bf) for item in args]
    scratch += [
        pltpu.VMEM((total_rows, width), bf),
        pltpu.VMEM((width, rows), bf),
        pltpu.SemaphoreType.DMA((len(args),)),
        pltpu.SemaphoreType.DMA((5,)),
    ]
    return pl.pallas_call(
        weight_grad_kernel,
        out_shape=jax.ShapeDtypeStruct((total_rows, width), bf),
        in_specs=[any_spec] * len(args),
        out_specs=any_spec,
        scratch_shapes=scratch,
        compiler_params=pltpu.CompilerParams(vmem_limit_bytes=VMEM_BYTES),
        cost_estimate=pl.CostEstimate(
            flops=2 * rows * used * width, bytes_accessed=30_000_000, transcendentals=0
        ),
    )(*args)


def ring_sum_kernel(
    chips,
    lanes,
    count,
    *refs,
):
    parts, vectors = refs[:count], refs[count : 2 * count]
    sum_ref, vector_ref = refs[2 * count : 2 * count + 2]
    refs = refs[2 * count + 2 :]
    own, from_core, refs = refs[:count], refs[count : 2 * count], refs[2 * count :]
    held = own[0]
    (
        arriving,
        final,
        vector_held,
        vector_twin,
        vector_arriving,
        vector_final,
        load_sem,
        core_send,
        core_recv,
        ring_send,
        ring_recv,
        spread_send,
        spread_recv,
        cross_send,
        cross_recv,
        store_sem,
        vector_send,
        vector_recv,
        vector_store,
    ) = refs
    line_len = chips // 2
    pipe = lax.axis_index("pipe")
    batch = lax.axis_index("batch")
    core = batch % 2
    side = (batch // 2) % 2
    line = batch // 4
    place = line * (1 - side) + (chips - 1 - line) * side

    def chip_at(spot):
        far = spot // line_len
        along = spot * (1 - far) + (chips - 1 - spot) * far
        return (pipe, (along * 2 + far) * 2 + core)

    onward = chip_at((place + 1) % chips)
    backward = chip_at((place + chips - 1) % chips)
    twin = (pipe, batch + 1 - 2 * core)

    barrier = pltpu.get_barrier_semaphore()
    for other in (onward, backward, twin):
        pl.semaphore_signal(barrier, inc=1, device_id=other, device_id_type=MESH_IDS)

    def chunk_of(rank):
        half_up = (rank + 1) // 2
        sign = 1 - 2 * (rank % 2)
        return (place + chips + sign * half_up) % chips

    def load(rank, which):
        chunk = chunk_of(rank)
        return pltpu.make_async_copy(
            parts[which].at[core, chunk], own[which].at[chunk], load_sem.at[which, rank]
        )

    def swap(rank, which):
        chunk = chunk_of(rank)
        return pltpu.make_async_remote_copy(
            src_ref=parts[which].at[1 - core, chunk],
            dst_ref=from_core[which].at[chunk],
            send_sem=core_send.at[which, rank],
            recv_sem=core_recv.at[which, rank],
            device_id=twin,
            device_id_type=MESH_IDS,
        )

    for rank in range(chips):
        for which in range(count):
            load(rank, which).start()
    pl.semaphore_wait(barrier, 3)
    for rank in range(chips):
        for which in range(count):
            swap(rank, which).start()

    def add_rows(chunk, first, count, sources):
        def one(index, carry):
            rows = pl.ds(pl.multiple_of(first + index * TILE, TILE), TILE)
            total = held[chunk, rows, :].astype(jnp.float32)
            for source in sources:
                total = total + source[rows, :].astype(jnp.float32)
            held[chunk, rows, :] = total.astype(jnp.bfloat16)
            return carry

        lax.fori_loop(0, count // TILE, one, 0, unroll=False)

    def prepare(rank):
        chunk = chunk_of(rank)
        for which in range(count):
            load(rank, which).wait()
            swap(rank, which).wait_recv()
        sources = [item.at[chunk] for item in own[1:] + from_core]
        add_rows(chunk, 0, held.shape[1], sources)

    my_rows = pl.ds(pl.multiple_of(core * TILE, TILE), TILE)
    twin_rows = pl.ds(pl.multiple_of((1 - core) * TILE, TILE), TILE)

    def vector_copy(at, source, target, device):
        return pltpu.make_async_remote_copy(
            src_ref=source,
            dst_ref=target,
            send_sem=vector_send.at[at],
            recv_sem=vector_recv.at[at],
            device_id=device,
            device_id_type=MESH_IDS,
        )

    vector_swap = vector_copy(0, vector_held.at[twin_rows], vector_twin, twin)
    vector_ring = vector_copy(1, vector_held.at[my_rows], vector_arriving, onward)
    vector_spread = vector_copy(2, vector_final, vector_final, onward)
    vector_cross = vector_copy(3, vector_final, vector_ref.at[my_rows], twin)
    vector_out = pltpu.make_async_copy(vector_final, vector_ref.at[my_rows], vector_store.at[0])
    total = vectors[0][...]
    for item in vectors[1:]:
        total = total + item[...]
    vector_held[...] = total.astype(jnp.bfloat16)
    vector_swap.start()

    def add_vectors(source):
        vector_held[my_rows, :] = (
            vector_held[my_rows, :].astype(jnp.float32) + source[...].astype(jnp.float32)
        ).astype(jnp.bfloat16)

    def pass_vectors(step):
        @pl.when(place == step)
        def _():
            vector_ring.wait_recv()
            add_vectors(vector_arriving)
            vector_ring.start()

    def spread_vectors(step, last=False):
        @pl.when((place + 1) % chips == step)
        def _():
            vector_spread.wait_recv()
            if not last:
                vector_spread.start()
            vector_cross.start()
            vector_out.start()

    def ring_chunk(lane, step):
        return (place + (chips - 1) * chips - lanes[lane][0] * step) % chips

    def ring_copy(lane, step):
        sign, first, count = lanes[lane]
        chunk = ring_chunk(lane, step)
        rows = pl.ds(first, count)
        return pltpu.make_async_remote_copy(
            src_ref=held.at[chunk, rows],
            dst_ref=arriving.at[step, rows],
            send_sem=ring_send.at[lane, step],
            recv_sem=ring_recv.at[lane, step],
            device_id=onward if sign > 0 else backward,
            device_id_type=MESH_IDS,
        )

    def take(lane, step):
        sign, first, count = lanes[lane]
        chunk = ring_chunk(lane, step)
        ring_copy(lane, step - 1).wait_recv()
        add_rows(chunk, first, count, [arriving.at[step - 1]])

    prepare(0)
    for lane in range(len(lanes)):
        ring_copy(lane, 0).start()
    vector_swap.wait_recv()
    add_vectors(vector_twin)

    @pl.when(place == 0)
    def _():
        vector_ring.start()

    def early_step(step, carry):
        prepare(2 * step - 1)

        @pl.when(2 * step < chips)
        def _():
            prepare(2 * step)

        for lane in range(len(lanes)):
            take(lane, step)
            ring_copy(lane, step).start()
        pass_vectors(step)
        return carry

    def late_step(step, carry):
        for lane in range(len(lanes)):
            take(lane, step)
            ring_copy(lane, step).start()
        pass_vectors(step)
        return carry

    lax.fori_loop(1, chips // 2 + 1, early_step, 0)
    lax.fori_loop(chips // 2 + 1, chips - 1, late_step, 0)

    def spread_parts(lane, step):
        sign, first, count = lanes[lane]
        chunk = (place + (chips + 1) * chips + sign * (1 - step)) % chips
        return sign, chunk, pl.ds(first, count)

    def spread_copy(lane, step, source):
        sign, chunk, rows = spread_parts(lane, step)
        return pltpu.make_async_remote_copy(
            src_ref=source.at[chunk, rows],
            dst_ref=final.at[chunk, rows],
            send_sem=spread_send.at[lane, step],
            recv_sem=spread_recv.at[lane, step],
            device_id=onward if sign > 0 else backward,
            device_id_type=MESH_IDS,
        )

    def cross_copy(lane, step, source):
        sign, chunk, rows = spread_parts(lane, step)
        return pltpu.make_async_remote_copy(
            src_ref=source.at[chunk, rows],
            dst_ref=sum_ref.at[core, chunk, rows],
            send_sem=cross_send.at[lane, step],
            recv_sem=cross_recv.at[lane, step],
            device_id=twin,
            device_id_type=MESH_IDS,
        )

    def store_copy(lane, step, source):
        sign, chunk, rows = spread_parts(lane, step)
        return pltpu.make_async_copy(
            source.at[chunk, rows], sum_ref.at[core, chunk, rows], store_sem.at[lane, step]
        )

    @pl.when(place == chips - 1)
    def _():
        vector_ring.wait_recv()
        add_vectors(vector_arriving)
        vector_final[...] = vector_held[my_rows, :]
        vector_spread.start()
        vector_cross.start()
        vector_out.start()

    for lane in range(len(lanes)):
        take(lane, chips - 1)
        spread_copy(lane, 0, held).start()
        cross_copy(lane, 0, held).start()
        store_copy(lane, 0, held).start()

    def spread_step(step, carry):
        for lane in range(len(lanes)):
            spread_copy(lane, step - 1, final).wait_recv()
            spread_copy(lane, step, final).start()
            cross_copy(lane, step, final).start()
            store_copy(lane, step, final).start()
        spread_vectors(step)
        return carry

    lax.fori_loop(1, chips - 1, spread_step, 0)
    for lane in range(len(lanes)):
        spread_copy(lane, chips - 2, final).wait_recv()
        cross_copy(lane, chips - 1, final).start()
        store_copy(lane, chips - 1, final).start()
    spread_vectors(chips - 1, last=True)

    def settle_swap(rank, carry):
        for which in range(count):
            swap(rank, which).wait_send()
        return carry

    def settle_ring(step, carry):
        for lane in range(len(lanes)):
            ring_copy(lane, step).wait_send()
            spread_copy(lane, step, final).wait_send()
        return carry

    def settle_out(step, carry):
        for lane in range(len(lanes)):
            cross_copy(lane, step, final).wait()
            store_copy(lane, step, final).wait()
        return carry

    lax.fori_loop(0, chips, settle_swap, 0)
    lax.fori_loop(0, chips - 1, settle_ring, 0)
    lax.fori_loop(0, chips, settle_out, 0)
    vector_swap.wait_send()
    vector_cross.wait()
    vector_out.wait()

    @pl.when(place != chips - 1)
    def _():
        vector_ring.wait_send()

    @pl.when(place != chips - 2)
    def _():
        vector_spread.wait_send()


def ring_sum(parts, vectors, devices):
    total_rows, columns = parts[0].shape
    count = len(parts)
    chips = devices // 2
    chunk_rows = total_rows // devices
    tiles = chunk_rows // TILE
    counts = [tiles // 4 + (1 if spot < tiles % 4 else 0) for spot in range(4)]
    lanes = []
    first = 0
    for sign, share in zip((1, -1, 1, -1), counts):
        lanes.append((sign, first * TILE, share * TILE))
        first += share
    block = (chips, chunk_rows, columns)
    bf = jnp.bfloat16
    dma = pltpu.SemaphoreType.DMA
    any_spec = pl.BlockSpec(memory_space=pl.ANY)
    vmem_spec = pl.BlockSpec(memory_space=pltpu.VMEM)
    vector_shape = vectors[0].shape
    summed, vector_sum = pl.pallas_call(
        functools.partial(ring_sum_kernel, chips, tuple(lanes), count),
        out_shape=[
            jax.ShapeDtypeStruct((2,) + block, bf),
            jax.ShapeDtypeStruct(vector_shape, bf),
        ],
        in_specs=[any_spec] * count + [vmem_spec] * count,
        out_specs=[any_spec] * 2,
        scratch_shapes=[pltpu.VMEM(block, bf)] * (2 * count + 2)
        + [pltpu.VMEM(vector_shape, bf)]
        + [pltpu.VMEM((TILE, columns), bf)] * 3
        + [dma((count, chips))] * 3
        + [dma((4, chips))] * 7
        + [dma((4,)), dma((4,)), dma((1,))],
        compiler_params=pltpu.CompilerParams(
            collective_id=0, has_side_effects=True, vmem_limit_bytes=VMEM_BYTES
        ),
    )(*[item.reshape((2,) + block) for item in parts], *vectors)
    return summed.reshape(total_rows, columns), vector_sum


def finish_kernel(steps, count, rows_hbm, vectors, *refs):
    moved, refs = refs[: 2 * count], refs[2 * count :]
    outs, refs = refs[:4], refs[4:]
    gains, shifts, hidden_gains, hidden_shifts = refs[:4]
    stacked, refs = refs[4:6], refs[6:]
    narrow, broad, passing, in_sem, out_sem, arrive_sem, leave_sem = refs
    width = rows_hbm.shape[1]
    arrivals, departures = [], []
    for at, source in enumerate(moved):
        target = stacked[at // count].at[at % count]
        arrivals.append(pltpu.make_async_copy(source, passing.at[at], arrive_sem.at[at]))
        departures.append(pltpu.make_async_copy(passing.at[at], target, leave_sem.at[at]))

    def load(step):
        at = pl.ds(step * width, width)
        return pltpu.make_async_copy(rows_hbm.at[at], narrow.at[step % DEPTH], in_sem.at[step % DEPTH])

    def store(step):
        which, row, column = steps[step]
        target = outs[which].at[pl.ds(row, width), pl.ds(column, width)]
        return pltpu.make_async_copy(broad.at[step % DEPTH], target, out_sem.at[step % DEPTH])

    for step in range(DEPTH):
        load(step).start()
    for item in arrivals:
        item.start()
    values = vectors[...].astype(jnp.float32)
    gains[...] = values[0:3]
    shifts[...] = values[3:10]
    wide = hidden_gains.shape[1] // width
    for block in range(wide):
        cols = slice(block * width, (block + 1) * width)
        hidden_gains[:, cols] = values[10 + block : 11 + block]
        for row in range(2):
            first = 10 + (row + 1) * wide + block
            hidden_shifts[row : row + 1, cols] = values[first : first + 1]
    for step in range(len(steps)):
        load(step).wait()
        if step >= DEPTH:
            store(step - DEPTH).wait()
        broad[step % DEPTH] = narrow[step % DEPTH].astype(jnp.float32)
        store(step).start()
        if step + DEPTH < len(steps):
            load(step + DEPTH).start()
        if step == DEPTH:
            for arrival, departure in zip(arrivals, departures):
                arrival.wait()
                departure.start()
    for step in range(len(steps) - DEPTH, len(steps)):
        store(step).wait()
    for item in departures:
        item.wait()


def finish(rows, vectors, slots_out, slots_grad, hidden):
    width = rows.shape[1]
    wide = hidden // width
    count = len(slots_out)
    steps = [(0, 0, block * width) for block in range(3)] + [(1, 0, 0)]
    steps += [(2, 0, block * width) for block in range(wide)]
    steps += [(3, block * width, 0) for block in range(wide)]
    f = jnp.float32
    shapes = [(width, 3 * width), (width, width), (width, hidden), (hidden, width)]
    shapes += [(3, width), (7, width), (1, hidden), (2, hidden)]
    any_spec = pl.BlockSpec(memory_space=pl.ANY)
    vmem_spec = pl.BlockSpec(memory_space=pltpu.VMEM)
    out_shape = [jax.ShapeDtypeStruct(shape, f) for shape in shapes]
    pile = jax.ShapeDtypeStruct((count,) + slots_out[0].shape, slots_out[0].dtype)
    return pl.pallas_call(
        functools.partial(finish_kernel, tuple(steps), count),
        out_shape=out_shape + [pile, pile],
        in_specs=[any_spec, vmem_spec] + [any_spec] * (2 * count),
        out_specs=[any_spec] * 4 + [vmem_spec] * 4 + [any_spec] * 2,
        scratch_shapes=[
            pltpu.VMEM((DEPTH, width, width), jnp.bfloat16),
            pltpu.VMEM((DEPTH, width, width), f),
            pltpu.VMEM((2 * count,) + slots_out[0].shape, slots_out[0].dtype),
            pltpu.SemaphoreType.DMA((DEPTH,)),
            pltpu.SemaphoreType.DMA((DEPTH,)),
            pltpu.SemaphoreType.DMA((2 * count,)),
            pltpu.SemaphoreType.DMA((2 * count,)),
        ],
        compiler_params=pltpu.CompilerParams(vmem_limit_bytes=VMEM_BYTES),
    )(rows, vectors, *slots_out, *slots_grad)


def passed_along(block, axis, distance):
    devices = range(lax.axis_size(axis))
    route = [(i - distance, i) for i in devices if i - distance in devices]
    return lax.ppermute(block, axis, route)


def shards(
    inputs,
    cotangent,
    lengths,
    assign,
    query_key_value,
    out_weight,
    up_weight,
    down_weight,
    model_gains,
    model_shifts,
    hidden_gains,
    hidden_shifts,
):
    micro_count = inputs.shape[0]
    hidden = up_weight.shape[2]
    slots = range(micro_count)
    weights = {
        N.wq: query_key_value[0],
        N.wo: out_weight[0],
        N.wu: up_weight[0],
        N.wd: down_weight[0],
    }
    vectors = (model_gains, model_shifts, hidden_gains, hidden_shifts)

    def run(steps, plane, slot, given, previous):
        return layer_call(
            steps, plane, slot, (lengths, assign), {**weights, **given}, vectors, previous
        )

    lower = [run((N.forward,), 0, slot, {N.x: inputs}, {}) for slot in slots]
    middle = [passed_along(lower[slot][N.y], "pipe", 1) for slot in slots]
    upper = [
        run(
            (N.forward, N.backward),
            1,
            slot,
            {N.x: middle[slot], N.dy: cotangent},
            lower[slot],
        )
        for slot in slots
    ]
    returned = [passed_along(upper[slot][N.dx], "pipe", -1) for slot in slots]
    kept = [{**lower[slot], **upper[slot]} for slot in slots]
    grads = [
        run((N.backward,), 0, slot, {**kept[slot], N.x: inputs, N.dy: returned[slot]}, kept[slot])
        for slot in slots
    ]
    devices = lax.axis_size("batch")
    parts = [weight_grads(kept[slot], grads[slot], devices) for slot in slots]
    rows, vectors = ring_sum(parts, [grads[slot][N.sums] for slot in slots], devices)
    outs = finish(
        rows,
        vectors,
        [kept[slot][N.y] for slot in slots],
        [grads[slot][N.dx] for slot in slots],
        hidden,
    )
    return tuple(item[None] for item in outs[8:] + outs[:6]) + (outs[6], outs[7][None])


def solution(mesh):
    return jax.shard_map(
        shards,
        mesh=mesh,
        in_specs=(
            P(None, "batch", None),
            P(None, "batch", None),
            P("batch"),
            P("batch"),
            P("pipe", None, None),
            P("pipe", None, None),
            P("pipe", None, None),
            P("pipe", None, None),
            P("pipe", None, None),
            P("pipe", None, None),
            P("pipe", None),
            P("pipe", None, None),
        ),
        out_specs=(
            P("pipe", None, "batch", None),
            P("pipe", None, "batch", None),
            P("pipe", None, None),
            P("pipe", None, None),
            P("pipe", None, None),
            P("pipe", None, None),
            P("pipe", None, None),
            P("pipe", None, None),
            P("pipe", None),
            P("pipe", None, None),
        ),
        check_vma=False,
    )
```

```python
import functools
import types

import jax
import jax.numpy as jnp
from jax import lax
from jax.experimental import pallas as pl
from jax.experimental.pallas import tpu as pltpu
from jax.sharding import PartitionSpec as P

HEAD = 64
PAIR = 2 * HEAD
EPSILON = 1e-05
SCALE = 0.125
HIDDEN_NEG = -1e30
CHUNK = 512
SUM_ROWS = 32
DEPTH = 3
HEAD_ROWS = 16

TILE = 16
VMEM_BYTES = 60 * 1024 * 1024
MESH_IDS = pl.DeviceIdType.MESH


def named(**given):
    return types.SimpleNamespace(**{name: name for name in given})


N = named(
    x=0,
    dy=0,
    y=0,
    dx=0,
    wq=0,
    wo=0,
    wu=0,
    wd=0,
    normed_in=0,
    projected=0,
    log_total=0,
    attended=0,
    normed_mix=0,
    residual=0,
    normed_ffn=0,
    normed_hidden=0,
    slope=0,
    spread=0,
    d_down=0,
    d_pre=0,
    d_branch=0,
    d_proj=0,
    sums=0,
    wide_scratch=0,
    d_residual=0,
    d_attended=0,
    delta=0,
    bias=0,
    bias_back=0,
    forward=0,
    backward=0,
)


def dot_nn(left, right):
    return jnp.dot(left, right, preferred_element_type=jnp.float32)


def dot_nt(left, right):
    return lax.dot_general(
        left, right, (((1,), (1,)), ((), ())), preferred_element_type=jnp.float32
    )


def standardize(values_in):
    centred = values_in - jnp.mean(values_in, axis=-1, keepdims=True)
    scale = lax.rsqrt(jnp.mean(centred * centred, axis=-1, keepdims=True) + EPSILON)
    return centred * scale, scale


def unit_backward(grad, unit, scale, gain):
    scaled = grad * gain
    first = jnp.mean(scaled, axis=-1, keepdims=True)
    second = jnp.mean(scaled * unit, axis=-1, keepdims=True)
    return (
        scale * (scaled - first - unit * second),
        jnp.sum(grad * unit, axis=0, keepdims=True),
        jnp.sum(grad, axis=0, keepdims=True),
    )


def column_sum(values):
    return jnp.sum(values.astype(jnp.float32), axis=0, keepdims=True)


def hiding_bias(rows, length, query_dim):
    query = lax.broadcasted_iota(jnp.int32, (rows, rows), query_dim)
    key = lax.broadcasted_iota(jnp.int32, (rows, rows), 1 - query_dim)
    visible = (key <= query) & ((key < length) | (key == query))
    return jnp.where(visible, 0.0, HIDDEN_NEG)


def own_lanes(values, which):
    lane = lax.broadcasted_iota(jnp.int32, values.shape, 1)
    mine = (lane >= HEAD) if which else (lane < HEAD)
    return jnp.where(mine, values, jnp.zeros_like(values))


def attend_forward(projected, attended, log_total, bias):
    rows, width = attended.shape
    half = rows // 2
    lane = lax.broadcasted_iota(jnp.int32, (half, PAIR), 1)

    def one_pair(pair, totals):
        first = pl.multiple_of(pair * PAIR, PAIR)
        items = []
        for block in range(2):
            at = slice(block * half, (block + 1) * half)
            reach = (block + 1) * half
            q = projected[at, pl.ds(first, PAIR)] * jnp.bfloat16(SCALE)
            k = projected[0:reach, pl.ds(width + first, PAIR)]
            v = projected[0:reach, pl.ds(2 * width + first, PAIR)]
            items += [(at, reach, own_lanes(q, which), k, v) for which in range(2)]
        scores = [dot_nt(q, k) + bias[at, 0:reach] for at, reach, q, k, v in items]
        softened = []
        for item in scores:
            top = jnp.max(item, axis=-1, keepdims=True)
            exps = jnp.exp(item - top)
            softened.append((exps, jnp.sum(exps, axis=-1, keepdims=True), top))
        mixed = [
            dot_nn(exps.astype(jnp.bfloat16), item[4]) * (1.0 / total)
            for item, (exps, total, top) in zip(items, softened)
        ]
        new_totals = []
        for block in range(2):
            at = items[2 * block][0]
            attended[at, pl.ds(first, PAIR)] = jnp.where(
                lane < HEAD, mixed[2 * block], mixed[2 * block + 1]
            )
            logs = totals[block]
            for which in range(2):
                exps, total, top = softened[2 * block + which]
                logs = jnp.where(lane == 2 * pair + which, top + jnp.log(total), logs)
            new_totals.append(logs)
        return tuple(new_totals)

    zero = jnp.zeros((half, PAIR), jnp.float32)
    totals = lax.fori_loop(0, width // PAIR, one_pair, (zero, zero), unroll=2)
    for block in range(2):
        log_total[:, block * half : (block + 1) * half] = totals[block].T[0:HEAD_ROWS]


def attend_backward(projected, d_attended, log_total, delta, bias, d_proj, tick):
    rows, width = d_attended.shape
    half = rows // 2

    def one_pair(pair, carry):
        first = pl.multiple_of(pair * PAIR, PAIR)
        k_all = projected[:, pl.ds(width + first, PAIR)]
        v_all = projected[:, pl.ds(2 * width + first, PAIR)]
        k_turned = k_all.T
        items = []
        for block in range(2):
            at = slice(block * half, (block + 1) * half)
            q = projected[at, pl.ds(first, PAIR)] * jnp.bfloat16(SCALE)
            grad = d_attended[at, pl.ds(first, PAIR)]
            for which in range(2):
                items.append((block, which, at, own_lanes(q, which), own_lanes(grad, which)))
        raw = []
        for block, which, at, q, grad in items:
            reach = (block + 1) * half
            raw.append((dot_nt(k_all[0:reach], q), dot_nt(v_all[0:reach], grad)))
        shaped = []
        for (block, which, at, q, grad), (scores, d_probs) in zip(items, raw):
            reach = (block + 1) * half
            head = pl.ds(2 * pair + which, 1)
            probs = jnp.exp(scores + bias[0:reach, at] - log_total[head, at])
            d_scores = (probs * (d_probs - delta[head, at])).astype(jnp.bfloat16)
            shaped.append((probs.astype(jnp.bfloat16), d_scores))
        dk = [None, None]
        dv = [None, None]
        dq = []
        for (block, which, at, q, grad), (probs, d_scores) in zip(items, shaped):
            reach = (block + 1) * half
            more_v = dot_nn(probs, grad)
            more_k = dot_nn(d_scores, q)
            dq.append(dot_nn(k_turned[which * HEAD : (which + 1) * HEAD, 0:reach], d_scores))
            for part in range(block + 1):
                piece = slice(part * half, (part + 1) * half)
                dv[part] = more_v[piece] if dv[part] is None else dv[part] + more_v[piece]
                dk[part] = more_k[piece] if dk[part] is None else dk[part] + more_k[piece]
        for block in range(2):
            at = slice(block * half, (block + 1) * half)
            turned = jnp.concatenate(dq[2 * block : 2 * block + 2], axis=0) * SCALE
            d_proj[at, pl.ds(first, PAIR)] = turned.T.astype(jnp.bfloat16)
            d_proj[at, pl.ds(width + first, PAIR)] = dk[block].astype(jnp.bfloat16)
            d_proj[at, pl.ds(2 * width + first, PAIR)] = dv[block].astype(jnp.bfloat16)
        return carry

    if tick is None:
        lax.fori_loop(0, width // PAIR, one_pair, 0, unroll=2)
    else:
        for first in range(0, width // PAIR, 2):
            lax.fori_loop(first, min(first + 2, width // PAIR), one_pair, 0, unroll=True)
            tick()


KEPT = (N.normed_in, N.projected, N.log_total, N.attended, N.normed_mix, N.residual,
        N.normed_ffn, N.normed_hidden, N.slope, N.spread)
GRADS = (N.d_down, N.d_pre, N.d_branch, N.d_proj, N.sums)


def buffer_shapes(rows, width, hidden):
    bf, f = jnp.bfloat16, jnp.float32
    return {
        N.x: ((rows, width), bf),
        N.dy: ((rows, width), bf),
        N.y: ((rows, width), bf),
        N.dx: ((rows, width), bf),
        N.wq: ((width, 3 * width), bf),
        N.wo: ((width, width), bf),
        N.wu: ((width, hidden), bf),
        N.wd: ((hidden, width), bf),
        N.normed_in: ((rows, width), bf),
        N.projected: ((rows, 3 * width), bf),
        N.log_total: ((HEAD_ROWS, rows), f),
        N.attended: ((rows, width), f),
        N.normed_mix: ((rows, width), bf),
        N.residual: ((rows, width), f),
        N.normed_ffn: ((rows, width), bf),
        N.normed_hidden: ((rows, hidden), bf),
        N.slope: ((rows, hidden), bf),
        N.spread: ((rows, PAIR), f),
        N.d_down: ((rows, width), bf),
        N.d_pre: ((rows, hidden), bf),
        N.d_branch: ((rows, width), bf),
        N.d_proj: ((rows, 3 * width), bf),
        N.sums: ((SUM_ROWS, width), f),
        N.wide_scratch: ((rows, hidden), f),
        N.d_residual: ((rows, width), f),
        N.d_attended: ((rows, width), bf),
        N.delta: ((HEAD_ROWS, rows), f),
        N.bias: ((rows, rows), f),
        N.bias_back: ((rows, rows), f),
    }


def forward_body(held, vectors, length, ready, emit):
    gm, sm, gh, sh = vectors
    gm, sm, sh = gm.at[0], sm.at[0], sh.at[0]
    bf = jnp.bfloat16
    rows, width = held[N.x].shape
    hidden = held[N.wu].shape[1]
    wide_scratch = held[N.wide_scratch]
    held[N.bias][...] = hiding_bias(rows, length, 0)
    ready(N.x)
    unit, unused = standardize(held[N.x][...].astype(jnp.float32))
    held[N.normed_in][...] = (unit * gm[0:1, :] + sm[0:1, :]).astype(bf)
    emit(N.normed_in)
    for block in range(3):
        cols = slice(block * width, (block + 1) * width)
        ready(N.wq)
        out = dot_nn(held[N.normed_in][...], held[N.wq][:, cols])
        if block != 1:
            out = out + sm[1 + block // 2 : 2 + block // 2, :]
        held[N.projected][:, cols] = out.astype(bf)
    emit(N.projected)
    attend_forward(held[N.projected], held[N.attended], held[N.log_total], held[N.bias])
    emit(N.log_total)
    emit(N.attended)

    unit, unused = standardize(held[N.attended][...])
    held[N.normed_mix][...] = (unit * gm[1:2, :] + sm[3:4, :]).astype(bf)
    emit(N.normed_mix)
    ready(N.wo)
    residual = held[N.x][...].astype(jnp.float32) + sm[4:5, :]
    residual = residual + dot_nn(held[N.normed_mix][...], held[N.wo][...])
    held[N.residual][...] = residual
    emit(N.residual)
    unit, unused = standardize(residual)
    held[N.normed_ffn][...] = (unit * gm[2:3, :] + sm[5:6, :]).astype(bf)
    emit(N.normed_ffn)
    ready(N.wu)
    total = jnp.zeros((rows, 1), jnp.float32)
    for first in range(0, hidden, CHUNK):
        cols = slice(first, first + CHUNK)
        pre = dot_nn(held[N.normed_ffn][...], held[N.wu][:, cols]) + sh[0:1, cols]
        share = 0.5 + 0.5 * lax.erf(pre * 0.7071067811865476)
        density = 0.3989422804014327 * jnp.exp(-0.5 * pre * pre)
        act = pre * share
        held[N.slope][:, cols] = (share + pre * density).astype(bf)
        wide_scratch[:, cols] = act
        total = total + jnp.sum(act, axis=-1, keepdims=True)
    emit(N.slope)
    mean = total * (1.0 / hidden)
    square = jnp.zeros((rows, 1), jnp.float32)
    for first in range(0, hidden, CHUNK):
        centred = wide_scratch[:, first : first + CHUNK] - mean
        square = square + jnp.sum(centred * centred, axis=-1, keepdims=True)
    scale = lax.rsqrt(square * (1.0 / hidden) + EPSILON)
    held[N.spread][...] = jnp.broadcast_to(scale, (rows, PAIR))
    emit(N.spread)
    for first in range(0, hidden, CHUNK):
        cols = slice(first, first + CHUNK)
        unit = (wide_scratch[:, cols] - mean) * scale
        held[N.normed_hidden][:, cols] = (unit * gh[0:1, cols] + sh[1:2, cols]).astype(bf)
    emit(N.normed_hidden)
    ready(N.wd)
    out = held[N.residual][...] + dot_nn(held[N.normed_hidden][...], held[N.wd][...])
    held[N.y][...] = (out + sm[6:7, :]).astype(bf)
    emit(N.y)


def backward_body(held, vectors, length, masked, ready, emit, tick=None):
    gm, sm, gh, sh = vectors
    gm, sm, sh = gm.at[0], sm.at[0], sh.at[0]
    bf = jnp.bfloat16
    rows, width = held[N.x].shape
    hidden = held[N.wu].shape[1]
    wide = hidden // width
    wide_scratch, sums = held[N.wide_scratch], held[N.sums]
    sums[...] = jnp.zeros_like(sums)
    held[N.bias_back][...] = hiding_bias(rows, length, 1)
    ready(N.dy)
    d_down = held[N.dy][...]
    if masked:
        live = lax.broadcasted_iota(jnp.int32, (rows, 1), 0) < length
        d_down = jnp.where(live, d_down.astype(jnp.float32), 0.0).astype(bf)
    if tick is None:
        held[N.d_down][...] = d_down
    emit(N.d_down)
    sums[9:10, :] = column_sum(d_down)

    first_total = jnp.zeros((rows, 1), jnp.float32)
    second_total = jnp.zeros((rows, 1), jnp.float32)
    for block in range(wide):
        cols = slice(block * width, (block + 1) * width)
        ready(N.wd)
        ready(N.normed_hidden)
        grad = dot_nt(held[N.d_down][...], held[N.wd][cols, :])
        normed = held[N.normed_hidden][:, cols].astype(jnp.float32)
        unit = (normed - sh[1:2, cols]) * (1.0 / gh[0:1, cols])
        sums[10 + block : 11 + block, :] = jnp.sum(grad * unit, axis=0, keepdims=True)
        sums[18 + block : 19 + block, :] = jnp.sum(grad, axis=0, keepdims=True)
        scaled = grad * gh[0:1, cols]
        wide_scratch[:, cols] = scaled
        first_total = first_total + jnp.sum(scaled, axis=-1, keepdims=True)
        second_total = second_total + jnp.sum(scaled * unit, axis=-1, keepdims=True)
        if tick is not None and block == wide // 2 - 1:
            tick()
    first_mean = first_total * (1.0 / hidden)
    second_mean = second_total * (1.0 / hidden)
    ready(N.spread)
    ready(N.slope)
    scale = held[N.spread][:, 0:1]
    for block in range(wide):
        cols = slice(block * width, (block + 1) * width)
        normed = held[N.normed_hidden][:, cols].astype(jnp.float32)
        unit = (normed - sh[1:2, cols]) * (1.0 / gh[0:1, cols])
        d_act = scale * (wide_scratch[:, cols] - first_mean - unit * second_mean)
        d_pre = (d_act * held[N.slope][:, cols].astype(jnp.float32)).astype(bf)
        held[N.d_pre][:, cols] = d_pre
        sums[14 + block : 15 + block, :] = column_sum(d_pre)
    emit(N.d_pre)
    if tick is not None:
        tick()

    ready(N.wu)
    d_ffn = dot_nt(held[N.d_pre][...], held[N.wu][...])
    ready(N.residual)
    unit, scale = standardize(held[N.residual][...])
    through, gain_sum, shift_sum = unit_backward(d_ffn, unit, scale, gm[2:3, :])
    sums[2:3, :] = gain_sum
    sums[8:9, :] = shift_sum
    through = through + held[N.d_down][...].astype(jnp.float32)
    held[N.d_residual][...] = through
    held[N.d_branch][...] = through.astype(bf)
    emit(N.d_branch)
    sums[7:8, :] = column_sum(held[N.d_branch][...])
    if tick is not None:
        tick()

    ready(N.wo)
    d_mix = dot_nt(held[N.d_branch][...], held[N.wo][...])
    ready(N.attended)
    attended = held[N.attended][...]
    unit, scale = standardize(attended)
    through, gain_sum, shift_sum = unit_backward(d_mix, unit, scale, gm[1:2, :])
    sums[1:2, :] = gain_sum
    sums[6:7, :] = shift_sum
    held[N.d_attended][...] = through.astype(bf)
    product = held[N.d_attended][...].astype(jnp.float32) * attended
    upper = product.astype(bf)
    lower = (product - upper.astype(jnp.float32)).astype(bf)
    head_row = lax.broadcasted_iota(jnp.int32, (HEAD_ROWS, width), 0)
    head_col = lax.broadcasted_iota(jnp.int32, (HEAD_ROWS, width), 1) // HEAD
    chooser = jnp.where(head_row == head_col, 1.0, 0.0).astype(bf)
    held[N.delta][...] = dot_nt(chooser, upper) + dot_nt(chooser, lower)
    if tick is not None:
        tick()

    ready(N.projected)
    ready(N.log_total)
    attend_backward(
        held[N.projected], held[N.d_attended], held[N.log_total], held[N.delta],
        held[N.bias_back], held[N.d_proj], tick,
    )
    emit(N.d_proj)
    ready(N.wq)
    d_norm = dot_nt(held[N.d_proj][...], held[N.wq][...])
    sums[4:5, :] = column_sum(held[N.d_proj][:, 0:width])
    sums[5:6, :] = column_sum(held[N.d_proj][:, 2 * width :])
    ready(N.x)
    unit, scale = standardize(held[N.x][...].astype(jnp.float32))
    through, gain_sum, shift_sum = unit_backward(d_norm, unit, scale, gm[0:1, :])
    sums[0:1, :] = gain_sum
    sums[3:4, :] = shift_sum
    held[N.dx][...] = (through + held[N.d_residual][...]).astype(bf)
    emit(N.dx)
    emit(N.sums)


def slot_length(lengths_ref, assign_ref, slot):
    total = jnp.int32(0)
    for at in range(lengths_ref.shape[0]):
        total = total + jnp.where(assign_ref[at] == slot, lengths_ref[at], 0)
    return total


def layer_kernel(
    steps, plane, slot, groups, stacked, out_names, unread, buffers, lengths_ref, assign_ref, *refs
):
    in_names = sum(groups, ())
    sources = dict(zip(in_names, refs))
    for name in stacked:
        sources[name] = sources[name].at[slot]
    vectors = refs[len(in_names) : len(in_names) + 4]
    refs = refs[len(in_names) + 4 + unread :]
    targets = dict(zip(out_names, refs))
    refs = refs[len(out_names) :]
    held = dict(zip(buffers, refs))
    in_sem, out_sem = refs[len(buffers) :]

    @pl.when(lax.axis_index("pipe") == plane)
    def _():
        loads = {
            name: pltpu.make_async_copy(sources[name], held[name], in_sem.at[at])
            for at, name in enumerate(in_names)
        }
        stores = {
            name: pltpu.make_async_copy(held[name], targets[name], out_sem.at[at])
            for at, name in enumerate(out_names)
        }
        for name in in_names:
            loads[name].start()
        waited = set()

        def ready(name):
            for group in groups:
                if name in group and name not in waited:
                    waited.update(group)
                    for item in group:
                        loads[item].wait()

        def emit(name):
            if name in stores:
                stores[name].start()

        length = slot_length(lengths_ref, assign_ref, slot)
        if N.forward in steps:
            forward_body(held, vectors, length, ready, emit)
        if N.backward in steps:
            backward_body(held, vectors, length, N.forward in steps, ready, emit)
        for name in out_names:
            stores[name].wait()


FORWARD_ONLY = (N.projected, N.log_total, N.attended, N.residual, N.slope, N.spread)


def layer_call(steps, plane, slot, sizes, given, vectors, previous, after=()):
    stacked = tuple(name for name in (N.x, N.dy) if name in given and given[name].ndim == 3)
    rows, width = given[N.x].shape[-2:]
    hidden = given[N.wu].shape[1]
    shapes = buffer_shapes(rows, width, hidden)
    if steps == (N.forward,):
        groups = ((N.x, N.wq), (N.wo, N.wu, N.wd))
        out_names = (N.y,) + KEPT
        spare = (N.wide_scratch, N.bias)
    elif steps == (N.backward,):
        groups = ((N.dy, N.wd, N.normed_hidden), (N.spread, N.slope, N.wu, N.residual),
                  (N.wo, N.attended, N.projected, N.log_total), (N.wq, N.x))
        out_names = (N.dx,) + GRADS
        spare = (N.wide_scratch, N.bias_back, N.d_residual, N.d_attended, N.delta)
    else:
        groups = ((N.x, N.wq), (N.wo, N.wu), (N.wd, N.dy))
        out_names = (N.y,) + tuple(name for name in KEPT if name not in FORWARD_ONLY)
        out_names += (N.dx,) + GRADS
        spare = (N.wide_scratch, N.bias, N.bias_back, N.d_residual, N.d_attended, N.delta)
        spare += FORWARD_ONLY
    in_names = sum(groups, ())
    buffers = in_names + tuple(name for name in out_names if name not in in_names) + spare
    any_spec = pl.BlockSpec(memory_space=pl.ANY)
    vmem_spec = pl.BlockSpec(memory_space=pltpu.VMEM)
    smem_spec = pl.BlockSpec(memory_space=pltpu.SMEM)
    in_specs = [smem_spec] * 2 + [any_spec] * len(in_names) + [vmem_spec] * 4
    args = list(sizes) + [given[name] for name in in_names] + list(vectors)
    shared = [name for name in out_names if name in previous]
    aliases = {len(args) + at: out_names.index(name) for at, name in enumerate(shared)}
    in_specs += [any_spec] * len(shared)
    args += [previous[name] for name in shared]
    in_specs += [any_spec] * len(after)
    args += list(after)
    scratch = [pltpu.VMEM(*shapes[name]) for name in buffers]
    scratch.append(pltpu.SemaphoreType.DMA((len(in_names),)))
    scratch.append(pltpu.SemaphoreType.DMA((len(out_names),)))
    outs = pl.pallas_call(
        functools.partial(
            layer_kernel, steps, plane, slot, groups, stacked, out_names, len(shared + list(after)), buffers
        ),
        out_shape=[jax.ShapeDtypeStruct(*shapes[name]) for name in out_names],
        in_specs=in_specs,
        out_specs=[any_spec] * len(out_names),
        input_output_aliases=aliases,
        scratch_shapes=scratch,
        compiler_params=pltpu.CompilerParams(vmem_limit_bytes=VMEM_BYTES),
        cost_estimate=pl.CostEstimate(
            flops=len(steps) * 2 * rows * width * (4 * width + 2 * hidden),
            bytes_accessed=40_000_000,
            transcendentals=0,
        ),
    )(*args)
    return dict(zip(out_names, outs))


LEFT = (N.normed_hidden, N.normed_ffn, N.normed_mix, N.normed_in)
RIGHT = (N.d_down, N.d_pre, N.d_branch, N.d_proj)


def down_rows(width, hidden, devices):
    return hidden + -hidden % (TILE * devices)


def rest_rows(width, hidden, devices):
    rows = 4 * width + hidden
    return rows + -rows % (TILE * devices)


def weight_grad_kernel(*refs):
    parts = len(LEFT)
    sources, refs = refs[: 2 * parts], refs[2 * parts :]
    targets, scratch = refs[:2], refs[2:]
    left, right = scratch[0:parts], scratch[parts : 2 * parts]
    out_s = scratch[2 * parts : 2 * parts + 2]
    turned, in_sem, out_sem = scratch[2 * parts + 2 :]
    width = left[3].shape[1]
    wide = left[0].shape[1] // width
    loads = [
        pltpu.make_async_copy(source, target, in_sem.at[at])
        for at, (source, target) in enumerate(zip(sources, left + right))
    ]
    for part in range(parts):
        loads[part].start()
        loads[parts + part].start()
    starts = (0, 4, 3, 0)
    stores = []

    def store(which, first, count):
        at = pl.ds(first, count)
        stores.append(
            pltpu.make_async_copy(
                out_s[which].at[at], targets[which].at[at], out_sem.at[len(stores)]
            )
        )
        stores[-1].start()

    for part in range(parts):
        loads[part].wait()
        loads[parts + part].wait()
        first = starts[part] * width
        if part == 0:

            def one(block, carry):
                at = pl.ds(pl.multiple_of(block * width, width), width)
                turned[...] = left[part][:, at].T
                out_s[0][at, :] = dot_nn(turned[...], right[part][...]).astype(jnp.bfloat16)
                return carry

            lax.fori_loop(0, wide, one, 0)
            used = wide * width
            if out_s[0].shape[0] > used:
                rest = out_s[0].shape[0] - used
                out_s[0][used:, :] = jnp.zeros((rest, width), jnp.bfloat16)
            store(0, 0, out_s[0].shape[0])
        else:
            turned[...] = left[part][...].T
            blocks = right[part].shape[1] // width

            def one(block, carry):
                cols = pl.ds(pl.multiple_of(block * width, width), width)
                at = pl.ds(pl.multiple_of(first + block * width, width), width)
                out_s[1][at, :] = dot_nn(turned[...], right[part][:, cols]).astype(jnp.bfloat16)
                return carry

            lax.fori_loop(0, blocks, one, 0)
            store(1, first, blocks * width)
    used = (4 + wide) * width
    rest = out_s[1].shape[0] - used
    if rest:
        out_s[1][used:, :] = jnp.zeros((rest, width), jnp.bfloat16)
        store(1, used, rest)
    for item in stores:
        item.wait()


def weight_grads(kept, grads, devices):
    args = [kept[name] for name in LEFT] + [grads[name] for name in RIGHT]
    rows, width = kept[N.normed_in].shape
    hidden = kept[N.normed_hidden].shape[1]
    bf = jnp.bfloat16
    shapes = [(down_rows(width, hidden, devices), width), (rest_rows(width, hidden, devices), width)]
    any_spec = pl.BlockSpec(memory_space=pl.ANY)
    scratch = [pltpu.VMEM(item.shape, bf) for item in args]
    scratch += [pltpu.VMEM(shape, bf) for shape in shapes]
    scratch += [
        pltpu.VMEM((width, rows), bf),
        pltpu.SemaphoreType.DMA((len(args),)),
        pltpu.SemaphoreType.DMA((5,)),
    ]
    return pl.pallas_call(
        weight_grad_kernel,
        out_shape=[jax.ShapeDtypeStruct(shape, bf) for shape in shapes],
        in_specs=[any_spec] * len(args),
        out_specs=[any_spec] * 2,
        scratch_shapes=scratch,
        compiler_params=pltpu.CompilerParams(vmem_limit_bytes=VMEM_BYTES),
        cost_estimate=pl.CostEstimate(
            flops=2 * rows * width * (4 * width + 2 * hidden),
            bytes_accessed=30_000_000,
            transcendentals=0,
        ),
    )(*args)


def down_grad_kernel(
    hidden_hbm, lower_hbm, upper_hbm, base_hbm, out_hbm, hidden_s, grad_s, base_s, out_s, in_sem,
    out_sem
):
    width = grad_s.shape[1]
    wide = hidden_s.shape[1] // width

    @pl.when(lax.axis_index("pipe") == 0)
    def _():
        pltpu.make_async_copy(lower_hbm, grad_s, in_sem.at[0]).start()

    @pl.when(lax.axis_index("pipe") != 0)
    def _():
        pltpu.make_async_copy(upper_hbm, grad_s, in_sem.at[0]).start()

    blocks = [pl.ds(block * width, width) for block in range(wide)]
    lefts = [
        pltpu.make_async_copy(hidden_hbm.at[:, at], hidden_s.at[:, at], in_sem.at[1 + block])
        for block, at in enumerate(blocks)
    ]
    base = pltpu.make_async_copy(base_hbm, base_s, in_sem.at[1 + wide])
    for item in lefts:
        item.start()
    base.start()
    pltpu.make_async_copy(lower_hbm, grad_s, in_sem.at[0]).wait()
    stores = []
    for block, at in enumerate(blocks):
        lefts[block].wait()
        if block == 0:
            base.wait()
        product = dot_nn(hidden_s[:, at].T, grad_s[...])
        out_s[at, :] = (product + base_s[at, :].astype(jnp.float32)).astype(jnp.bfloat16)
        stores.append(pltpu.make_async_copy(out_s.at[at], out_hbm.at[at], out_sem.at[block]))
        stores[-1].start()
    used = wide * width
    rest = out_s.shape[0] - used
    if rest:
        out_s[used:, :] = jnp.zeros((rest, width), jnp.bfloat16)
        at = pl.ds(used, rest)
        stores.append(pltpu.make_async_copy(out_s.at[at], out_hbm.at[at], out_sem.at[wide]))
        stores[-1].start()
    for item in stores:
        item.wait()


def down_grad(normed_hidden, lower_grad, upper_grad, base):
    bf = jnp.bfloat16
    wide = normed_hidden.shape[1] // lower_grad.shape[1]
    any_spec = pl.BlockSpec(memory_space=pl.ANY)
    return pl.pallas_call(
        down_grad_kernel,
        out_shape=jax.ShapeDtypeStruct(base.shape, bf),
        in_specs=[any_spec] * 4,
        out_specs=any_spec,
        scratch_shapes=[
            pltpu.VMEM(normed_hidden.shape, bf),
            pltpu.VMEM(lower_grad.shape, bf),
            pltpu.VMEM(base.shape, bf),
            pltpu.VMEM(base.shape, bf),
            pltpu.SemaphoreType.DMA((wide + 2,)),
            pltpu.SemaphoreType.DMA((wide + 1,)),
        ],
        compiler_params=pltpu.CompilerParams(vmem_limit_bytes=VMEM_BYTES),
        cost_estimate=pl.CostEstimate(
            flops=2 * normed_hidden.size * lower_grad.shape[1],
            bytes_accessed=14_000_000,
            transcendentals=0,
        ),
    )(normed_hidden, lower_grad, upper_grad, base)


def ring_places(chips):
    line_len = chips // 2
    pipe = lax.axis_index("pipe")
    batch = lax.axis_index("batch")
    core = batch % 2
    side = (batch // 2) % 2
    line = batch // 4
    place = line * (1 - side) + (chips - 1 - line) * side

    def chip_at(spot):
        far = spot // line_len
        along = spot * (1 - far) + (chips - 1 - spot) * far
        return (pipe, (along * 2 + far) * 2 + core)

    onward = chip_at((place + 1) % chips)
    backward = chip_at((place + chips - 1) % chips)
    twin = (pipe, batch + 1 - 2 * core)
    return place, core, onward, backward, twin


def greet(devices):
    barrier = pltpu.get_barrier_semaphore()
    for other in devices:
        pl.semaphore_signal(barrier, inc=1, device_id=other, device_id_type=MESH_IDS)
    return barrier


class Ring:
    def __init__(self, chips, lanes, places, parts, sum_ref, buffers, sems):
        self.chips, self.lanes, self.parts, self.sum_ref = chips, lanes, parts, sum_ref
        self.place, self.core, self.onward, self.backward, self.twin = places
        count = len(parts)
        self.own, self.from_core = buffers[:count], buffers[count : 2 * count]
        self.arriving, self.final = buffers[2 * count :]
        self.held = self.own[0]
        (self.load_sem, self.core_send, self.core_recv, self.ring_send, self.ring_recv,
         self.spread_send, self.spread_recv, self.cross_send, self.cross_recv,
         self.store_sem) = sems

    def chunk_of(self, rank):
        half_up = (rank + 1) // 2
        sign = 1 - 2 * (rank % 2)
        return (self.place + self.chips + sign * half_up) % self.chips

    def load(self, rank, which):
        chunk = self.chunk_of(rank)
        return pltpu.make_async_copy(
            self.parts[which].at[self.core, chunk],
            self.own[which].at[chunk],
            self.load_sem.at[which, rank],
        )

    def remote(self, source, target, send_sem, recv_sem, device):
        return pltpu.make_async_remote_copy(
            src_ref=source,
            dst_ref=target,
            send_sem=send_sem,
            recv_sem=recv_sem,
            device_id=device,
            device_id_type=MESH_IDS,
        )

    def swap(self, rank, which):
        chunk = self.chunk_of(rank)
        return self.remote(
            self.parts[which].at[1 - self.core, chunk],
            self.from_core[which].at[chunk],
            self.core_send.at[which, rank],
            self.core_recv.at[which, rank],
            self.twin,
        )

    def start_loads(self):
        for rank in range(self.chips):
            for which in range(len(self.parts)):
                self.load(rank, which).start()

    def start_swaps(self):
        for rank in range(self.chips):
            for which in range(len(self.parts)):
                self.swap(rank, which).start()

    def add_rows(self, chunk, first, count, sources):
        def one(index, carry):
            rows = pl.ds(pl.multiple_of(first + index * TILE, TILE), TILE)
            total = self.held[chunk, rows, :].astype(jnp.float32)
            for source in sources:
                total = total + source[rows, :].astype(jnp.float32)
            self.held[chunk, rows, :] = total.astype(jnp.bfloat16)
            return carry

        lax.fori_loop(0, count // TILE, one, 0)

    def prepare(self, rank):
        chunk = self.chunk_of(rank)
        for which in range(len(self.parts)):
            self.load(rank, which).wait()
            self.swap(rank, which).wait_recv()
        sources = [item.at[chunk] for item in self.own[1:] + self.from_core]
        self.add_rows(chunk, 0, self.held.shape[1], sources)

    def neighbour(self, lane):
        return self.onward if self.lanes[lane][0] > 0 else self.backward

    def ring_chunk(self, lane, step):
        return (self.place + (self.chips - 1) * self.chips - self.lanes[lane][0] * step) % self.chips

    def ring_copy(self, lane, step):
        sign, first, count = self.lanes[lane]
        rows = pl.ds(first, count)
        return self.remote(
            self.held.at[self.ring_chunk(lane, step), rows],
            self.arriving.at[step, rows],
            self.ring_send.at[lane, step],
            self.ring_recv.at[lane, step],
            self.neighbour(lane),
        )

    def take(self, lane, step):
        sign, first, count = self.lanes[lane]
        self.ring_copy(lane, step - 1).wait_recv()
        chunk = self.ring_chunk(lane, step)
        self.add_rows(chunk, first, count, [self.arriving.at[step - 1]])

    def first(self):
        self.prepare(0)
        for lane in range(len(self.lanes)):
            self.ring_copy(lane, 0).start()

    def reduce_step(self, step):
        for rank in (2 * step - 1, 2 * step):

            @pl.when(rank < self.chips)
            def _():
                self.prepare(rank)

        for lane in range(len(self.lanes)):
            self.take(lane, step)
            self.ring_copy(lane, step).start()

    def spread_parts(self, lane, step):
        sign, first, count = self.lanes[lane]
        chunk = (self.place + (self.chips + 1) * self.chips + sign * (1 - step)) % self.chips
        return chunk, pl.ds(first, count)

    def spread_copy(self, lane, step, source):
        chunk, rows = self.spread_parts(lane, step)
        return self.remote(
            source.at[chunk, rows],
            self.final.at[chunk, rows],
            self.spread_send.at[lane, step],
            self.spread_recv.at[lane, step],
            self.neighbour(lane),
        )

    def cross_copy(self, lane, step, source):
        chunk, rows = self.spread_parts(lane, step)
        return self.remote(
            source.at[chunk, rows],
            self.sum_ref.at[self.core, chunk, rows],
            self.cross_send.at[lane, step],
            self.cross_recv.at[lane, step],
            self.twin,
        )

    def store_copy(self, lane, step, source):
        chunk, rows = self.spread_parts(lane, step)
        return pltpu.make_async_copy(
            source.at[chunk, rows],
            self.sum_ref.at[self.core, chunk, rows],
            self.store_sem.at[lane, step],
        )

    def turn(self):
        for lane in range(len(self.lanes)):
            self.take(lane, self.chips - 1)
            self.spread_copy(lane, 0, self.held).start()
            self.cross_copy(lane, 0, self.held).start()
            self.store_copy(lane, 0, self.held).start()

    def spread_step(self, step):
        for lane in range(len(self.lanes)):
            self.spread_copy(lane, step - 1, self.final).wait_recv()
            self.spread_copy(lane, step, self.final).start()
            self.cross_copy(lane, step, self.final).start()
            self.store_copy(lane, step, self.final).start()

    def last(self):
        for lane in range(len(self.lanes)):
            self.spread_copy(lane, self.chips - 2, self.final).wait_recv()
            self.cross_copy(lane, self.chips - 1, self.final).start()
            self.store_copy(lane, self.chips - 1, self.final).start()

    def run(self, begin, end):
        chips = self.chips

        def loop(low, high, step_of):
            def one(step, carry):
                step_of(step)
                return carry

            if low < high:
                lax.fori_loop(low, high, one, 0)

        loop(begin + 1, min(end, chips - 2) + 1, self.reduce_step)
        if begin <= chips - 2 < end:
            self.turn()
        loop(max(begin - chips + 2, 1), min(end - chips + 1, chips - 2) + 1, self.spread_step)
        if end == 2 * (chips - 1):
            self.last()

    def settle(self):
        def swaps(rank, carry):
            for which in range(len(self.parts)):
                self.swap(rank, which).wait_send()
            return carry

        def steps(step, carry):
            for lane in range(len(self.lanes)):
                self.ring_copy(lane, step).wait_send()
                self.spread_copy(lane, step, self.final).wait_send()
            return carry

        def outs(step, carry):
            for lane in range(len(self.lanes)):
                self.cross_copy(lane, step, self.final).wait()
                self.store_copy(lane, step, self.final).wait()
            return carry

        lax.fori_loop(0, self.chips, swaps, 0)
        lax.fori_loop(0, self.chips - 1, steps, 0)
        lax.fori_loop(0, self.chips, outs, 0)


def ring_plan(total_rows, columns, devices, count):
    chips = devices // 2
    chunk_rows = total_rows // devices
    tiles = chunk_rows // TILE
    shares = [tiles // 4 + (1 if spot < tiles % 4 else 0) for spot in range(4)]
    lanes = []
    first = 0
    for sign, share in zip((1, -1, 1, -1), shares):
        if share:
            lanes.append((sign, first * TILE, share * TILE))
        first += share
    block = (chips, chunk_rows, columns)
    dma = pltpu.SemaphoreType.DMA
    buffers = [pltpu.VMEM(block, jnp.bfloat16)] * (2 * count + 2)
    sems = [dma((count, chips))] * 3 + [dma((len(lanes), chips))] * 7
    return chips, tuple(lanes), block, buffers, sems


def ring_sum_kernel(chips, lanes, count, *refs):
    parts, vectors = refs[:count], refs[count : 2 * count]
    sum_ref, vector_ref = refs[2 * count : 2 * count + 2]
    refs = refs[2 * count + 2 :]
    buffers, refs = refs[: 2 * count + 2], refs[2 * count + 2 :]
    sems, refs = refs[:10], refs[10:]
    (vector_held, vector_twin, vector_arriving, vector_final, vector_send, vector_recv,
     vector_store) = refs
    places = ring_places(chips)
    place, core, onward, backward, twin = places
    barrier = greet((onward, backward, twin))
    ring = Ring(chips, lanes, places, parts, sum_ref, buffers, sems)
    ring.start_loads()
    pl.semaphore_wait(barrier, 3)
    ring.start_swaps()

    my_rows = pl.ds(pl.multiple_of(core * TILE, TILE), TILE)
    twin_rows = pl.ds(pl.multiple_of((1 - core) * TILE, TILE), TILE)

    def vector_copy(at, source, target, device):
        return ring.remote(source, target, vector_send.at[at], vector_recv.at[at], device)

    vector_swap = vector_copy(0, vector_held.at[twin_rows], vector_twin, twin)
    vector_ring = vector_copy(1, vector_held.at[my_rows], vector_arriving, onward)
    vector_spread = vector_copy(2, vector_final, vector_final, onward)
    vector_cross = vector_copy(3, vector_final, vector_ref.at[my_rows], twin)
    vector_out = pltpu.make_async_copy(vector_final, vector_ref.at[my_rows], vector_store.at[0])
    total = vectors[0][...]
    for item in vectors[1:]:
        total = total + item[...]
    vector_held[...] = total.astype(jnp.bfloat16)
    vector_swap.start()

    def add_vectors(source):
        vector_held[my_rows, :] = (
            vector_held[my_rows, :].astype(jnp.float32) + source[...].astype(jnp.float32)
        ).astype(jnp.bfloat16)

    ring.first()
    vector_swap.wait_recv()
    add_vectors(vector_twin)

    @pl.when(place == 0)
    def _():
        vector_ring.start()

    def reduce_step(step, carry):
        ring.reduce_step(step)

        @pl.when(place == step)
        def _():
            vector_ring.wait_recv()
            add_vectors(vector_arriving)
            vector_ring.start()

        return carry

    lax.fori_loop(1, chips - 1, reduce_step, 0)

    @pl.when(place == chips - 1)
    def _():
        vector_ring.wait_recv()
        add_vectors(vector_arriving)
        vector_final[...] = vector_held[my_rows, :]
        vector_spread.start()
        vector_cross.start()
        vector_out.start()

    ring.turn()

    def spread_vectors(step, last):
        @pl.when((place + 1) % chips == step)
        def _():
            vector_spread.wait_recv()
            if not last:
                vector_spread.start()
            vector_cross.start()
            vector_out.start()

    def spread_step(step, carry):
        ring.spread_step(step)
        spread_vectors(step, False)
        return carry

    lax.fori_loop(1, chips - 1, spread_step, 0)
    ring.last()
    spread_vectors(chips - 1, True)
    ring.settle()
    vector_swap.wait_send()
    vector_cross.wait()
    vector_out.wait()

    @pl.when(place != chips - 1)
    def _():
        vector_ring.wait_send()

    @pl.when(place != chips - 2)
    def _():
        vector_spread.wait_send()


def ring_sum(parts, vectors, devices):
    total_rows, columns = parts[0].shape
    count = len(parts)
    chips, lanes, block, buffers, sems = ring_plan(total_rows, columns, devices, count)
    bf = jnp.bfloat16
    dma = pltpu.SemaphoreType.DMA
    any_spec = pl.BlockSpec(memory_space=pl.ANY)
    vmem_spec = pl.BlockSpec(memory_space=pltpu.VMEM)
    vector_shape = vectors[0].shape
    return pl.pallas_call(
        functools.partial(ring_sum_kernel, chips, lanes, count),
        out_shape=[
            jax.ShapeDtypeStruct((2,) + block, bf),
            jax.ShapeDtypeStruct(vector_shape, bf),
        ],
        in_specs=[any_spec] * count + [vmem_spec] * count,
        out_specs=[any_spec] * 2,
        scratch_shapes=buffers
        + sems
        + [pltpu.VMEM(vector_shape, bf)]
        + [pltpu.VMEM((TILE, columns), bf)] * 3
        + [dma((4,)), dma((4,)), dma((1,))],
        compiler_params=pltpu.CompilerParams(
            collective_id=0, has_side_effects=True, vmem_limit_bytes=VMEM_BYTES
        ),
    )(*[item.reshape((2,) + block) for item in parts], *vectors)


REST_LEFT = (N.normed_ffn, N.normed_mix, N.normed_in)
REST_RIGHT = (N.d_pre, N.d_branch, N.d_proj)
BACK_GROUPS = ((N.dy, N.wd, N.normed_hidden), (N.spread, N.slope, N.wu, N.residual),
               (N.wo, N.attended, N.projected, N.log_total), (N.wq, N.x))
TICKS = 14
BACK_TICKS = 8


def tail_kernel(chips, lanes, slot, buffers, lengths_ref, assign_ref, *refs):
    back_names = sum(BACK_GROUPS, ())
    sources = dict(zip(back_names, refs))
    sources[N.x] = sources[N.x].at[slot]
    refs = refs[len(back_names) :]
    vectors, refs = refs[:4], refs[4:]
    rest_sources, refs = dict(zip(REST_LEFT + REST_RIGHT, refs)), refs[6:]
    part_ref, refs = refs[0], refs[1 + 2 :]
    dx_out, sums_out, rest_out, sum_ref = refs[:4]
    refs = refs[4:]
    held = dict(zip(buffers, refs))
    refs = refs[len(buffers) :]
    stage, turned, back_sem, rest_sem, out_sem = refs[:5]
    ring_buffers, ring_sems = refs[5:9], refs[9:]
    rows, width = held[N.dy].shape
    wide = held[N.wu].shape[1] // width
    held[N.d_down] = held[N.dy]
    held[N.d_pre] = held[N.slope]
    held[N.d_proj] = held[N.projected]
    held[N.d_residual] = held[N.wide_scratch].at[:, 0:width]

    places = ring_places(chips)
    barrier = greet(places[2:])
    ring = Ring(chips, lanes, places, (part_ref,), sum_ref, ring_buffers, ring_sems)
    ring.start_loads()
    on_lower = lax.axis_index("pipe") == 0
    loads = {
        name: pltpu.make_async_copy(sources[name], held[name], back_sem.at[at])
        for at, name in enumerate(back_names)
    }
    rest_loads = {
        name: pltpu.make_async_copy(rest_sources[name], held[name], rest_sem.at[at])
        for at, name in enumerate(REST_LEFT + REST_RIGHT)
    }

    @pl.when(on_lower)
    def _():
        for name in back_names:
            loads[name].start()

    @pl.when(jnp.logical_not(on_lower))
    def _():
        for name in REST_RIGHT:
            rest_loads[name].start()

    for name in REST_LEFT:
        rest_loads[name].start()
    pl.semaphore_wait(barrier, 3)
    ring.start_swaps()
    ring.first()

    steps = 2 * (chips - 1)

    def run_ticks(first, last):
        ring.run(first * steps // TICKS, last * steps // TICKS)

    @pl.when(on_lower)
    def _():
        waited = set()
        done = []

        def ready(name):
            for group in BACK_GROUPS:
                if name in group and name not in waited:
                    waited.update(group)
                    for item in group:
                        loads[item].wait()

        def emit(name):
            if name == N.dx:
                pltpu.make_async_copy(held[N.dx], dx_out, out_sem.at[2]).start()
            if name == N.sums:
                pltpu.make_async_copy(held[N.sums], sums_out, out_sem.at[3]).start()

        def tick():
            run_ticks(len(done), len(done) + 1)
            done.append(0)

        length = slot_length(lengths_ref, assign_ref, slot)
        backward_body(held, vectors, length, False, ready, emit, tick)
        run_ticks(len(done), BACK_TICKS)

    @pl.when(jnp.logical_not(on_lower))
    def _():
        run_ticks(0, BACK_TICKS)
        for name in REST_RIGHT:
            rest_loads[name].wait()

    for name in REST_LEFT:
        rest_loads[name].wait()
    firsts = (4, 3, 0)
    stores = []
    ticks = BACK_TICKS
    for left, right, first in zip(REST_LEFT, REST_RIGHT, firsts):
        turned[...] = held[left][...].T
        for block in range(held[right].shape[1] // width):
            at = len(stores)
            if at >= 2:
                stores[at - 2].wait()
            cols = slice(block * width, (block + 1) * width)
            stage[at % 2] = dot_nn(turned[...], held[right][:, cols]).astype(jnp.bfloat16)
            target = rest_out.at[pl.ds((first + block) * width, width)]
            stores.append(pltpu.make_async_copy(stage.at[at % 2], target, out_sem.at[at % 2]))
            stores[-1].start()
            if at % 2 and ticks < TICKS - 1:
                run_ticks(ticks, ticks + 1)
                ticks += 1
    for item in stores[-2:]:
        item.wait()
    used = (4 + wide) * width
    rest = rest_out.shape[0] - used
    for first in range(used, used + rest, width):
        count = min(width, used + rest - first)
        stage[0, 0:count] = jnp.zeros((count, width), jnp.bfloat16)
        zeros = pltpu.make_async_copy(
            stage.at[0, pl.ds(0, count)], rest_out.at[pl.ds(first, count)], out_sem.at[0]
        )
        zeros.start()
        zeros.wait()
    run_ticks(ticks, TICKS)
    ring.settle()

    @pl.when(on_lower)
    def _():
        pltpu.make_async_copy(held[N.dx], dx_out, out_sem.at[2]).wait()
        pltpu.make_async_copy(held[N.sums], sums_out, out_sem.at[3]).wait()


def tail_call(slot, sizes, given, vectors, kept, grads, part, devices):
    rows, width = given[N.dy].shape
    hidden = given[N.wu].shape[1]
    shapes = buffer_shapes(rows, width, hidden)
    chips, lanes, block, ring_buffers, ring_sems = ring_plan(part.shape[0], width, devices, 1)
    back_names = sum(BACK_GROUPS, ())
    buffers = back_names + REST_LEFT
    buffers += (N.d_branch, N.dx, N.sums, N.wide_scratch, N.d_attended, N.delta, N.bias_back)
    any_spec = pl.BlockSpec(memory_space=pl.ANY)
    vmem_spec = pl.BlockSpec(memory_space=pltpu.VMEM)
    smem_spec = pl.BlockSpec(memory_space=pltpu.SMEM)
    bf = jnp.bfloat16
    args = list(sizes) + [given[name] for name in back_names] + list(vectors)
    args += [kept[name] for name in REST_LEFT] + [grads[name] for name in REST_RIGHT]
    args += [part.reshape((2,) + block), grads[N.dx], grads[N.sums]]
    in_specs = [smem_spec] * 2 + [any_spec] * len(back_names) + [vmem_spec] * 4 + [any_spec] * 9
    out_shape = [
        jax.ShapeDtypeStruct((rows, width), bf),
        jax.ShapeDtypeStruct(*shapes[N.sums]),
        jax.ShapeDtypeStruct((rest_rows(width, hidden, devices), width), bf),
        jax.ShapeDtypeStruct((2,) + block, bf),
    ]
    dma = pltpu.SemaphoreType.DMA
    return pl.pallas_call(
        functools.partial(tail_kernel, chips, lanes, slot, buffers),
        out_shape=out_shape,
        in_specs=in_specs,
        out_specs=[any_spec] * 4,
        input_output_aliases={len(args) - 2: 0, len(args) - 1: 1},
        scratch_shapes=[pltpu.VMEM(*shapes[name]) for name in buffers]
        + [
            pltpu.VMEM((2, width, width), bf),
            pltpu.VMEM((width, rows), bf),
            dma((len(back_names),)),
            dma((6,)),
            dma((4,)),
        ]
        + ring_buffers
        + ring_sems,
        compiler_params=pltpu.CompilerParams(
            collective_id=1, has_side_effects=True, vmem_limit_bytes=VMEM_BYTES
        ),
    )(*args)


def finish_kernel(steps, count, rest_hbm, down_hbm, vectors, *refs):
    moved, refs = refs[: 2 * count], refs[2 * count :]
    outs, refs = refs[:4], refs[4:]
    gains, shifts, hidden_gains, hidden_shifts = refs[:4]
    stacked, refs = refs[4:6], refs[6:]
    narrow, broad, passing, in_sem, out_sem, arrive_sem, leave_sem = refs
    width = rest_hbm.shape[1]
    arrivals, departures = [], []
    for at, source in enumerate(moved):
        target = stacked[at // count].at[at % count]
        arrivals.append(pltpu.make_async_copy(source, passing.at[at], arrive_sem.at[at]))
        departures.append(pltpu.make_async_copy(passing.at[at], target, leave_sem.at[at]))

    def load(step):
        which, first, row, column = steps[step]
        source = (down_hbm if which == 3 else rest_hbm).at[pl.ds(first, width)]
        return pltpu.make_async_copy(source, narrow.at[step % DEPTH], in_sem.at[step % DEPTH])

    def store(step):
        which, first, row, column = steps[step]
        target = outs[which].at[pl.ds(row, width), pl.ds(column, width)]
        return pltpu.make_async_copy(broad.at[step % DEPTH], target, out_sem.at[step % DEPTH])

    for step in range(DEPTH):
        load(step).start()
    for item in arrivals:
        item.start()
    values = vectors[...].astype(jnp.float32)
    gains[...] = values[0:3]
    shifts[...] = values[3:10]
    wide = hidden_gains.shape[1] // width
    for block in range(wide):
        cols = slice(block * width, (block + 1) * width)
        hidden_gains[:, cols] = values[10 + block : 11 + block]
        for row in range(2):
            first = 10 + (row + 1) * wide + block
            hidden_shifts[row : row + 1, cols] = values[first : first + 1]
    for step in range(len(steps)):
        load(step).wait()
        if step >= DEPTH:
            store(step - DEPTH).wait()
        broad[step % DEPTH] = narrow[step % DEPTH].astype(jnp.float32)
        store(step).start()
        if step + DEPTH < len(steps):
            load(step + DEPTH).start()
        if step == DEPTH:
            for arrival, departure in zip(arrivals, departures):
                arrival.wait()
                departure.start()
    for step in range(len(steps) - DEPTH, len(steps)):
        store(step).wait()
    for item in departures:
        item.wait()


def finish(rest, down, vectors, slots_out, slots_grad, hidden):
    width = rest.shape[1]
    wide = hidden // width
    count = len(slots_out)
    steps = [(3, block * width, block * width, 0) for block in range(wide)]
    steps += [(0, block * width, 0, block * width) for block in range(3)]
    steps.append((1, 3 * width, 0, 0))
    steps += [(2, (4 + block) * width, 0, block * width) for block in range(wide)]
    f = jnp.float32
    shapes = [(width, 3 * width), (width, width), (width, hidden), (hidden, width)]
    shapes += [(3, width), (7, width), (1, hidden), (2, hidden)]
    any_spec = pl.BlockSpec(memory_space=pl.ANY)
    vmem_spec = pl.BlockSpec(memory_space=pltpu.VMEM)
    out_shape = [jax.ShapeDtypeStruct(shape, f) for shape in shapes]
    pile = jax.ShapeDtypeStruct((count,) + slots_out[0].shape, slots_out[0].dtype)
    return pl.pallas_call(
        functools.partial(finish_kernel, tuple(steps), count),
        out_shape=out_shape + [pile, pile],
        in_specs=[any_spec, any_spec, vmem_spec] + [any_spec] * (2 * count),
        out_specs=[any_spec] * 4 + [vmem_spec] * 4 + [any_spec] * 2,
        scratch_shapes=[
            pltpu.VMEM((DEPTH, width, width), jnp.bfloat16),
            pltpu.VMEM((DEPTH, width, width), f),
            pltpu.VMEM((2 * count,) + slots_out[0].shape, slots_out[0].dtype),
            pltpu.SemaphoreType.DMA((DEPTH,)),
            pltpu.SemaphoreType.DMA((DEPTH,)),
            pltpu.SemaphoreType.DMA((2 * count,)),
            pltpu.SemaphoreType.DMA((2 * count,)),
        ],
        compiler_params=pltpu.CompilerParams(vmem_limit_bytes=VMEM_BYTES),
    )(rest, down, vectors, *slots_out, *slots_grad)


def passed_along(block, axis, distance):
    devices = range(lax.axis_size(axis))
    route = [(i - distance, i) for i in devices if i - distance in devices]
    return lax.ppermute(block, axis, route)


def shards(
    inputs,
    cotangent,
    lengths,
    assign,
    query_key_value,
    out_weight,
    up_weight,
    down_weight,
    model_gains,
    model_shifts,
    hidden_gains,
    hidden_shifts,
):
    micro_count = inputs.shape[0]
    hidden = up_weight.shape[2]
    slots = range(micro_count)
    weights = {
        N.wq: query_key_value[0],
        N.wo: out_weight[0],
        N.wu: up_weight[0],
        N.wd: down_weight[0],
    }
    vectors = (model_gains, model_shifts, hidden_gains, hidden_shifts)

    sizes = (lengths, assign)

    def run(steps, plane, slot, given, previous, after=()):
        return layer_call(
            steps, plane, slot, sizes, {**weights, **given}, vectors, previous, after
        )

    lower, upper = [], []
    for slot in slots:
        after = [lower[-1][N.spread]] if lower else []
        lower.append(run((N.forward,), 0, slot, {N.x: inputs}, {}, after))
    middle = [passed_along(lower[slot][N.y], "pipe", 1) for slot in slots]
    for slot in slots:
        after = [upper[-1][N.sums]] if upper else []
        given = {N.x: middle[slot], N.dy: cotangent}
        upper.append(run((N.forward, N.backward), 1, slot, given, lower[slot], after))
    returned = [passed_along(upper[slot][N.dx], "pipe", -1) for slot in slots]
    kept = [{**lower[slot], **upper[slot]} for slot in slots]
    devices = lax.axis_size("batch")
    grads, downs, rests = [], [], []
    for slot in slots[:-1]:
        given = {**kept[slot], N.x: inputs, N.dy: returned[slot]}
        grads.append(run((N.backward,), 0, slot, given, kept[slot]))
        down, rest = weight_grads(kept[slot], grads[slot], devices)
        downs.append(down)
        rests.append(rest)
    final = slots[-1]
    down_part = down_grad(
        kept[final][N.normed_hidden], returned[final], upper[final][N.d_down], downs[0]
    )
    given = {**weights, **kept[final], N.x: inputs, N.dy: returned[final]}
    dx, sums, rest, down_sum = tail_call(
        final, sizes, given, vectors, kept[final], upper[final], down_part, devices
    )
    vector_parts = [item[N.sums] for item in grads] + [sums]
    rest_sum, vector_sum = ring_sum(rests + [rest], vector_parts, devices)
    width = dx.shape[1]
    outs = finish(
        rest_sum.reshape(-1, width),
        down_sum.reshape(-1, width),
        vector_sum,
        [kept[slot][N.y] for slot in slots],
        [item[N.dx] for item in grads] + [dx],
        hidden,
    )
    return tuple(item[None] for item in outs[8:] + outs[:6]) + (outs[6], outs[7][None])


def solution(mesh):
    return jax.shard_map(
        shards,
        mesh=mesh,
        in_specs=(
            P(None, "batch", None),
            P(None, "batch", None),
            P("batch"),
            P("batch"),
            P("pipe", None, None),
            P("pipe", None, None),
            P("pipe", None, None),
            P("pipe", None, None),
            P("pipe", None, None),
            P("pipe", None, None),
            P("pipe", None),
            P("pipe", None, None),
        ),
        out_specs=(
            P("pipe", None, "batch", None),
            P("pipe", None, "batch", None),
            P("pipe", None, None),
            P("pipe", None, None),
            P("pipe", None, None),
            P("pipe", None, None),
            P("pipe", None, None),
            P("pipe", None, None),
            P("pipe", None),
            P("pipe", None, None),
        ),
        check_vma=False,
    )
```

```python
import functools
import types

import jax
import jax.numpy as jnp
from jax import lax
from jax.experimental import pallas as pl
from jax.experimental.pallas import tpu as pltpu
from jax.sharding import PartitionSpec as P

HEAD = 64
PAIR = 2 * HEAD
EPSILON = 1e-05
SCALE = 0.125
HIDDEN_NEG = -1e30
CHUNK = 512
SUM_ROWS = 32
DEPTH = 3
HEAD_ROWS = 16

TILE = 16
VMEM_BYTES = 60 * 1024 * 1024
TAIL_VMEM_BYTES = 63 * 1024 * 1024
MESH_IDS = pl.DeviceIdType.MESH


def named(**given):
    return types.SimpleNamespace(**{name: name for name in given})


N = named(
    x=0,
    dy=0,
    y=0,
    dx=0,
    wq=0,
    wo=0,
    wu=0,
    wd=0,
    normed_in=0,
    projected=0,
    log_total=0,
    attended=0,
    normed_mix=0,
    residual=0,
    normed_ffn=0,
    normed_hidden=0,
    slope=0,
    spread=0,
    d_down=0,
    d_pre=0,
    d_branch=0,
    d_proj=0,
    sums=0,
    wide_scratch=0,
    d_residual=0,
    d_attended=0,
    delta=0,
    bias=0,
    bias_back=0,
    forward=0,
    backward=0,
)


def dot_nn(left, right):
    return jnp.dot(left, right, preferred_element_type=jnp.float32)


def dot_nt(left, right):
    return lax.dot_general(
        left, right, (((1,), (1,)), ((), ())), preferred_element_type=jnp.float32
    )


def standardize(values_in):
    centred = values_in - jnp.mean(values_in, axis=-1, keepdims=True)
    scale = lax.rsqrt(jnp.mean(centred * centred, axis=-1, keepdims=True) + EPSILON)
    return centred * scale, scale


def unit_backward(grad, unit, scale, gain):
    scaled = grad * gain
    first = jnp.mean(scaled, axis=-1, keepdims=True)
    second = jnp.mean(scaled * unit, axis=-1, keepdims=True)
    return (
        scale * (scaled - first - unit * second),
        jnp.sum(grad * unit, axis=0, keepdims=True),
        jnp.sum(grad, axis=0, keepdims=True),
    )


def column_sum(values):
    return jnp.sum(values.astype(jnp.float32), axis=0, keepdims=True)


def hiding_bias(rows, length, query_dim):
    query = lax.broadcasted_iota(jnp.int32, (rows, rows), query_dim)
    key = lax.broadcasted_iota(jnp.int32, (rows, rows), 1 - query_dim)
    visible = (key <= query) & ((key < length) | (key == query))
    return jnp.where(visible, 0.0, HIDDEN_NEG)


def own_lanes(values, which):
    lane = lax.broadcasted_iota(jnp.int32, values.shape, 1)
    mine = (lane >= HEAD) if which else (lane < HEAD)
    return jnp.where(mine, values, jnp.zeros_like(values))


def attend_forward(projected, attended, log_total, bias):
    rows, width = attended.shape
    half = rows // 2
    lane = lax.broadcasted_iota(jnp.int32, (half, PAIR), 1)

    def one_pair(pair, totals):
        first = pl.multiple_of(pair * PAIR, PAIR)
        items = []
        for block in range(2):
            at = slice(block * half, (block + 1) * half)
            reach = (block + 1) * half
            q = projected[at, pl.ds(first, PAIR)] * jnp.bfloat16(SCALE)
            k = projected[0:reach, pl.ds(width + first, PAIR)]
            v = projected[0:reach, pl.ds(2 * width + first, PAIR)]
            items += [(at, reach, own_lanes(q, which), k, v) for which in range(2)]
        scores = [dot_nt(q, k) + bias[at, 0:reach] for at, reach, q, k, v in items]
        softened = []
        for item in scores:
            top = jnp.max(item, axis=-1, keepdims=True)
            exps = jnp.exp(item - top)
            softened.append((exps, jnp.sum(exps, axis=-1, keepdims=True), top))
        mixed = [
            dot_nn(exps.astype(jnp.bfloat16), item[4]) * (1.0 / total)
            for item, (exps, total, top) in zip(items, softened)
        ]
        new_totals = []
        for block in range(2):
            at = items[2 * block][0]
            attended[at, pl.ds(first, PAIR)] = jnp.where(
                lane < HEAD, mixed[2 * block], mixed[2 * block + 1]
            )
            logs = totals[block]
            for which in range(2):
                exps, total, top = softened[2 * block + which]
                logs = jnp.where(lane == 2 * pair + which, top + jnp.log(total), logs)
            new_totals.append(logs)
        return tuple(new_totals)

    zero = jnp.zeros((half, PAIR), jnp.float32)
    totals = lax.fori_loop(0, width // PAIR, one_pair, (zero, zero), unroll=2)
    for block in range(2):
        log_total[:, block * half : (block + 1) * half] = totals[block].T[0:HEAD_ROWS]


def attend_backward(projected, d_attended, log_total, delta, bias, d_proj, tick):
    rows, width = d_attended.shape
    half = rows // 2

    def one_pair(pair, carry):
        first = pl.multiple_of(pair * PAIR, PAIR)
        k_all = projected[:, pl.ds(width + first, PAIR)]
        v_all = projected[:, pl.ds(2 * width + first, PAIR)]
        k_turned = k_all.T
        items = []
        for block in range(2):
            at = slice(block * half, (block + 1) * half)
            q = projected[at, pl.ds(first, PAIR)] * jnp.bfloat16(SCALE)
            grad = d_attended[at, pl.ds(first, PAIR)]
            for which in range(2):
                items.append((block, which, at, own_lanes(q, which), own_lanes(grad, which)))
        raw = []
        for block, which, at, q, grad in items:
            reach = (block + 1) * half
            raw.append((dot_nt(k_all[0:reach], q), dot_nt(v_all[0:reach], grad)))
        shaped = []
        for (block, which, at, q, grad), (scores, d_probs) in zip(items, raw):
            reach = (block + 1) * half
            head = pl.ds(2 * pair + which, 1)
            probs = jnp.exp(scores + bias[0:reach, at] - log_total[head, at])
            d_scores = (probs * (d_probs - delta[head, at])).astype(jnp.bfloat16)
            shaped.append((probs.astype(jnp.bfloat16), d_scores))
        dk = [None, None]
        dv = [None, None]
        dq = []
        for (block, which, at, q, grad), (probs, d_scores) in zip(items, shaped):
            reach = (block + 1) * half
            more_v = dot_nn(probs, grad)
            more_k = dot_nn(d_scores, q)
            dq.append(dot_nn(k_turned[which * HEAD : (which + 1) * HEAD, 0:reach], d_scores))
            for part in range(block + 1):
                piece = slice(part * half, (part + 1) * half)
                dv[part] = more_v[piece] if dv[part] is None else dv[part] + more_v[piece]
                dk[part] = more_k[piece] if dk[part] is None else dk[part] + more_k[piece]
        for block in range(2):
            at = slice(block * half, (block + 1) * half)
            turned = jnp.concatenate(dq[2 * block : 2 * block + 2], axis=0) * SCALE
            d_proj[at, pl.ds(first, PAIR)] = turned.T.astype(jnp.bfloat16)
            d_proj[at, pl.ds(width + first, PAIR)] = dk[block].astype(jnp.bfloat16)
            d_proj[at, pl.ds(2 * width + first, PAIR)] = dv[block].astype(jnp.bfloat16)
        return carry

    if tick is None:
        lax.fori_loop(0, width // PAIR, one_pair, 0, unroll=2)
    else:
        for first in range(0, width // PAIR, 2):
            lax.fori_loop(first, min(first + 2, width // PAIR), one_pair, 0, unroll=True)
            tick()


KEPT = (N.normed_in, N.projected, N.log_total, N.attended, N.normed_mix, N.residual,
        N.normed_ffn, N.normed_hidden, N.slope, N.spread)
GRADS = (N.d_down, N.d_pre, N.d_branch, N.d_proj, N.sums)


def buffer_shapes(rows, width, hidden):
    bf, f = jnp.bfloat16, jnp.float32
    return {
        N.x: ((rows, width), bf),
        N.dy: ((rows, width), bf),
        N.y: ((rows, width), bf),
        N.dx: ((rows, width), bf),
        N.wq: ((width, 3 * width), bf),
        N.wo: ((width, width), bf),
        N.wu: ((width, hidden), bf),
        N.wd: ((hidden, width), bf),
        N.normed_in: ((rows, width), bf),
        N.projected: ((rows, 3 * width), bf),
        N.log_total: ((HEAD_ROWS, rows), f),
        N.attended: ((rows, width), f),
        N.normed_mix: ((rows, width), bf),
        N.residual: ((rows, width), f),
        N.normed_ffn: ((rows, width), bf),
        N.normed_hidden: ((rows, hidden), bf),
        N.slope: ((rows, hidden), bf),
        N.spread: ((rows, PAIR), f),
        N.d_down: ((rows, width), bf),
        N.d_pre: ((rows, hidden), bf),
        N.d_branch: ((rows, width), bf),
        N.d_proj: ((rows, 3 * width), bf),
        N.sums: ((SUM_ROWS, width), f),
        N.wide_scratch: ((rows, hidden), f),
        N.d_residual: ((rows, width), f),
        N.d_attended: ((rows, width), bf),
        N.delta: ((HEAD_ROWS, rows), f),
        N.bias: ((rows, rows), f),
        N.bias_back: ((rows, rows), f),
    }


def forward_body(held, vectors, length, ready, emit):
    gm, sm, gh, sh = vectors
    sh = sh.at[0]
    bf = jnp.bfloat16
    rows, width = held[N.x].shape
    hidden = held[N.wu].shape[1]
    wide_scratch = held[N.wide_scratch]
    held[N.bias][...] = hiding_bias(rows, length, 0)
    ready(N.x)
    unit, unused = standardize(held[N.x][...].astype(jnp.float32))
    held[N.normed_in][...] = (unit * gm[0] + sm[0]).astype(bf)
    emit(N.normed_in)
    for block in range(3):
        cols = slice(block * width, (block + 1) * width)
        ready(N.wq)
        out = dot_nn(held[N.normed_in][...], held[N.wq][:, cols])
        if block != 1:
            out = out + sm[1 + block // 2]
        held[N.projected][:, cols] = out.astype(bf)
    emit(N.projected)
    attend_forward(held[N.projected], held[N.attended], held[N.log_total], held[N.bias])
    emit(N.log_total)
    emit(N.attended)

    unit, unused = standardize(held[N.attended][...])
    held[N.normed_mix][...] = (unit * gm[1] + sm[3]).astype(bf)
    emit(N.normed_mix)
    ready(N.wo)
    residual = held[N.x][...].astype(jnp.float32) + sm[4]
    residual = residual + dot_nn(held[N.normed_mix][...], held[N.wo][...])
    held[N.residual][...] = residual
    emit(N.residual)
    unit, unused = standardize(residual)
    held[N.normed_ffn][...] = (unit * gm[2] + sm[5]).astype(bf)
    emit(N.normed_ffn)
    ready(N.wu)
    total = jnp.zeros((rows, 1), jnp.float32)
    for first in range(0, hidden, CHUNK):
        cols = slice(first, first + CHUNK)
        pre = dot_nn(held[N.normed_ffn][...], held[N.wu][:, cols]) + sh[0:1, cols]
        share = 0.5 + 0.5 * lax.erf(pre * 0.7071067811865476)
        density = 0.3989422804014327 * jnp.exp(-0.5 * pre * pre)
        act = pre * share
        held[N.slope][:, cols] = (share + pre * density).astype(bf)
        wide_scratch[:, cols] = act
        total = total + jnp.sum(act, axis=-1, keepdims=True)
    emit(N.slope)
    mean = total * (1.0 / hidden)
    square = jnp.zeros((rows, 1), jnp.float32)
    for first in range(0, hidden, CHUNK):
        centred = wide_scratch[:, first : first + CHUNK] - mean
        square = square + jnp.sum(centred * centred, axis=-1, keepdims=True)
    scale = lax.rsqrt(square * (1.0 / hidden) + EPSILON)
    held[N.spread][...] = jnp.broadcast_to(scale, (rows, PAIR))
    emit(N.spread)
    for first in range(0, hidden, CHUNK):
        cols = slice(first, first + CHUNK)
        unit = (wide_scratch[:, cols] - mean) * scale
        held[N.normed_hidden][:, cols] = (unit * gh[0:1, cols] + sh[1:2, cols]).astype(bf)
    emit(N.normed_hidden)
    ready(N.wd)
    out = held[N.residual][...] + dot_nn(held[N.normed_hidden][...], held[N.wd][...])
    held[N.y][...] = (out + sm[6]).astype(bf)
    emit(N.y)


def pool_block(pool, block, width):
    each = width // pool.shape[1]
    return pool[block * each : (block + 1) * each].reshape(width, width)


def backward_body(held, vectors, length, masked, ready, emit, tick=None, pools=None, middle=None):
    gm, sm, gh, sh = vectors
    sh = sh.at[0]
    bf = jnp.bfloat16
    rows, width = held[N.x].shape
    hidden = held[N.wide_scratch].shape[1]
    wide = hidden // width
    wide_scratch, sums = held[N.wide_scratch], held[N.sums]
    sums[...] = jnp.zeros_like(sums)
    if pools is None:
        held[N.bias_back][...] = hiding_bias(rows, length, 1)
    ready(N.dy)
    d_down = held[N.dy][...]
    if masked:
        live = lax.broadcasted_iota(jnp.int32, (rows, 1), 0) < length
        d_down = jnp.where(live, d_down.astype(jnp.float32), 0.0).astype(bf)
    if tick is None:
        held[N.d_down][...] = d_down
    emit(N.d_down)
    sums[9:10, :] = column_sum(d_down)

    first_total = jnp.zeros((rows, 1), jnp.float32)
    second_total = jnp.zeros((rows, 1), jnp.float32)
    for block in range(wide):
        cols = slice(block * width, (block + 1) * width)
        ready(N.wd)
        ready(N.normed_hidden)
        weight = held[N.wd][cols, :] if pools is None else pool_block(pools[0], block, width)
        grad = dot_nt(held[N.d_down][...], weight)
        normed = held[N.normed_hidden][:, cols].astype(jnp.float32)
        unit = (normed - sh[1:2, cols]) * (1.0 / gh[0:1, cols])
        sums[10 + block : 11 + block, :] = jnp.sum(grad * unit, axis=0, keepdims=True)
        sums[18 + block : 19 + block, :] = jnp.sum(grad, axis=0, keepdims=True)
        scaled = grad * gh[0:1, cols]
        wide_scratch[:, cols] = scaled
        first_total = first_total + jnp.sum(scaled, axis=-1, keepdims=True)
        second_total = second_total + jnp.sum(scaled * unit, axis=-1, keepdims=True)
        if tick is not None and block == wide // 2 - 1:
            tick()
    first_mean = first_total * (1.0 / hidden)
    second_mean = second_total * (1.0 / hidden)
    ready(N.spread)
    ready(N.slope)
    scale = held[N.spread][:, 0:1]
    for block in range(wide):
        cols = slice(block * width, (block + 1) * width)
        normed = held[N.normed_hidden][:, cols].astype(jnp.float32)
        unit = (normed - sh[1:2, cols]) * (1.0 / gh[0:1, cols])
        d_act = scale * (wide_scratch[:, cols] - first_mean - unit * second_mean)
        d_pre = (d_act * held[N.slope][:, cols].astype(jnp.float32)).astype(bf)
        held[N.d_pre][:, cols] = d_pre
        sums[14 + block : 15 + block, :] = column_sum(d_pre)
    emit(N.d_pre)
    if middle is not None:
        middle()

    ready(N.wu)
    if pools is None:
        d_ffn = dot_nt(held[N.d_pre][...], held[N.wu][...])
    else:
        d_ffn = jnp.zeros((rows, width), jnp.float32)
        for block in range(wide):
            cols = slice(block * width, (block + 1) * width)
            d_ffn = d_ffn + dot_nt(held[N.d_pre][:, cols], pool_block(pools[1], block, width))
    ready(N.residual)
    unit, scale = standardize(held[N.residual][...])
    through, gain_sum, shift_sum = unit_backward(d_ffn, unit, scale, gm[2])
    sums[2:3, :] = gain_sum
    sums[8:9, :] = shift_sum
    through = through + held[N.d_down][...].astype(jnp.float32)
    held[N.d_residual][...] = through
    held[N.d_branch][...] = through.astype(bf)
    emit(N.d_branch)
    sums[7:8, :] = column_sum(held[N.d_branch][...])
    if tick is not None:
        tick()

    ready(N.wo)
    d_mix = dot_nt(held[N.d_branch][...], held[N.wo][...])
    ready(N.attended)
    attended = held[N.attended][...]
    unit, scale = standardize(attended)
    through, gain_sum, shift_sum = unit_backward(d_mix, unit, scale, gm[1])
    sums[1:2, :] = gain_sum
    sums[6:7, :] = shift_sum
    held[N.d_attended][...] = through.astype(bf)
    product = held[N.d_attended][...].astype(jnp.float32) * attended
    upper = product.astype(bf)
    lower = (product - upper.astype(jnp.float32)).astype(bf)
    head_row = lax.broadcasted_iota(jnp.int32, (HEAD_ROWS, width), 0)
    head_col = lax.broadcasted_iota(jnp.int32, (HEAD_ROWS, width), 1) // HEAD
    chooser = jnp.where(head_row == head_col, 1.0, 0.0).astype(bf)
    held[N.delta][...] = dot_nt(chooser, upper) + dot_nt(chooser, lower)
    if tick is not None:
        tick()

    ready(N.projected)
    ready(N.log_total)
    if pools is not None:
        held[N.bias_back][...] = hiding_bias(rows, length, 1)
    attend_backward(
        held[N.projected], held[N.d_attended], held[N.log_total], held[N.delta],
        held[N.bias_back], held[N.d_proj], tick,
    )
    emit(N.d_proj)
    ready(N.wq)
    d_norm = dot_nt(held[N.d_proj][...], held[N.wq][...])
    sums[4:5, :] = column_sum(held[N.d_proj][:, 0:width])
    sums[5:6, :] = column_sum(held[N.d_proj][:, 2 * width :])
    ready(N.x)
    unit, scale = standardize(held[N.x][...].astype(jnp.float32))
    through, gain_sum, shift_sum = unit_backward(d_norm, unit, scale, gm[0])
    sums[0:1, :] = gain_sum
    sums[3:4, :] = shift_sum
    held[N.dx][...] = (through + held[N.d_residual][...]).astype(bf)
    emit(N.dx)
    emit(N.sums)


def slot_length(lengths_ref, assign_ref, slot):
    total = jnp.int32(0)
    for at in range(lengths_ref.shape[0]):
        total = total + jnp.where(assign_ref[at] == slot, lengths_ref[at], 0)
    return total


def layer_kernel(
    steps, plane, slot, groups, stacked, out_names, unread, buffers, lengths_ref, assign_ref, *refs
):
    in_names = sum(groups, ())
    sources = dict(zip(in_names, refs))
    for name in stacked:
        sources[name] = sources[name].at[slot]
    vectors = refs[len(in_names) : len(in_names) + 4]
    refs = refs[len(in_names) + 4 + unread :]
    targets = dict(zip(out_names, refs))
    refs = refs[len(out_names) :]
    held = dict(zip(buffers, refs))
    in_sem, out_sem = refs[len(buffers) :]

    @pl.when(lax.axis_index("pipe") == plane)
    def _():
        loads = {
            name: pltpu.make_async_copy(sources[name], held[name], in_sem.at[at])
            for at, name in enumerate(in_names)
        }
        stores = {
            name: pltpu.make_async_copy(held[name], targets[name], out_sem.at[at])
            for at, name in enumerate(out_names)
        }
        for name in in_names:
            loads[name].start()
        waited = set()

        def ready(name):
            for group in groups:
                if name in group and name not in waited:
                    waited.update(group)
                    for item in group:
                        loads[item].wait()

        def emit(name):
            if name in stores:
                stores[name].start()

        length = slot_length(lengths_ref, assign_ref, slot)
        if N.forward in steps:
            forward_body(held, vectors, length, ready, emit)
        if N.backward in steps:
            backward_body(held, vectors, length, N.forward in steps, ready, emit)
        for name in out_names:
            stores[name].wait()


FORWARD_ONLY = (N.projected, N.log_total, N.attended, N.residual, N.slope, N.spread)


def layer_call(steps, plane, slot, sizes, given, vectors, previous, after=()):
    stacked = tuple(name for name in (N.x, N.dy) if name in given and given[name].ndim == 3)
    rows, width = given[N.x].shape[-2:]
    hidden = given[N.wu].shape[1]
    shapes = buffer_shapes(rows, width, hidden)
    if steps == (N.forward,):
        groups = ((N.x, N.wq), (N.wo, N.wu, N.wd))
        out_names = (N.y,) + KEPT
        spare = (N.wide_scratch, N.bias)
    elif steps == (N.backward,):
        groups = ((N.dy, N.wd, N.normed_hidden), (N.spread, N.slope, N.wu, N.residual),
                  (N.wo, N.attended, N.projected, N.log_total), (N.wq, N.x))
        out_names = (N.dx,) + GRADS
        spare = (N.wide_scratch, N.bias_back, N.d_residual, N.d_attended, N.delta)
    else:
        groups = ((N.x, N.wq), (N.wo, N.wu), (N.wd, N.dy))
        out_names = (N.y,) + tuple(name for name in KEPT if name not in FORWARD_ONLY)
        out_names += (N.dx,) + GRADS
        spare = (N.wide_scratch, N.bias, N.bias_back, N.d_residual, N.d_attended, N.delta)
        spare += FORWARD_ONLY
    in_names = sum(groups, ())
    buffers = in_names + tuple(name for name in out_names if name not in in_names) + spare
    any_spec = pl.BlockSpec(memory_space=pl.ANY)
    vmem_spec = pl.BlockSpec(memory_space=pltpu.VMEM)
    smem_spec = pl.BlockSpec(memory_space=pltpu.SMEM)
    in_specs = [smem_spec] * 2 + [any_spec] * len(in_names) + [vmem_spec] * 4
    args = list(sizes) + [given[name] for name in in_names] + list(vectors)
    shared = [name for name in out_names if name in previous]
    aliases = {len(args) + at: out_names.index(name) for at, name in enumerate(shared)}
    in_specs += [any_spec] * len(shared)
    args += [previous[name] for name in shared]
    in_specs += [any_spec] * len(after)
    args += list(after)
    scratch = [pltpu.VMEM(*shapes[name]) for name in buffers]
    scratch.append(pltpu.SemaphoreType.DMA((len(in_names),)))
    scratch.append(pltpu.SemaphoreType.DMA((len(out_names),)))
    outs = pl.pallas_call(
        functools.partial(
            layer_kernel, steps, plane, slot, groups, stacked, out_names, len(shared + list(after)), buffers
        ),
        out_shape=[jax.ShapeDtypeStruct(*shapes[name]) for name in out_names],
        in_specs=in_specs,
        out_specs=[any_spec] * len(out_names),
        input_output_aliases=aliases,
        scratch_shapes=scratch,
        compiler_params=pltpu.CompilerParams(vmem_limit_bytes=VMEM_BYTES),
        cost_estimate=pl.CostEstimate(
            flops=len(steps) * 2 * rows * width * (4 * width + 2 * hidden),
            bytes_accessed=40_000_000,
            transcendentals=0,
        ),
    )(*args)
    return dict(zip(out_names, outs))


LEFT = (N.normed_hidden, N.normed_ffn, N.normed_mix, N.normed_in)
RIGHT = (N.d_down, N.d_pre, N.d_branch, N.d_proj)


def chunk_rows(width, hidden, devices):
    chips = devices // 2
    return -(-(hidden // 2) // (chips * TILE)) * TILE


def block_row(block, width, hidden, half_rows):
    each = hidden // width // 2
    return (block // each) * half_rows + (block % each) * width


def weight_grad_kernel(*refs):
    parts = len(LEFT)
    sources, refs = refs[: 2 * parts], refs[2 * parts :]
    targets, scratch = refs[:2], refs[2:]
    left, right = scratch[0:parts], scratch[parts : 2 * parts]
    out_s = scratch[2 * parts : 2 * parts + 2]
    turned, in_sem, out_sem = scratch[2 * parts + 2 :]
    width = left[3].shape[1]
    wide = left[0].shape[1] // width
    loads = [
        pltpu.make_async_copy(source, target, in_sem.at[at])
        for at, (source, target) in enumerate(zip(sources, left + right))
    ]
    for part in range(parts):
        loads[part].start()
        loads[parts + part].start()
    starts = (0, 4, 3, 0)
    stores = []

    def store(which, first, count):
        at = pl.ds(first, count)
        stores.append(
            pltpu.make_async_copy(
                out_s[which].at[at], targets[which].at[at], out_sem.at[len(stores)]
            )
        )
        stores[-1].start()

    for part in range(parts):
        loads[part].wait()
        loads[parts + part].wait()
        first = starts[part] * width
        if part == 0:

            def one(block, carry):
                at = pl.ds(pl.multiple_of(block * width, width), width)
                turned[...] = left[part][:, at].T
                out_s[0][at, :] = dot_nn(turned[...], right[part][...]).astype(jnp.bfloat16)
                return carry

            lax.fori_loop(0, wide, one, 0)
            store(0, 0, out_s[0].shape[0])
        else:
            turned[...] = left[part][...].T
            blocks = right[part].shape[1] // width

            def one(block, carry):
                cols = pl.ds(pl.multiple_of(block * width, width), width)
                at = pl.ds(pl.multiple_of(first + block * width, width), width)
                out_s[1][at, :] = dot_nn(turned[...], right[part][:, cols]).astype(jnp.bfloat16)
                return carry

            lax.fori_loop(0, blocks, one, 0)
            store(1, first, blocks * width)
    for item in stores:
        item.wait()


def weight_grads(kept, grads):
    args = [kept[name] for name in LEFT] + [grads[name] for name in RIGHT]
    rows, width = kept[N.normed_in].shape
    hidden = kept[N.normed_hidden].shape[1]
    bf = jnp.bfloat16
    shapes = [(hidden, width), (4 * width + hidden, width)]
    any_spec = pl.BlockSpec(memory_space=pl.ANY)
    scratch = [pltpu.VMEM(item.shape, bf) for item in args]
    scratch += [pltpu.VMEM(shape, bf) for shape in shapes]
    scratch += [
        pltpu.VMEM((width, rows), bf),
        pltpu.SemaphoreType.DMA((len(args),)),
        pltpu.SemaphoreType.DMA((5,)),
    ]
    return pl.pallas_call(
        weight_grad_kernel,
        out_shape=[jax.ShapeDtypeStruct(shape, bf) for shape in shapes],
        in_specs=[any_spec] * len(args),
        out_specs=[any_spec] * 2,
        scratch_shapes=scratch,
        compiler_params=pltpu.CompilerParams(vmem_limit_bytes=VMEM_BYTES),
        cost_estimate=pl.CostEstimate(
            flops=2 * rows * width * (4 * width + 2 * hidden),
            bytes_accessed=30_000_000,
            transcendentals=0,
        ),
    )(*args)


def down_grad_kernel(
    hidden_hbm, lower_hbm, upper_hbm, base_hbm, out_hbm, hidden_s, grad_s, base_s, out_s, in_sem,
    out_sem
):
    width = grad_s.shape[1]
    wide = hidden_s.shape[1] // width

    @pl.when(lax.axis_index("pipe") == 0)
    def _():
        pltpu.make_async_copy(lower_hbm, grad_s, in_sem.at[0]).start()

    @pl.when(lax.axis_index("pipe") != 0)
    def _():
        pltpu.make_async_copy(upper_hbm, grad_s, in_sem.at[0]).start()

    blocks = [pl.ds(block * width, width) for block in range(wide)]
    lefts = [
        pltpu.make_async_copy(hidden_hbm.at[:, at], hidden_s.at[:, at], in_sem.at[1 + block])
        for block, at in enumerate(blocks)
    ]
    base = pltpu.make_async_copy(base_hbm, base_s, in_sem.at[1 + wide])
    for item in lefts:
        item.start()
    base.start()
    pltpu.make_async_copy(lower_hbm, grad_s, in_sem.at[0]).wait()
    stores = []

    def store(first, count):
        at = pl.ds(first, count)
        stores.append(pltpu.make_async_copy(out_s.at[at], out_hbm.at[at], out_sem.at[len(stores)]))
        stores[-1].start()

    half_rows = out_s.shape[0] // 2
    used = wide // 2 * width
    if half_rows > used:
        for half in range(2):
            first = half * half_rows + used
            out_s[first : (half + 1) * half_rows, :] = jnp.zeros(
                (half_rows - used, width), jnp.bfloat16
            )
            store(first, half_rows - used)
    for block, at in enumerate(blocks):
        lefts[block].wait()
        if block == 0:
            base.wait()
        product = dot_nn(hidden_s[:, at].T, grad_s[...])
        first = block_row(block, width, wide * width, half_rows)
        out_s[first : first + width, :] = (
            product + base_s[at, :].astype(jnp.float32)
        ).astype(jnp.bfloat16)
        store(first, width)
    for item in stores:
        item.wait()


def down_grad(normed_hidden, lower_grad, upper_grad, base, half_rows):
    bf = jnp.bfloat16
    wide = normed_hidden.shape[1] // lower_grad.shape[1]
    out_shape = (2 * half_rows, lower_grad.shape[1])
    any_spec = pl.BlockSpec(memory_space=pl.ANY)
    return pl.pallas_call(
        down_grad_kernel,
        out_shape=jax.ShapeDtypeStruct(out_shape, bf),
        in_specs=[any_spec] * 4,
        out_specs=any_spec,
        scratch_shapes=[
            pltpu.VMEM(normed_hidden.shape, bf),
            pltpu.VMEM(lower_grad.shape, bf),
            pltpu.VMEM(base.shape, bf),
            pltpu.VMEM(out_shape, bf),
            pltpu.SemaphoreType.DMA((wide + 2,)),
            pltpu.SemaphoreType.DMA((wide + 2,)),
        ],
        compiler_params=pltpu.CompilerParams(vmem_limit_bytes=VMEM_BYTES),
        cost_estimate=pl.CostEstimate(
            flops=2 * normed_hidden.size * lower_grad.shape[1],
            bytes_accessed=14_000_000,
            transcendentals=0,
        ),
    )(normed_hidden, lower_grad, upper_grad, base)


def ring_places(chips):
    line_len = chips // 2
    pipe = lax.axis_index("pipe")
    batch = lax.axis_index("batch")
    core = batch % 2
    side = (batch // 2) % 2
    line = batch // 4
    place = line * (1 - side) + (chips - 1 - line) * side

    def chip_at(spot):
        far = spot // line_len
        along = spot * (1 - far) + (chips - 1 - spot) * far
        return (pipe, (along * 2 + far) * 2 + core)

    onward = chip_at((place + 1) % chips)
    backward = chip_at((place + chips - 1) % chips)
    twin = (pipe, batch + 1 - 2 * core)
    return place, core, onward, backward, twin


def greet(devices):
    barrier = pltpu.get_barrier_semaphore()
    for other in devices:
        pl.semaphore_signal(barrier, inc=1, device_id=other, device_id_type=MESH_IDS)
    return barrier


class Ring:
    def __init__(self, chips, lanes, places, parts, sum_ref, buffers, sems):
        self.chips, self.lanes, self.parts, self.sum_ref = chips, lanes, parts, sum_ref
        self.place, self.core, self.onward, self.backward, self.twin = places
        count = max(len(parts), 1)
        self.own, self.from_core = buffers[:count], buffers[count : 2 * count]
        self.arriving, self.final = buffers[2 * count :]
        self.held = self.own[0]
        (self.load_sem, self.core_send, self.core_recv, self.ring_send, self.ring_recv,
         self.spread_send, self.spread_recv, self.cross_send, self.cross_recv,
         self.store_sem) = sems

    def chunk_of(self, rank):
        half_up = (rank + 1) // 2
        sign = 1 - 2 * (rank % 2)
        return (self.place + self.chips + sign * half_up) % self.chips

    def load(self, rank, which):
        chunk = self.chunk_of(rank)
        return pltpu.make_async_copy(
            self.parts[which].at[self.core, chunk],
            self.own[which].at[chunk],
            self.load_sem.at[which, rank],
        )

    def remote(self, source, target, send_sem, recv_sem, device):
        return pltpu.make_async_remote_copy(
            src_ref=source,
            dst_ref=target,
            send_sem=send_sem,
            recv_sem=recv_sem,
            device_id=device,
            device_id_type=MESH_IDS,
        )

    def swap(self, rank, which):
        chunk = self.chunk_of(rank)
        return self.remote(
            self.parts[which].at[1 - self.core, chunk],
            self.from_core[which].at[chunk],
            self.core_send.at[which, rank],
            self.core_recv.at[which, rank],
            self.twin,
        )

    def start_loads(self):
        for rank in range(self.chips):
            for which in range(len(self.parts)):
                self.load(rank, which).start()

    def start_swaps(self):
        for rank in range(self.chips):
            for which in range(len(self.parts)):
                self.swap(rank, which).start()

    def add_rows(self, chunk, first, count, sources):
        def one(index, carry):
            rows = pl.ds(pl.multiple_of(first + index * TILE, TILE), TILE)
            total = self.held[chunk, rows, :].astype(jnp.float32)
            for source in sources:
                total = total + source[rows, :].astype(jnp.float32)
            self.held[chunk, rows, :] = total.astype(jnp.bfloat16)
            return carry

        lax.fori_loop(0, count // TILE, one, 0)

    def prepare(self, rank):
        chunk = self.chunk_of(rank)
        for which in range(len(self.parts)):
            self.load(rank, which).wait()
            self.swap(rank, which).wait_recv()
        sources = [item.at[chunk] for item in self.own[1:] + self.from_core]
        self.add_rows(chunk, 0, self.held.shape[1], sources)

    def neighbour(self, lane):
        return self.onward if self.lanes[lane][0] > 0 else self.backward

    def ring_chunk(self, lane, step):
        return (self.place + (self.chips - 1) * self.chips - self.lanes[lane][0] * step) % self.chips

    def ring_copy(self, lane, step):
        sign, first, count = self.lanes[lane]
        rows = pl.ds(first, count)
        return self.remote(
            self.held.at[self.ring_chunk(lane, step), rows],
            self.arriving.at[step, rows],
            self.ring_send.at[lane, step],
            self.ring_recv.at[lane, step],
            self.neighbour(lane),
        )

    def take(self, lane, step):
        sign, first, count = self.lanes[lane]
        self.ring_copy(lane, step - 1).wait_recv()
        chunk = self.ring_chunk(lane, step)
        self.add_rows(chunk, first, count, [self.arriving.at[step - 1]])

    def first(self):
        self.prepare(0)
        for lane in range(len(self.lanes)):
            self.ring_copy(lane, 0).start()

    def reduce_step(self, step):
        for rank in (2 * step - 1, 2 * step):

            @pl.when(rank < self.chips)
            def _():
                self.prepare(rank)

        for lane in range(len(self.lanes)):
            self.take(lane, step)
            self.ring_copy(lane, step).start()

    def spread_parts(self, lane, step):
        sign, first, count = self.lanes[lane]
        chunk = (self.place + (self.chips + 1) * self.chips + sign * (1 - step)) % self.chips
        return chunk, pl.ds(first, count)

    def spread_copy(self, lane, step, source):
        chunk, rows = self.spread_parts(lane, step)
        return self.remote(
            source.at[chunk, rows],
            self.final.at[chunk, rows],
            self.spread_send.at[lane, step],
            self.spread_recv.at[lane, step],
            self.neighbour(lane),
        )

    def cross_copy(self, lane, step, source):
        chunk, rows = self.spread_parts(lane, step)
        return self.remote(
            source.at[chunk, rows],
            self.sum_ref.at[self.core, chunk, rows],
            self.cross_send.at[lane, step],
            self.cross_recv.at[lane, step],
            self.twin,
        )

    def store_copy(self, lane, step, source):
        chunk, rows = self.spread_parts(lane, step)
        return pltpu.make_async_copy(
            source.at[chunk, rows],
            self.sum_ref.at[self.core, chunk, rows],
            self.store_sem.at[lane, step],
        )

    def turn(self):
        for lane in range(len(self.lanes)):
            self.take(lane, self.chips - 1)
            self.spread_copy(lane, 0, self.held).start()
            self.cross_copy(lane, 0, self.held).start()
            self.store_copy(lane, 0, self.held).start()

    def spread_step(self, step):
        for lane in range(len(self.lanes)):
            self.spread_copy(lane, step - 1, self.final).wait_recv()
            self.spread_copy(lane, step, self.final).start()
            self.cross_copy(lane, step, self.final).start()
            self.store_copy(lane, step, self.final).start()

    def last(self):
        for lane in range(len(self.lanes)):
            self.spread_copy(lane, self.chips - 2, self.final).wait_recv()
            self.cross_copy(lane, self.chips - 1, self.final).start()
            self.store_copy(lane, self.chips - 1, self.final).start()

    def run(self, begin, end):
        chips = self.chips

        def loop(low, high, step_of):
            def one(step, carry):
                step_of(step)
                return carry

            if low < high:
                lax.fori_loop(low, high, one, 0)

        loop(begin + 1, min(end, chips - 2) + 1, self.reduce_step)
        if begin <= chips - 2 < end:
            self.turn()
        loop(max(begin - chips + 2, 1), min(end - chips + 1, chips - 2) + 1, self.spread_step)
        if end == 2 * (chips - 1):
            self.last()

    def settle(self):
        def swaps(rank, carry):
            for which in range(len(self.parts)):
                self.swap(rank, which).wait_send()
            return carry

        def steps(step, carry):
            for lane in range(len(self.lanes)):
                self.ring_copy(lane, step).wait_send()
                self.spread_copy(lane, step, self.final).wait_send()
            return carry

        def outs(step, carry):
            for lane in range(len(self.lanes)):
                self.cross_copy(lane, step, self.final).wait()
                self.store_copy(lane, step, self.final).wait()
            return carry

        if self.parts:
            lax.fori_loop(0, self.chips, swaps, 0)
        lax.fori_loop(0, self.chips - 1, steps, 0)
        lax.fori_loop(0, self.chips, outs, 0)


def ring_plan(total_rows, columns, devices, count):
    chips = devices // 2
    chunk_rows = total_rows // devices
    tiles = chunk_rows // TILE
    shares = [tiles // 4 + (1 if spot < tiles % 4 else 0) for spot in range(4)]
    lanes = []
    first = 0
    for sign, share in zip((1, -1, 1, -1), shares):
        if share:
            lanes.append((sign, first * TILE, share * TILE))
        first += share
    block = (chips, chunk_rows, columns)
    dma = pltpu.SemaphoreType.DMA
    buffers = [pltpu.VMEM(block, jnp.bfloat16)] * (2 * count + 2)
    sems = [dma((count, chips))] * 3 + [dma((len(lanes), chips))] * 7
    return chips, tuple(lanes), block, buffers, sems


class VectorRing(Ring):
    def carry_vectors(self, held, from_twin, arriving, final, sum_ref, send, recv, store):
        my_rows = pl.ds(pl.multiple_of(self.core * TILE, TILE), TILE)
        twin_rows = pl.ds(pl.multiple_of((1 - self.core) * TILE, TILE), TILE)
        self.vectors, self.from_twin, self.vector_in, self.vector_sum = held, from_twin, arriving, final
        self.my_rows = my_rows

        def copy(at, source, target, device):
            return self.remote(source, target, send.at[at], recv.at[at], device)

        self.vector_swap = copy(0, held.at[twin_rows], from_twin, self.twin)
        self.vector_ring = copy(1, held.at[my_rows], arriving, self.onward)
        self.vector_spread = copy(2, final, final, self.onward)
        self.vector_cross = copy(3, final, sum_ref.at[my_rows], self.twin)
        self.vector_out = pltpu.make_async_copy(final, sum_ref.at[my_rows], store.at[0])

    def add_vectors(self, source):
        self.vectors[self.my_rows, :] = (
            self.vectors[self.my_rows, :].astype(jnp.float32) + source[...].astype(jnp.float32)
        ).astype(jnp.bfloat16)

    def first(self):
        super().first()
        self.vector_swap.wait_recv()
        self.add_vectors(self.from_twin)

        @pl.when(self.place == 0)
        def _():
            self.vector_ring.start()

    def reduce_step(self, step):
        super().reduce_step(step)

        @pl.when(self.place == step)
        def _():
            self.vector_ring.wait_recv()
            self.add_vectors(self.vector_in)
            self.vector_ring.start()

    def turn(self):
        @pl.when(self.place == self.chips - 1)
        def _():
            self.vector_ring.wait_recv()
            self.add_vectors(self.vector_in)
            self.vector_sum[...] = self.vectors[self.my_rows, :]
            self.vector_spread.start()
            self.vector_cross.start()
            self.vector_out.start()

        super().turn()

    def pass_vectors(self, step, last):
        @pl.when((self.place + 1) % self.chips == step)
        def _():
            self.vector_spread.wait_recv()
            if not last:
                self.vector_spread.start()
            self.vector_cross.start()
            self.vector_out.start()

    def spread_step(self, step):
        super().spread_step(step)
        self.pass_vectors(step, False)

    def last(self):
        super().last()
        self.pass_vectors(self.chips - 1, True)

    def settle(self):
        super().settle()
        self.vector_swap.wait_send()
        self.vector_cross.wait()
        self.vector_out.wait()

        @pl.when(self.place != self.chips - 1)
        def _():
            self.vector_ring.wait_send()

        @pl.when(self.place != self.chips - 2)
        def _():
            self.vector_spread.wait_send()


def ring_sum_kernel(chips, lanes, count, *refs):
    parts, vectors = refs[:count], refs[count : 2 * count]
    sum_ref, vector_ref = refs[2 * count : 2 * count + 2]
    refs = refs[2 * count + 2 :]
    buffers, refs = refs[: 2 * count + 2], refs[2 * count + 2 :]
    sems, refs = refs[:10], refs[10:]
    places = ring_places(chips)
    barrier = greet(places[2:])
    ring = VectorRing(chips, lanes, places, parts, sum_ref, buffers, sems)
    ring.carry_vectors(*refs[:4], vector_ref, *refs[4:])
    ring.start_loads()
    total = vectors[0][...]
    for item in vectors[1:]:
        total = total + item[...]
    refs[0][...] = total.astype(jnp.bfloat16)
    pl.semaphore_wait(barrier, 3)
    ring.start_swaps()
    ring.vector_swap.start()
    ring.first()
    ring.run(0, 2 * (chips - 1))
    ring.settle()


def ring_sum(parts, vectors, devices):
    total_rows, columns = parts[0].shape
    count = len(parts)
    chips, lanes, block, buffers, sems = ring_plan(total_rows, columns, devices, count)
    bf = jnp.bfloat16
    dma = pltpu.SemaphoreType.DMA
    any_spec = pl.BlockSpec(memory_space=pl.ANY)
    vmem_spec = pl.BlockSpec(memory_space=pltpu.VMEM)
    vector_shape = vectors[0].shape
    return pl.pallas_call(
        functools.partial(ring_sum_kernel, chips, lanes, count),
        out_shape=[
            jax.ShapeDtypeStruct((2,) + block, bf),
            jax.ShapeDtypeStruct(vector_shape, bf),
        ],
        in_specs=[any_spec] * count + [vmem_spec] * count,
        out_specs=[any_spec] * 2,
        scratch_shapes=buffers
        + sems
        + [pltpu.VMEM(vector_shape, bf)]
        + [pltpu.VMEM((TILE, columns), bf)] * 3
        + [dma((4,)), dma((4,)), dma((1,))],
        compiler_params=pltpu.CompilerParams(
            collective_id=1, has_side_effects=True, vmem_limit_bytes=VMEM_BYTES
        ),
    )(*[item.reshape((2,) + block) for item in parts], *vectors)


BACK_GROUPS = ((N.dy, N.wd, N.normed_hidden), (N.spread, N.slope, N.wu, N.residual),
               (N.wo, N.attended, N.projected, N.log_total), (N.wq, N.x))
REST_LEFT = (N.normed_ffn, N.normed_mix, N.normed_in)
REST_RIGHT = (N.d_pre, N.d_branch, N.d_proj)
TICKS = 14


def tail_kernel(chips, lanes, slot, buffers, lengths_ref, assign_ref, *refs):
    back_names = sum(BACK_GROUPS, ())
    sources = dict(zip(back_names, refs))
    sources[N.x] = sources[N.x].at[slot]
    refs = refs[len(back_names) :]
    vectors, refs = refs[:4], refs[4:]
    rest_names = REST_LEFT + REST_RIGHT + (N.sums,)
    rest_sources, refs = dict(zip(rest_names, refs)), refs[len(rest_names) :]
    base_sums, base_ref, part_ref, refs = refs[0], refs[1], refs[2], refs[4:]
    dx_out, sum_refs, vector_out, refs = refs[0], refs[1:4], refs[4], refs[5:]
    held = dict(zip(buffers, refs))
    refs = refs[len(buffers) :]
    pools, refs = refs[:2], refs[2:]
    ring_buffers, refs = (refs[:4], refs[4:8]), refs[8:]
    stage, turned, refs = refs[0], refs[1], refs[2:]
    vector_buffers, refs = refs[:4], refs[4:]
    ring_sems, refs = (refs[:10], refs[10:20], refs[20:30]), refs[30:]
    vector_sems, refs = refs[:3], refs[3:]
    back_sem, rest_sem, base_sem, dx_sem, free_sem = refs
    rows, width = held[N.dy].shape
    hidden = held[N.wide_scratch].shape[1]
    wide = hidden // width
    half_blocks = wide // 2
    each = width // stage.shape[2]
    spent, scratch = held[N.normed_hidden], held[N.wide_scratch]
    held[N.d_down] = held[N.dy]
    held[N.d_pre] = held[N.slope]
    held[N.d_proj] = held[N.projected]
    held[N.d_attended] = spent.at[:, 0:width]
    held[N.dx] = spent.at[:, width : 2 * width]
    held[N.d_branch] = spent.at[:, 2 * width : 3 * width]
    held[N.d_residual] = scratch.at[:, 0:width]
    held[N.bias_back] = scratch.at[:, width : width + rows]

    places = ring_places(chips)
    place, core, onward, backward, twin = places
    barrier = greet(places[2:])
    late_buffers = [pool.at[pl.ds(half * chips, chips)] for pool in pools for half in range(2)]
    first_ring = Ring(chips, lanes, places, (part_ref,), sum_refs[0], ring_buffers[0], ring_sems[0])
    second_ring = Ring(chips, lanes, places, (), sum_refs[1], ring_buffers[1], ring_sems[1])
    third_ring = VectorRing(chips, lanes, places, (), sum_refs[2], late_buffers, ring_sems[2])
    third_ring.carry_vectors(*vector_buffers, vector_out, *vector_sems)
    on_lower = lax.axis_index("pipe") == 0

    def base_loads(ring, at, first):
        own = first * each + core * half_blocks * each
        other = first * each + (1 - core) * half_blocks * each
        count = half_blocks * each
        copies = [
            pltpu.make_async_copy(
                base_ref.at[pl.ds(own, count)], ring.held.at[pl.ds(0, count)], base_sem.at[at, 0]
            )
        ]
        for block in range(half_blocks):
            copies.append(
                pltpu.make_async_copy(
                    base_ref.at[pl.ds(other + block * each, each)],
                    stage.at[block],
                    base_sem.at[at, 1 + block],
                )
            )
        return copies

    def clear_padding(ring):
        count = half_blocks * each
        if chips > count:
            for item in (ring.held, ring.from_core[0]):
                item[count:] = jnp.zeros((chips - count,) + item.shape[1:], jnp.bfloat16)

    def block_swap(ring, block):
        return ring.remote(
            stage.at[block],
            ring.from_core[0].at[pl.ds(block * each, each)],
            ring.core_send.at[0, block],
            ring.core_recv.at[0, block],
            twin,
        )

    def add_block(ring, index, right):
        half, block = index // half_blocks, index % half_blocks
        chunks = slice(block * each, (block + 1) * each)
        product = dot_nn(turned[...], right).reshape((each,) + stage.shape[2:])

        @pl.when(core == half)
        def _():
            total = ring.held[chunks].astype(jnp.float32) + product
            ring.held[chunks] = total.astype(jnp.bfloat16)

        @pl.when(core != half)
        def _():
            total = stage[block].astype(jnp.float32) + product
            stage[block] = total.astype(jnp.bfloat16)
            block_swap(ring, block).start()

    def begin(ring):
        for block in range(half_blocks):
            block_swap(ring, block).wait_recv()
        ring.first()

    loads = {}
    for at, name in enumerate(back_names):
        copies = [(sources[name], held.get(name))]
        if name == N.wd:
            copies = [(sources[name], pools[0].at[pl.ds(0, wide * each)])]
        if name == N.wu:
            copies = []
            for block in range(wide):
                cols = pl.ds(block * width, width)
                target = pools[1].at[pl.ds(block * each, each)]
                copies.append((sources[name].at[:, :, cols], target))
        loads[name] = [
            pltpu.make_async_copy(source, target, back_sem.at[at, piece])
            for piece, (source, target) in enumerate(copies)
        ]
    rest_loads = {
        name: pltpu.make_async_copy(rest_sources[name], held[name], rest_sem.at[at])
        for at, name in enumerate(rest_names)
    }
    first_ring.start_loads()

    @pl.when(on_lower)
    def _():
        for name in back_names:
            for item in loads[name]:
                item.start()

    @pl.when(jnp.logical_not(on_lower))
    def _():
        for name in REST_RIGHT + (N.sums,):
            rest_loads[name].start()

    for name in REST_LEFT:
        rest_loads[name].start()
    second_base = base_loads(second_ring, 0, 4)
    for item in second_base:
        item.start()
    clear_padding(second_ring)
    pl.semaphore_wait(barrier, 3)
    first_ring.start_swaps()
    first_ring.first()

    steps = 2 * (chips - 1)
    rings = (first_ring, second_ring, third_ring)

    def tick(which, done):
        at = done[which]
        if at < TICKS:
            rings[which].run(at * steps // TICKS, (at + 1) * steps // TICKS)
            done[which] += 1

    def up_grads(done):
        rest_loads[N.normed_ffn].wait()
        turned[...] = held[N.normed_ffn][...].T
        for item in second_base:
            item.wait()
        for block in range(wide):
            cols = slice(block * width, (block + 1) * width)
            add_block(second_ring, block, held[N.d_pre][:, cols])
            if block == half_blocks - 1:
                tick(0, done)
        begin(second_ring)

    def free_pools():
        for other in (onward, backward, twin):
            pl.semaphore_signal(free_sem, inc=1, device_id=other, device_id_type=MESH_IDS)

    order = (0, 1, 0, 1, 0, 1)
    start = [0, 0, 0]

    @pl.when(on_lower)
    def _():
        waited = set()
        done = list(start)
        count = []

        def ready(name):
            for group in BACK_GROUPS:
                if name in group and name not in waited:
                    waited.update(group)
                    for item in group:
                        for piece in loads[item]:
                            piece.wait()

        def emit(name):
            if name == N.dx:
                pltpu.make_async_copy(held[N.dx], dx_out, dx_sem.at[0]).start()

        def one_tick():
            if len(count) == 0:
                tick(0, done)
            else:
                if len(count) == 1:
                    free_pools()
                tick(order[len(count) - 1], done)
            count.append(0)

        def middle():
            tick(0, done)
            up_grads(done)

        length = slot_length(lengths_ref, assign_ref, slot)
        backward_body(
            held, vectors, length, False, ready, emit, one_tick, pools=pools, middle=middle
        )
        tick(order[-1], done)

    @pl.when(jnp.logical_not(on_lower))
    def _():
        done = list(start)
        free_pools()
        for name in REST_RIGHT + (N.sums,):
            rest_loads[name].wait()
        tick(0, done)
        tick(0, done)
        up_grads(done)
        for which in order:
            tick(which, done)

    done = [3 + order.count(0), order.count(1), 0]
    for name in REST_LEFT[1:]:
        rest_loads[name].wait()
    vector_buffers[0][...] = (base_sums[...] + held[N.sums][...]).astype(jnp.bfloat16)

    pl.semaphore_wait(free_sem, 3)
    third_ring.vector_swap.start()
    third_base = base_loads(third_ring, 1, 0)
    third_base[0].start()
    for block in range(half_blocks):
        for half in range(2):

            @pl.when(core != half)
            def _():
                block_swap(second_ring, block).wait_send()

        third_base[1 + block].start()
    clear_padding(third_ring)
    turned[...] = held[N.normed_in][...].T
    for item in third_base:
        item.wait()
    for block in range(4):
        if block == 3:
            turned[...] = held[N.normed_mix][...].T
        right = held[N.d_branch][...] if block == 3 else None
        if right is None:
            right = held[N.d_proj][:, block * width : (block + 1) * width]
        add_block(third_ring, block, right)
        if block == 1:
            tick(0, done)
            tick(1, done)
    begin(third_ring)
    while min(done) < TICKS:
        for which in range(3):
            tick(which, done)
    for ring in rings:
        ring.settle()
    for block in range(half_blocks):
        block_swap(third_ring, block).wait_send()

    @pl.when(on_lower)
    def _():
        pltpu.make_async_copy(held[N.dx], dx_out, dx_sem.at[0]).wait()


def tail_call(slot, sizes, given, vectors, kept, grads, base_sums, base, part, devices):
    rows, width = given[N.dy].shape
    hidden = given[N.wu].shape[1]
    wide = hidden // width
    shapes = buffer_shapes(rows, width, hidden)
    chunk = chunk_rows(width, hidden, devices)
    chips, lanes, block, ring_buffers, ring_sems = ring_plan(chunk * devices, width, devices, 1)
    back_names = sum(BACK_GROUPS, ())
    rest_names = REST_LEFT + REST_RIGHT + (N.sums,)
    given = dict(given)
    given[N.wd] = given[N.wd].reshape(hidden // chunk, chunk, width)
    given[N.wu] = given[N.wu].reshape(width // chunk, chunk, hidden)
    buffers = tuple(name for name in back_names if name not in (N.wd, N.wu)) + REST_LEFT
    buffers += (N.sums, N.wide_scratch, N.delta)
    any_spec = pl.BlockSpec(memory_space=pl.ANY)
    vmem_spec = pl.BlockSpec(memory_space=pltpu.VMEM)
    smem_spec = pl.BlockSpec(memory_space=pltpu.SMEM)
    bf = jnp.bfloat16
    args = list(sizes) + [given[name] for name in back_names] + list(vectors)
    args += [kept[name] for name in REST_LEFT] + [grads[name] for name in REST_RIGHT + (N.sums,)]
    args += [base_sums, base.reshape(-1, chunk, width), part.reshape((2,) + block), grads[N.dx]]
    in_specs = [smem_spec] * 2 + [any_spec] * len(back_names) + [vmem_spec] * 4
    in_specs += [any_spec] * len(rest_names) + [vmem_spec] + [any_spec] * 3
    sum_shape = jax.ShapeDtypeStruct((2,) + block, bf)
    out_shape = [jax.ShapeDtypeStruct((rows, width), bf)] + [sum_shape] * 3
    out_shape.append(jax.ShapeDtypeStruct((SUM_ROWS, width), bf))
    dma = pltpu.SemaphoreType.DMA
    pool = pltpu.VMEM((2 * chips,) + block[1:], bf)
    return pl.pallas_call(
        functools.partial(tail_kernel, chips, lanes, slot, buffers),
        out_shape=out_shape,
        in_specs=in_specs,
        out_specs=[any_spec] * len(out_shape),
        input_output_aliases={len(args) - 1: 0},
        scratch_shapes=[pltpu.VMEM(*shapes[name]) for name in buffers]
        + [pool] * 2
        + ring_buffers * 2
        + [pltpu.VMEM((wide // 2, width // chunk, chunk, width), bf), pltpu.VMEM((width, rows), bf)]
        + [pltpu.VMEM((SUM_ROWS, width), bf)]
        + [pltpu.VMEM((TILE, width), bf)] * 3
        + ring_sems * 3
        + [dma((4,)), dma((4,)), dma((1,))]
        + [dma((len(back_names), wide)), dma((len(rest_names),)), dma((2, 1 + wide // 2)), dma((1,))]
        + [pltpu.SemaphoreType.REGULAR],
        compiler_params=pltpu.CompilerParams(
            collective_id=0, has_side_effects=True, vmem_limit_bytes=TAIL_VMEM_BYTES
        ),
    )(*args)


def finish_kernel(steps, count, down_hbm, up_hbm, rest_hbm, vectors, *refs):
    moved, refs = refs[: 2 * count], refs[2 * count :]
    outs, refs = refs[:4], refs[4:]
    gains, shifts, hidden_gains, hidden_shifts = refs[:4]
    stacked, refs = refs[4:6], refs[6:]
    narrow, broad, passing, in_sem, out_sem, arrive_sem, leave_sem = refs
    width = rest_hbm.shape[1]
    arrivals, departures = [], []
    for at, source in enumerate(moved):
        target = stacked[at // count].at[at % count]
        arrivals.append(pltpu.make_async_copy(source, passing.at[at], arrive_sem.at[at]))
        departures.append(pltpu.make_async_copy(passing.at[at], target, leave_sem.at[at]))

    def load(step):
        which, first, row, column = steps[step]
        source = (rest_hbm, rest_hbm, up_hbm, down_hbm)[which].at[pl.ds(first, width)]
        return pltpu.make_async_copy(source, narrow.at[step % DEPTH], in_sem.at[step % DEPTH])

    def store(step):
        which, first, row, column = steps[step]
        target = outs[which].at[pl.ds(row, width), pl.ds(column, width)]
        return pltpu.make_async_copy(broad.at[step % DEPTH], target, out_sem.at[step % DEPTH])

    for step in range(DEPTH):
        load(step).start()
    for item in arrivals:
        item.start()
    values = vectors[...].astype(jnp.float32)
    for row in range(3):
        gains[row] = values[row : row + 1]
    for row in range(7):
        shifts[row] = values[3 + row : 4 + row]
    wide = hidden_gains.shape[1] // width
    for block in range(wide):
        cols = slice(block * width, (block + 1) * width)
        hidden_gains[:, cols] = values[10 + block : 11 + block]
        for row in range(2):
            first = 10 + (row + 1) * wide + block
            hidden_shifts[row : row + 1, cols] = values[first : first + 1]
    for step in range(len(steps)):
        load(step).wait()
        if step >= DEPTH:
            store(step - DEPTH).wait()
        broad[step % DEPTH] = narrow[step % DEPTH].astype(jnp.float32)
        store(step).start()
        if step + DEPTH < len(steps):
            load(step + DEPTH).start()
        if step == DEPTH:
            for arrival, departure in zip(arrivals, departures):
                arrival.wait()
                departure.start()
    for step in range(len(steps) - DEPTH, len(steps)):
        store(step).wait()
    for item in departures:
        item.wait()


def finish(down, up, rest, vectors, slots_out, slots_grad, hidden):
    width = rest.shape[1]
    wide = hidden // width
    count = len(slots_out)
    half_rows = down.shape[0] // 2
    firsts = [block_row(block, width, hidden, half_rows) for block in range(wide)]
    steps = [(3, firsts[block], block * width, 0) for block in range(wide)]
    steps += [(2, firsts[block], 0, block * width) for block in range(wide)]
    steps += [(0, firsts[block], 0, block * width) for block in range(3)]
    steps.append((1, firsts[3], 0, 0))
    f = jnp.float32
    shapes = [(width, 3 * width), (width, width), (width, hidden), (hidden, width)]
    shapes += [(3, 1, width), (7, 1, width), (1, hidden), (2, hidden)]
    any_spec = pl.BlockSpec(memory_space=pl.ANY)
    vmem_spec = pl.BlockSpec(memory_space=pltpu.VMEM)
    out_shape = [jax.ShapeDtypeStruct(shape, f) for shape in shapes]
    pile = jax.ShapeDtypeStruct((count,) + slots_out[0].shape, slots_out[0].dtype)
    return pl.pallas_call(
        functools.partial(finish_kernel, tuple(steps), count),
        out_shape=out_shape + [pile, pile],
        in_specs=[any_spec] * 3 + [vmem_spec] + [any_spec] * (2 * count),
        out_specs=[any_spec] * 4 + [vmem_spec] * 4 + [any_spec] * 2,
        scratch_shapes=[
            pltpu.VMEM((DEPTH, width, width), jnp.bfloat16),
            pltpu.VMEM((DEPTH, width, width), f),
            pltpu.VMEM((2 * count,) + slots_out[0].shape, slots_out[0].dtype),
            pltpu.SemaphoreType.DMA((DEPTH,)),
            pltpu.SemaphoreType.DMA((DEPTH,)),
            pltpu.SemaphoreType.DMA((2 * count,)),
            pltpu.SemaphoreType.DMA((2 * count,)),
        ],
        compiler_params=pltpu.CompilerParams(vmem_limit_bytes=VMEM_BYTES),
    )(down, up, rest, vectors, *slots_out, *slots_grad)


def passed_along(block, axis, distance):
    devices = range(lax.axis_size(axis))
    route = [(i - distance, i) for i in devices if i - distance in devices]
    return lax.ppermute(block, axis, route)


def shards(
    inputs,
    cotangent,
    lengths,
    assign,
    query_key_value,
    out_weight,
    up_weight,
    down_weight,
    model_gains,
    model_shifts,
    hidden_gains,
    hidden_shifts,
):
    micro_count = inputs.shape[0]
    hidden = up_weight.shape[2]
    slots = range(micro_count)
    weights = {
        N.wq: query_key_value[0],
        N.wo: out_weight[0],
        N.wu: up_weight[0],
        N.wd: down_weight[0],
    }
    by_row = [jnp.transpose(item, (1, 0, 2)) for item in (model_gains, model_shifts)]
    vectors = (*by_row, hidden_gains, hidden_shifts)

    sizes = (lengths, assign)

    def run(steps, plane, slot, given, previous, after=()):
        return layer_call(
            steps, plane, slot, sizes, {**weights, **given}, vectors, previous, after
        )

    lower, upper = [], []
    for slot in slots:
        after = [lower[-1][N.spread]] if lower else []
        lower.append(run((N.forward,), 0, slot, {N.x: inputs}, {}, after))
    middle = [passed_along(lower[slot][N.y], "pipe", 1) for slot in slots]
    for slot in slots:
        after = [upper[-1][N.sums]] if upper else []
        given = {N.x: middle[slot], N.dy: cotangent}
        upper.append(run((N.forward, N.backward), 1, slot, given, lower[slot], after))
    returned = [passed_along(upper[slot][N.dx], "pipe", -1) for slot in slots]
    kept = [{**lower[slot], **upper[slot]} for slot in slots]
    devices = lax.axis_size("batch")
    first, final = slots
    given = {**kept[first], N.x: inputs, N.dy: returned[first]}
    first_grads = run((N.backward,), 0, first, given, kept[first])
    base_down, base_rest = weight_grads(kept[first], first_grads)
    width = inputs.shape[2]
    half_rows = chunk_rows(width, hidden, devices) * (devices // 2)
    given = {**kept[final], N.x: inputs, N.dy: returned[final]}
    if 2 * half_rows == hidden:
        down_part = down_grad(
            kept[final][N.normed_hidden],
            returned[final],
            upper[final][N.d_down],
            base_down,
            half_rows,
        )
        dx, *sums, vector_sum = tail_call(
            final, sizes, {**weights, **given}, vectors, kept[final], upper[final], first_grads[N.sums], base_rest,
            down_part, devices,
        )
    else:
        final_grads = run((N.backward,), 0, final, given, kept[final])
        dx = final_grads[N.dx]
        last_down, last_rest = weight_grads(kept[final], final_grads)
        parts = []
        for pair in ((base_down, base_rest), (last_down, last_rest)):
            packed = jnp.concatenate(pair, axis=0)
            missing = -packed.shape[0] % (TILE * devices)
            parts.append(jnp.pad(packed, ((0, missing), (0, 0))))
        packed, vector_sum = ring_sum(parts, [first_grads[N.sums], final_grads[N.sums]], devices)
        packed = packed.reshape(-1, width)
        ends = (hidden, hidden + 4 * width, 2 * hidden + 4 * width)
        sums = (packed[: ends[0]], packed[ends[1] : ends[2]], packed[ends[0] : ends[1]])
    outs = finish(
        *[item.reshape(-1, width) for item in sums],
        vector_sum,
        [kept[slot][N.y] for slot in slots],
        [first_grads[N.dx], dx],
        hidden,
    )
    by_row = [jnp.transpose(item, (1, 0, 2)) for item in outs[4:6]]
    return (*[item[None] for item in outs[8:] + outs[:4]], *by_row, outs[6], outs[7][None])


def solution(mesh):
    return jax.shard_map(
        shards,
        mesh=mesh,
        in_specs=(
            P(None, "batch", None),
            P(None, "batch", None),
            P("batch"),
            P("batch"),
            P("pipe", None, None),
            P("pipe", None, None),
            P("pipe", None, None),
            P("pipe", None, None),
            P("pipe", None, None),
            P("pipe", None, None),
            P("pipe", None),
            P("pipe", None, None),
        ),
        out_specs=(
            P("pipe", None, "batch", None),
            P("pipe", None, "batch", None),
            P("pipe", None, None),
            P("pipe", None, None),
            P("pipe", None, None),
            P("pipe", None, None),
            P("pipe", None, None),
            P("pipe", None, None),
            P("pipe", None),
            P("pipe", None, None),
        ),
        check_vma=False,
    )
```

```python
import functools
import types

import jax
import jax.numpy as jnp
from jax import lax
from jax.experimental import pallas as pl
from jax.experimental.pallas import tpu as pltpu
from jax.sharding import PartitionSpec as P

HEAD = 64
PAIR = 2 * HEAD
EPSILON = 1e-05
SCALE = 0.125
HIDDEN_NEG = -1e30
CHUNK = 512
SUM_ROWS = 32
DEPTH = 3
HEAD_ROWS = 16

TILE = 16
VMEM_BYTES = 60 * 1024 * 1024
TAIL_VMEM_BYTES = 63 * 1024 * 1024
MESH_IDS = pl.DeviceIdType.MESH


def named(**given):
    return types.SimpleNamespace(**{name: name for name in given})


N = named(
    x=0,
    dy=0,
    y=0,
    dx=0,
    wq=0,
    wo=0,
    wu=0,
    wd=0,
    normed_in=0,
    projected=0,
    log_total=0,
    attended=0,
    normed_mix=0,
    residual=0,
    normed_ffn=0,
    normed_hidden=0,
    slope=0,
    spread=0,
    d_down=0,
    d_pre=0,
    d_branch=0,
    d_proj=0,
    sums=0,
    wide_scratch=0,
    d_residual=0,
    d_attended=0,
    delta=0,
    bias=0,
    bias_back=0,
    forward=0,
    backward=0,
)


def dot_nn(left, right):
    return jnp.dot(left, right, preferred_element_type=jnp.float32)


def dot_nt(left, right):
    return lax.dot_general(
        left, right, (((1,), (1,)), ((), ())), preferred_element_type=jnp.float32
    )


def standardize(values_in):
    centred = values_in - jnp.mean(values_in, axis=-1, keepdims=True)
    scale = lax.rsqrt(jnp.mean(centred * centred, axis=-1, keepdims=True) + EPSILON)
    return centred * scale, scale


def unit_backward(grad, unit, scale, gain):
    scaled = grad * gain
    first = jnp.mean(scaled, axis=-1, keepdims=True)
    second = jnp.mean(scaled * unit, axis=-1, keepdims=True)
    return (
        scale * (scaled - first - unit * second),
        jnp.sum(grad * unit, axis=0, keepdims=True),
        jnp.sum(grad, axis=0, keepdims=True),
    )


def column_sum(values):
    return jnp.sum(values.astype(jnp.float32), axis=0, keepdims=True)


def hiding_bias(rows, length, query_dim):
    query = lax.broadcasted_iota(jnp.int32, (rows, rows), query_dim)
    key = lax.broadcasted_iota(jnp.int32, (rows, rows), 1 - query_dim)
    visible = (key <= query) & ((key < length) | (key == query))
    return jnp.where(visible, 0.0, HIDDEN_NEG)


def own_lanes(values, which):
    lane = lax.broadcasted_iota(jnp.int32, values.shape, 1)
    mine = (lane >= HEAD) if which else (lane < HEAD)
    return jnp.where(mine, values, jnp.zeros_like(values))


def attend_forward(projected, attended, log_total, bias):
    rows, width = attended.shape
    half = rows // 2
    lane = lax.broadcasted_iota(jnp.int32, (half, PAIR), 1)

    def one_pair(pair, totals):
        first = pl.multiple_of(pair * PAIR, PAIR)
        items = []
        for block in range(2):
            at = slice(block * half, (block + 1) * half)
            reach = (block + 1) * half
            q = projected[at, pl.ds(first, PAIR)] * jnp.bfloat16(SCALE)
            k = projected[0:reach, pl.ds(width + first, PAIR)]
            v = projected[0:reach, pl.ds(2 * width + first, PAIR)]
            items += [(at, reach, own_lanes(q, which), k, v) for which in range(2)]
        scores = [dot_nt(q, k) + bias[at, 0:reach] for at, reach, q, k, v in items]
        softened = []
        for item in scores:
            top = jnp.max(item, axis=-1, keepdims=True)
            exps = jnp.exp(item - top)
            softened.append((exps, jnp.sum(exps, axis=-1, keepdims=True), top))
        mixed = [
            dot_nn(exps.astype(jnp.bfloat16), item[4]) * (1.0 / total)
            for item, (exps, total, top) in zip(items, softened)
        ]
        new_totals = []
        for block in range(2):
            at = items[2 * block][0]
            attended[at, pl.ds(first, PAIR)] = jnp.where(
                lane < HEAD, mixed[2 * block], mixed[2 * block + 1]
            )
            logs = totals[block]
            for which in range(2):
                exps, total, top = softened[2 * block + which]
                logs = jnp.where(lane == 2 * pair + which, top + jnp.log(total), logs)
            new_totals.append(logs)
        return tuple(new_totals)

    zero = jnp.zeros((half, PAIR), jnp.float32)
    totals = lax.fori_loop(0, width // PAIR, one_pair, (zero, zero), unroll=2)
    for block in range(2):
        log_total[:, block * half : (block + 1) * half] = totals[block].T[0:HEAD_ROWS]


def attend_backward(projected, d_attended, log_total, delta, bias, d_proj, tick):
    rows, width = d_attended.shape
    half = rows // 2

    def one_pair(pair, carry):
        first = pl.multiple_of(pair * PAIR, PAIR)
        k_all = projected[:, pl.ds(width + first, PAIR)]
        v_all = projected[:, pl.ds(2 * width + first, PAIR)]
        k_turned = k_all.T
        items = []
        for block in range(2):
            at = slice(block * half, (block + 1) * half)
            q = projected[at, pl.ds(first, PAIR)] * jnp.bfloat16(SCALE)
            grad = d_attended[at, pl.ds(first, PAIR)]
            for which in range(2):
                items.append((block, which, at, own_lanes(q, which), own_lanes(grad, which)))
        raw = []
        for block, which, at, q, grad in items:
            reach = (block + 1) * half
            raw.append((dot_nt(k_all[0:reach], q), dot_nt(v_all[0:reach], grad)))
        shaped = []
        for (block, which, at, q, grad), (scores, d_probs) in zip(items, raw):
            reach = (block + 1) * half
            head = pl.ds(2 * pair + which, 1)
            probs = jnp.exp(scores + bias[0:reach, at] - log_total[head, at])
            d_scores = (probs * (d_probs - delta[head, at])).astype(jnp.bfloat16)
            shaped.append((probs.astype(jnp.bfloat16), d_scores))
        dk = [None, None]
        dv = [None, None]
        dq = []
        for (block, which, at, q, grad), (probs, d_scores) in zip(items, shaped):
            reach = (block + 1) * half
            more_v = dot_nn(probs, grad)
            more_k = dot_nn(d_scores, q)
            dq.append(dot_nn(k_turned[which * HEAD : (which + 1) * HEAD, 0:reach], d_scores))
            for part in range(block + 1):
                piece = slice(part * half, (part + 1) * half)
                dv[part] = more_v[piece] if dv[part] is None else dv[part] + more_v[piece]
                dk[part] = more_k[piece] if dk[part] is None else dk[part] + more_k[piece]
        for block in range(2):
            at = slice(block * half, (block + 1) * half)
            turned = jnp.concatenate(dq[2 * block : 2 * block + 2], axis=0) * SCALE
            d_proj[at, pl.ds(first, PAIR)] = turned.T.astype(jnp.bfloat16)
            d_proj[at, pl.ds(width + first, PAIR)] = dk[block].astype(jnp.bfloat16)
            d_proj[at, pl.ds(2 * width + first, PAIR)] = dv[block].astype(jnp.bfloat16)
        return carry

    if tick is None:
        lax.fori_loop(0, width // PAIR, one_pair, 0, unroll=2)
    else:
        for first in range(0, width // PAIR, 2):
            lax.fori_loop(first, min(first + 2, width // PAIR), one_pair, 0, unroll=True)
            tick()


KEPT = (N.normed_in, N.projected, N.log_total, N.attended, N.normed_mix, N.residual,
        N.normed_ffn, N.normed_hidden, N.slope, N.spread)
GRADS = (N.d_down, N.d_pre, N.d_branch, N.d_proj, N.sums)


def buffer_shapes(rows, width, hidden):
    bf, f = jnp.bfloat16, jnp.float32
    return {
        N.x: ((rows, width), bf),
        N.dy: ((rows, width), bf),
        N.y: ((rows, width), bf),
        N.dx: ((rows, width), bf),
        N.wq: ((width, 3 * width), bf),
        N.wo: ((width, width), bf),
        N.wu: ((width, hidden), bf),
        N.wd: ((hidden, width), bf),
        N.normed_in: ((rows, width), bf),
        N.projected: ((rows, 3 * width), bf),
        N.log_total: ((HEAD_ROWS, rows), f),
        N.attended: ((rows, width), f),
        N.normed_mix: ((rows, width), bf),
        N.residual: ((rows, width), f),
        N.normed_ffn: ((rows, width), bf),
        N.normed_hidden: ((rows, hidden), bf),
        N.slope: ((rows, hidden), bf),
        N.spread: ((rows, PAIR), f),
        N.d_down: ((rows, width), bf),
        N.d_pre: ((rows, hidden), bf),
        N.d_branch: ((rows, width), bf),
        N.d_proj: ((rows, 3 * width), bf),
        N.sums: ((SUM_ROWS, width), f),
        N.wide_scratch: ((rows, hidden), f),
        N.d_residual: ((rows, width), f),
        N.d_attended: ((rows, width), bf),
        N.delta: ((HEAD_ROWS, rows), f),
        N.bias: ((rows, rows), f),
        N.bias_back: ((rows, rows), f),
    }


def forward_body(held, vectors, length, ready, emit):
    gm, sm, gh, sh = vectors
    sh = sh.at[0]
    bf = jnp.bfloat16
    rows, width = held[N.x].shape
    hidden = held[N.wu].shape[1]
    wide_scratch = held[N.wide_scratch]
    held[N.bias][...] = hiding_bias(rows, length, 0)
    ready(N.x)
    unit, unused = standardize(held[N.x][...].astype(jnp.float32))
    held[N.normed_in][...] = (unit * gm[0] + sm[0]).astype(bf)
    emit(N.normed_in)
    for block in range(3):
        cols = slice(block * width, (block + 1) * width)
        ready(N.wq)
        out = dot_nn(held[N.normed_in][...], held[N.wq][:, cols])
        if block != 1:
            out = out + sm[1 + block // 2]
        held[N.projected][:, cols] = out.astype(bf)
    emit(N.projected)
    attend_forward(held[N.projected], held[N.attended], held[N.log_total], held[N.bias])
    emit(N.log_total)
    emit(N.attended)

    unit, unused = standardize(held[N.attended][...])
    held[N.normed_mix][...] = (unit * gm[1] + sm[3]).astype(bf)
    emit(N.normed_mix)
    ready(N.wo)
    residual = held[N.x][...].astype(jnp.float32) + sm[4]
    residual = residual + dot_nn(held[N.normed_mix][...], held[N.wo][...])
    held[N.residual][...] = residual
    emit(N.residual)
    unit, unused = standardize(residual)
    held[N.normed_ffn][...] = (unit * gm[2] + sm[5]).astype(bf)
    emit(N.normed_ffn)
    ready(N.wu)
    total = jnp.zeros((rows, 1), jnp.float32)
    for first in range(0, hidden, CHUNK):
        cols = slice(first, first + CHUNK)
        pre = dot_nn(held[N.normed_ffn][...], held[N.wu][:, cols]) + sh[0:1, cols]
        share = 0.5 + 0.5 * lax.erf(pre * 0.7071067811865476)
        density = 0.3989422804014327 * jnp.exp(-0.5 * pre * pre)
        act = pre * share
        held[N.slope][:, cols] = (share + pre * density).astype(bf)
        wide_scratch[:, cols] = act
        total = total + jnp.sum(act, axis=-1, keepdims=True)
    emit(N.slope)
    mean = total * (1.0 / hidden)
    square = jnp.zeros((rows, 1), jnp.float32)
    for first in range(0, hidden, CHUNK):
        centred = wide_scratch[:, first : first + CHUNK] - mean
        square = square + jnp.sum(centred * centred, axis=-1, keepdims=True)
    scale = lax.rsqrt(square * (1.0 / hidden) + EPSILON)
    held[N.spread][...] = jnp.broadcast_to(scale, (rows, PAIR))
    emit(N.spread)
    for first in range(0, hidden, CHUNK):
        cols = slice(first, first + CHUNK)
        unit = (wide_scratch[:, cols] - mean) * scale
        held[N.normed_hidden][:, cols] = (unit * gh[0:1, cols] + sh[1:2, cols]).astype(bf)
    emit(N.normed_hidden)
    ready(N.wd)
    out = held[N.residual][...] + dot_nn(held[N.normed_hidden][...], held[N.wd][...])
    held[N.y][...] = (out + sm[6]).astype(bf)
    emit(N.y)


def pool_block(pool, block, width):
    each = width // pool.shape[1]
    return pool[block * each : (block + 1) * each].reshape(width, width)


def backward_body(held, vectors, length, masked, ready, emit, tick=None, pools=None, middle=None):
    gm, sm, gh, sh = vectors
    sh = sh.at[0]
    bf = jnp.bfloat16
    rows, width = held[N.x].shape
    hidden = held[N.wide_scratch].shape[1]
    wide = hidden // width
    wide_scratch, sums = held[N.wide_scratch], held[N.sums]
    sums[...] = jnp.zeros_like(sums)
    if pools is None:
        held[N.bias_back][...] = hiding_bias(rows, length, 1)
    ready(N.dy)
    d_down = held[N.dy][...]
    if masked:
        live = lax.broadcasted_iota(jnp.int32, (rows, 1), 0) < length
        d_down = jnp.where(live, d_down.astype(jnp.float32), 0.0).astype(bf)
    if tick is None:
        held[N.d_down][...] = d_down
    emit(N.d_down)
    sums[9:10, :] = column_sum(d_down)

    first_total = jnp.zeros((rows, 1), jnp.float32)
    second_total = jnp.zeros((rows, 1), jnp.float32)
    for block in range(wide):
        cols = slice(block * width, (block + 1) * width)
        ready(N.wd)
        ready(N.normed_hidden)
        weight = held[N.wd][cols, :] if pools is None else pool_block(pools[0], block, width)
        grad = dot_nt(held[N.d_down][...], weight)
        normed = held[N.normed_hidden][:, cols].astype(jnp.float32)
        unit = (normed - sh[1:2, cols]) * (1.0 / gh[0:1, cols])
        sums[10 + block : 11 + block, :] = jnp.sum(grad * unit, axis=0, keepdims=True)
        sums[18 + block : 19 + block, :] = jnp.sum(grad, axis=0, keepdims=True)
        scaled = grad * gh[0:1, cols]
        wide_scratch[:, cols] = scaled
        first_total = first_total + jnp.sum(scaled, axis=-1, keepdims=True)
        second_total = second_total + jnp.sum(scaled * unit, axis=-1, keepdims=True)
        if tick is not None and block == wide // 2 - 1:
            tick()
    first_mean = first_total * (1.0 / hidden)
    second_mean = second_total * (1.0 / hidden)
    ready(N.spread)
    ready(N.slope)
    scale = held[N.spread][:, 0:1]
    for block in range(wide):
        cols = slice(block * width, (block + 1) * width)
        normed = held[N.normed_hidden][:, cols].astype(jnp.float32)
        unit = (normed - sh[1:2, cols]) * (1.0 / gh[0:1, cols])
        d_act = scale * (wide_scratch[:, cols] - first_mean - unit * second_mean)
        d_pre = (d_act * held[N.slope][:, cols].astype(jnp.float32)).astype(bf)
        held[N.d_pre][:, cols] = d_pre
        sums[14 + block : 15 + block, :] = column_sum(d_pre)
    emit(N.d_pre)
    if middle is not None:
        middle()

    ready(N.wu)
    if pools is None:
        d_ffn = dot_nt(held[N.d_pre][...], held[N.wu][...])
    else:
        d_ffn = jnp.zeros((rows, width), jnp.float32)
        for block in range(wide):
            cols = slice(block * width, (block + 1) * width)
            d_ffn = d_ffn + dot_nt(held[N.d_pre][:, cols], pool_block(pools[1], block, width))
    ready(N.residual)
    unit, scale = standardize(held[N.residual][...])
    through, gain_sum, shift_sum = unit_backward(d_ffn, unit, scale, gm[2])
    sums[2:3, :] = gain_sum
    sums[8:9, :] = shift_sum
    through = through + held[N.d_down][...].astype(jnp.float32)
    held[N.d_residual][...] = through
    held[N.d_branch][...] = through.astype(bf)
    emit(N.d_branch)
    sums[7:8, :] = column_sum(held[N.d_branch][...])
    if tick is not None:
        tick()

    ready(N.wo)
    d_mix = dot_nt(held[N.d_branch][...], held[N.wo][...])
    ready(N.attended)
    attended = held[N.attended][...]
    unit, scale = standardize(attended)
    through, gain_sum, shift_sum = unit_backward(d_mix, unit, scale, gm[1])
    sums[1:2, :] = gain_sum
    sums[6:7, :] = shift_sum
    held[N.d_attended][...] = through.astype(bf)
    product = held[N.d_attended][...].astype(jnp.float32) * attended
    upper = product.astype(bf)
    lower = (product - upper.astype(jnp.float32)).astype(bf)
    head_row = lax.broadcasted_iota(jnp.int32, (HEAD_ROWS, width), 0)
    head_col = lax.broadcasted_iota(jnp.int32, (HEAD_ROWS, width), 1) // HEAD
    chooser = jnp.where(head_row == head_col, 1.0, 0.0).astype(bf)
    held[N.delta][...] = dot_nt(chooser, upper) + dot_nt(chooser, lower)
    if tick is not None:
        tick()

    ready(N.projected)
    ready(N.log_total)
    if pools is not None:
        held[N.bias_back][...] = hiding_bias(rows, length, 1)
    attend_backward(
        held[N.projected], held[N.d_attended], held[N.log_total], held[N.delta],
        held[N.bias_back], held[N.d_proj], tick,
    )
    emit(N.d_proj)
    ready(N.wq)
    d_norm = dot_nt(held[N.d_proj][...], held[N.wq][...])
    sums[4:5, :] = column_sum(held[N.d_proj][:, 0:width])
    sums[5:6, :] = column_sum(held[N.d_proj][:, 2 * width :])
    ready(N.x)
    unit, scale = standardize(held[N.x][...].astype(jnp.float32))
    through, gain_sum, shift_sum = unit_backward(d_norm, unit, scale, gm[0])
    sums[0:1, :] = gain_sum
    sums[3:4, :] = shift_sum
    held[N.dx][...] = (through + held[N.d_residual][...]).astype(bf)
    emit(N.dx)
    emit(N.sums)


def slot_length(lengths_ref, assign_ref, slot):
    total = jnp.int32(0)
    for at in range(lengths_ref.shape[0]):
        total = total + jnp.where(assign_ref[at] == slot, lengths_ref[at], 0)
    return total


def layer_kernel(
    steps, plane, slot, groups, stacked, out_names, unread, buffers, lengths_ref, assign_ref, *refs
):
    in_names = sum(groups, ())
    sources = dict(zip(in_names, refs))
    for name in stacked:
        sources[name] = sources[name].at[slot]
    vectors = refs[len(in_names) : len(in_names) + 4]
    refs = refs[len(in_names) + 4 + unread :]
    targets = dict(zip(out_names, refs))
    refs = refs[len(out_names) :]
    held = dict(zip(buffers, refs))
    in_sem, out_sem = refs[len(buffers) :]

    @pl.when(lax.axis_index("pipe") == plane)
    def _():
        loads = {
            name: pltpu.make_async_copy(sources[name], held[name], in_sem.at[at])
            for at, name in enumerate(in_names)
        }
        stores = {
            name: pltpu.make_async_copy(held[name], targets[name], out_sem.at[at])
            for at, name in enumerate(out_names)
        }
        for name in in_names:
            loads[name].start()
        waited = set()

        def ready(name):
            for group in groups:
                if name in group and name not in waited:
                    waited.update(group)
                    for item in group:
                        loads[item].wait()

        def emit(name):
            if name in stores:
                stores[name].start()

        length = slot_length(lengths_ref, assign_ref, slot)
        if N.forward in steps:
            forward_body(held, vectors, length, ready, emit)
        if N.backward in steps:
            backward_body(held, vectors, length, N.forward in steps, ready, emit)
        for name in out_names:
            stores[name].wait()


FORWARD_ONLY = (N.projected, N.log_total, N.attended, N.residual, N.slope, N.spread)


def layer_call(steps, plane, slot, sizes, given, vectors, previous, after=()):
    stacked = tuple(name for name in (N.x, N.dy) if name in given and given[name].ndim == 3)
    rows, width = given[N.x].shape[-2:]
    hidden = given[N.wu].shape[1]
    shapes = buffer_shapes(rows, width, hidden)
    if steps == (N.forward,):
        groups = ((N.x, N.wq), (N.wo, N.wu, N.wd))
        out_names = (N.y,) + KEPT
        spare = (N.wide_scratch, N.bias)
    elif steps == (N.backward,):
        groups = ((N.dy, N.wd, N.normed_hidden), (N.spread, N.slope, N.wu, N.residual),
                  (N.wo, N.attended, N.projected, N.log_total), (N.wq, N.x))
        out_names = (N.dx,) + GRADS
        spare = (N.wide_scratch, N.bias_back, N.d_residual, N.d_attended, N.delta)
    else:
        groups = ((N.x, N.wq), (N.wo, N.wu), (N.wd, N.dy))
        out_names = (N.y,) + tuple(name for name in KEPT if name not in FORWARD_ONLY)
        out_names += (N.dx,) + GRADS
        spare = (N.wide_scratch, N.bias, N.bias_back, N.d_residual, N.d_attended, N.delta)
        spare += FORWARD_ONLY
    in_names = sum(groups, ())
    buffers = in_names + tuple(name for name in out_names if name not in in_names) + spare
    any_spec = pl.BlockSpec(memory_space=pl.ANY)
    vmem_spec = pl.BlockSpec(memory_space=pltpu.VMEM)
    smem_spec = pl.BlockSpec(memory_space=pltpu.SMEM)
    in_specs = [smem_spec] * 2 + [any_spec] * len(in_names) + [vmem_spec] * 4
    args = list(sizes) + [given[name] for name in in_names] + list(vectors)
    shared = [name for name in out_names if name in previous]
    aliases = {len(args) + at: out_names.index(name) for at, name in enumerate(shared)}
    in_specs += [any_spec] * len(shared)
    args += [previous[name] for name in shared]
    in_specs += [any_spec] * len(after)
    args += list(after)
    scratch = [pltpu.VMEM(*shapes[name]) for name in buffers]
    scratch.append(pltpu.SemaphoreType.DMA((len(in_names),)))
    scratch.append(pltpu.SemaphoreType.DMA((len(out_names),)))
    outs = pl.pallas_call(
        functools.partial(
            layer_kernel, steps, plane, slot, groups, stacked, out_names, len(shared + list(after)), buffers
        ),
        out_shape=[jax.ShapeDtypeStruct(*shapes[name]) for name in out_names],
        in_specs=in_specs,
        out_specs=[any_spec] * len(out_names),
        input_output_aliases=aliases,
        scratch_shapes=scratch,
        compiler_params=pltpu.CompilerParams(vmem_limit_bytes=VMEM_BYTES),
        cost_estimate=pl.CostEstimate(
            flops=len(steps) * 2 * rows * width * (4 * width + 2 * hidden),
            bytes_accessed=40_000_000,
            transcendentals=0,
        ),
    )(*args)
    return dict(zip(out_names, outs))


LEFT = (N.normed_hidden, N.normed_ffn, N.normed_mix, N.normed_in)
RIGHT = (N.d_down, N.d_pre, N.d_branch, N.d_proj)


def chunk_rows(width, hidden, devices):
    chips = devices // 2
    return -(-(hidden // 2) // (chips * TILE)) * TILE


def block_row(block, width, hidden, half_rows):
    each = hidden // width // 2
    return (block // each) * half_rows + (block % each) * width


def weight_grad_kernel(*refs):
    parts = len(LEFT)
    sources, refs = refs[: 2 * parts], refs[2 * parts :]
    targets, scratch = refs[:2], refs[2:]
    left, right = scratch[0:parts], scratch[parts : 2 * parts]
    out_s = scratch[2 * parts : 2 * parts + 2]
    turned, in_sem, out_sem = scratch[2 * parts + 2 :]
    width = left[3].shape[1]
    wide = left[0].shape[1] // width
    loads = [
        pltpu.make_async_copy(source, target, in_sem.at[at])
        for at, (source, target) in enumerate(zip(sources, left + right))
    ]
    for part in range(parts):
        loads[part].start()
        loads[parts + part].start()
    starts = (0, 4, 3, 0)
    stores = []

    def store(which, first, count):
        at = pl.ds(first, count)
        stores.append(
            pltpu.make_async_copy(
                out_s[which].at[at], targets[which].at[at], out_sem.at[len(stores)]
            )
        )
        stores[-1].start()

    for part in range(parts):
        loads[part].wait()
        loads[parts + part].wait()
        first = starts[part] * width
        if part == 0:

            def one(block, carry):
                at = pl.ds(pl.multiple_of(block * width, width), width)
                turned[...] = left[part][:, at].T
                out_s[0][at, :] = dot_nn(turned[...], right[part][...]).astype(jnp.bfloat16)
                return carry

            lax.fori_loop(0, wide, one, 0)
            store(0, 0, out_s[0].shape[0])
        else:
            turned[...] = left[part][...].T
            blocks = right[part].shape[1] // width

            def one(block, carry):
                cols = pl.ds(pl.multiple_of(block * width, width), width)
                at = pl.ds(pl.multiple_of(first + block * width, width), width)
                out_s[1][at, :] = dot_nn(turned[...], right[part][:, cols]).astype(jnp.bfloat16)
                return carry

            lax.fori_loop(0, blocks, one, 0)
            store(1, first, blocks * width)
    for item in stores:
        item.wait()


def weight_grads(kept, grads):
    args = [kept[name] for name in LEFT] + [grads[name] for name in RIGHT]
    rows, width = kept[N.normed_in].shape
    hidden = kept[N.normed_hidden].shape[1]
    bf = jnp.bfloat16
    shapes = [(hidden, width), (4 * width + hidden, width)]
    any_spec = pl.BlockSpec(memory_space=pl.ANY)
    scratch = [pltpu.VMEM(item.shape, bf) for item in args]
    scratch += [pltpu.VMEM(shape, bf) for shape in shapes]
    scratch += [
        pltpu.VMEM((width, rows), bf),
        pltpu.SemaphoreType.DMA((len(args),)),
        pltpu.SemaphoreType.DMA((5,)),
    ]
    return pl.pallas_call(
        weight_grad_kernel,
        out_shape=[jax.ShapeDtypeStruct(shape, bf) for shape in shapes],
        in_specs=[any_spec] * len(args),
        out_specs=[any_spec] * 2,
        scratch_shapes=scratch,
        compiler_params=pltpu.CompilerParams(vmem_limit_bytes=VMEM_BYTES),
        cost_estimate=pl.CostEstimate(
            flops=2 * rows * width * (4 * width + 2 * hidden),
            bytes_accessed=30_000_000,
            transcendentals=0,
        ),
    )(*args)


def ring_places(chips):
    line_len = chips // 2
    pipe = lax.axis_index("pipe")
    batch = lax.axis_index("batch")
    core = batch % 2
    side = (batch // 2) % 2
    line = batch // 4
    place = line * (1 - side) + (chips - 1 - line) * side

    def chip_at(spot):
        far = spot // line_len
        along = spot * (1 - far) + (chips - 1 - spot) * far
        return (pipe, (along * 2 + far) * 2 + core)

    onward = chip_at((place + 1) % chips)
    backward = chip_at((place + chips - 1) % chips)
    twin = (pipe, batch + 1 - 2 * core)
    return place, core, onward, backward, twin


def greet(devices):
    barrier = pltpu.get_barrier_semaphore()
    for other in devices:
        pl.semaphore_signal(barrier, inc=1, device_id=other, device_id_type=MESH_IDS)
    return barrier


class Ring:
    def __init__(self, chips, lanes, places, parts, sum_ref, buffers, sems):
        self.chips, self.lanes, self.parts, self.sum_ref = chips, lanes, parts, sum_ref
        self.place, self.core, self.onward, self.backward, self.twin = places
        count = max(len(parts), 1)
        self.own, self.from_core = buffers[:count], buffers[count : 2 * count]
        self.arriving, self.final = buffers[2 * count :]
        self.held = self.own[0]
        (self.load_sem, self.core_send, self.core_recv, self.ring_send, self.ring_recv,
         self.spread_send, self.spread_recv, self.cross_send, self.cross_recv,
         self.store_sem) = sems

    def chunk_of(self, rank):
        half_up = (rank + 1) // 2
        sign = 1 - 2 * (rank % 2)
        return (self.place + self.chips + sign * half_up) % self.chips

    def load(self, rank, which):
        chunk = self.chunk_of(rank)
        return pltpu.make_async_copy(
            self.parts[which].at[self.core, chunk],
            self.own[which].at[chunk],
            self.load_sem.at[which, rank],
        )

    def remote(self, source, target, send_sem, recv_sem, device):
        return pltpu.make_async_remote_copy(
            src_ref=source,
            dst_ref=target,
            send_sem=send_sem,
            recv_sem=recv_sem,
            device_id=device,
            device_id_type=MESH_IDS,
        )

    def swap(self, rank, which):
        chunk = self.chunk_of(rank)
        return self.remote(
            self.parts[which].at[1 - self.core, chunk],
            self.from_core[which].at[chunk],
            self.core_send.at[which, rank],
            self.core_recv.at[which, rank],
            self.twin,
        )

    def start_loads(self):
        for rank in range(self.chips):
            for which in range(len(self.parts)):
                self.load(rank, which).start()

    def start_swaps(self):
        for rank in range(self.chips):
            for which in range(len(self.parts)):
                self.swap(rank, which).start()

    def add_rows(self, chunk, first, count, sources):
        def one(index, carry):
            rows = pl.ds(pl.multiple_of(first + index * TILE, TILE), TILE)
            total = self.held[chunk, rows, :].astype(jnp.float32)
            for source in sources:
                total = total + source[rows, :].astype(jnp.float32)
            self.held[chunk, rows, :] = total.astype(jnp.bfloat16)
            return carry

        lax.fori_loop(0, count // TILE, one, 0)

    def prepare(self, rank):
        chunk = self.chunk_of(rank)
        for which in range(len(self.parts)):
            self.load(rank, which).wait()
            self.swap(rank, which).wait_recv()
        sources = [item.at[chunk] for item in self.own[1:] + self.from_core]
        self.add_rows(chunk, 0, self.held.shape[1], sources)

    def neighbour(self, lane):
        return self.onward if self.lanes[lane][0] > 0 else self.backward

    def ring_chunk(self, lane, step):
        return (self.place + (self.chips - 1) * self.chips - self.lanes[lane][0] * step) % self.chips

    def ring_copy(self, lane, step):
        sign, first, count = self.lanes[lane]
        rows = pl.ds(first, count)
        return self.remote(
            self.held.at[self.ring_chunk(lane, step), rows],
            self.arriving.at[step, rows],
            self.ring_send.at[lane, step],
            self.ring_recv.at[lane, step],
            self.neighbour(lane),
        )

    def take(self, lane, step):
        sign, first, count = self.lanes[lane]
        self.ring_copy(lane, step - 1).wait_recv()
        chunk = self.ring_chunk(lane, step)
        self.add_rows(chunk, first, count, [self.arriving.at[step - 1]])

    def first(self):
        self.prepare(0)
        for lane in range(len(self.lanes)):
            self.ring_copy(lane, 0).start()

    def reduce_step(self, step):
        for rank in (2 * step - 1, 2 * step):

            @pl.when(rank < self.chips)
            def _():
                self.prepare(rank)

        for lane in range(len(self.lanes)):
            self.take(lane, step)
            self.ring_copy(lane, step).start()

    def spread_parts(self, lane, step):
        sign, first, count = self.lanes[lane]
        chunk = (self.place + (self.chips + 1) * self.chips + sign * (1 - step)) % self.chips
        return chunk, pl.ds(first, count)

    def spread_copy(self, lane, step, source):
        chunk, rows = self.spread_parts(lane, step)
        return self.remote(
            source.at[chunk, rows],
            self.final.at[chunk, rows],
            self.spread_send.at[lane, step],
            self.spread_recv.at[lane, step],
            self.neighbour(lane),
        )

    def cross_copy(self, lane, step, source):
        chunk, rows = self.spread_parts(lane, step)
        return self.remote(
            source.at[chunk, rows],
            self.sum_ref.at[self.core, chunk, rows],
            self.cross_send.at[lane, step],
            self.cross_recv.at[lane, step],
            self.twin,
        )

    def store_copy(self, lane, step, source):
        chunk, rows = self.spread_parts(lane, step)
        return pltpu.make_async_copy(
            source.at[chunk, rows],
            self.sum_ref.at[self.core, chunk, rows],
            self.store_sem.at[lane, step],
        )

    def turn(self):
        for lane in range(len(self.lanes)):
            self.take(lane, self.chips - 1)
            self.spread_copy(lane, 0, self.held).start()
            self.cross_copy(lane, 0, self.held).start()
            self.store_copy(lane, 0, self.held).start()

    def spread_step(self, step):
        for lane in range(len(self.lanes)):
            self.spread_copy(lane, step - 1, self.final).wait_recv()
            self.spread_copy(lane, step, self.final).start()
            self.cross_copy(lane, step, self.final).start()
            self.store_copy(lane, step, self.final).start()

    def last(self):
        for lane in range(len(self.lanes)):
            self.spread_copy(lane, self.chips - 2, self.final).wait_recv()
            self.cross_copy(lane, self.chips - 1, self.final).start()
            self.store_copy(lane, self.chips - 1, self.final).start()

    def run(self, begin, end):
        chips = self.chips

        def loop(low, high, step_of):
            def one(step, carry):
                step_of(step)
                return carry

            if low < high:
                lax.fori_loop(low, high, one, 0)

        loop(begin + 1, min(end, chips - 2) + 1, self.reduce_step)
        if begin <= chips - 2 < end:
            self.turn()
        loop(max(begin - chips + 2, 1), min(end - chips + 1, chips - 2) + 1, self.spread_step)
        if end == 2 * (chips - 1):
            self.last()

    def settle(self):
        def swaps(rank, carry):
            for which in range(len(self.parts)):
                self.swap(rank, which).wait_send()
            return carry

        def steps(step, carry):
            for lane in range(len(self.lanes)):
                self.ring_copy(lane, step).wait_send()
                self.spread_copy(lane, step, self.final).wait_send()
            return carry

        def outs(step, carry):
            for lane in range(len(self.lanes)):
                self.cross_copy(lane, step, self.final).wait()
                self.store_copy(lane, step, self.final).wait()
            return carry

        if self.parts:
            lax.fori_loop(0, self.chips, swaps, 0)
        lax.fori_loop(0, self.chips - 1, steps, 0)
        lax.fori_loop(0, self.chips, outs, 0)


def ring_plan(total_rows, columns, devices, count):
    chips = devices // 2
    chunk_rows = total_rows // devices
    tiles = chunk_rows // TILE
    shares = [tiles // 4 + (1 if spot < tiles % 4 else 0) for spot in range(4)]
    lanes = []
    first = 0
    for sign, share in zip((1, -1, 1, -1), shares):
        if share:
            lanes.append((sign, first * TILE, share * TILE))
        first += share
    block = (chips, chunk_rows, columns)
    dma = pltpu.SemaphoreType.DMA
    buffers = [pltpu.VMEM(block, jnp.bfloat16)] * (2 * count + 2)
    sems = [dma((count, chips))] * 3 + [dma((len(lanes), chips))] * 7
    return chips, tuple(lanes), block, buffers, sems


class VectorRing(Ring):
    def carry_vectors(self, held, from_twin, arriving, final, sum_ref, send, recv, store):
        my_rows = pl.ds(pl.multiple_of(self.core * TILE, TILE), TILE)
        twin_rows = pl.ds(pl.multiple_of((1 - self.core) * TILE, TILE), TILE)
        self.vectors, self.from_twin, self.vector_in, self.vector_sum = held, from_twin, arriving, final
        self.my_rows = my_rows

        def copy(at, source, target, device):
            return self.remote(source, target, send.at[at], recv.at[at], device)

        self.vector_swap = copy(0, held.at[twin_rows], from_twin, self.twin)
        self.vector_ring = copy(1, held.at[my_rows], arriving, self.onward)
        self.vector_spread = copy(2, final, final, self.onward)
        self.vector_cross = copy(3, final, sum_ref.at[my_rows], self.twin)
        self.vector_out = pltpu.make_async_copy(final, sum_ref.at[my_rows], store.at[0])

    def add_vectors(self, source):
        self.vectors[self.my_rows, :] = (
            self.vectors[self.my_rows, :].astype(jnp.float32) + source[...].astype(jnp.float32)
        ).astype(jnp.bfloat16)

    def first(self):
        super().first()
        self.vector_swap.wait_recv()
        self.add_vectors(self.from_twin)

        @pl.when(self.place == 0)
        def _():
            self.vector_ring.start()

    def reduce_step(self, step):
        super().reduce_step(step)

        @pl.when(self.place == step)
        def _():
            self.vector_ring.wait_recv()
            self.add_vectors(self.vector_in)
            self.vector_ring.start()

    def turn(self):
        @pl.when(self.place == self.chips - 1)
        def _():
            self.vector_ring.wait_recv()
            self.add_vectors(self.vector_in)
            self.vector_sum[...] = self.vectors[self.my_rows, :]
            self.vector_spread.start()
            self.vector_cross.start()
            self.vector_out.start()

        super().turn()

    def pass_vectors(self, step, last):
        @pl.when((self.place + 1) % self.chips == step)
        def _():
            self.vector_spread.wait_recv()
            if not last:
                self.vector_spread.start()
            self.vector_cross.start()
            self.vector_out.start()

    def spread_step(self, step):
        super().spread_step(step)
        self.pass_vectors(step, False)

    def last(self):
        super().last()
        self.pass_vectors(self.chips - 1, True)

    def settle(self):
        super().settle()
        self.vector_swap.wait_send()
        self.vector_cross.wait()
        self.vector_out.wait()

        @pl.when(self.place != self.chips - 1)
        def _():
            self.vector_ring.wait_send()

        @pl.when(self.place != self.chips - 2)
        def _():
            self.vector_spread.wait_send()


def ring_sum_kernel(chips, lanes, count, *refs):
    parts, vectors = refs[:count], refs[count : 2 * count]
    sum_ref, vector_ref = refs[2 * count : 2 * count + 2]
    refs = refs[2 * count + 2 :]
    buffers, refs = refs[: 2 * count + 2], refs[2 * count + 2 :]
    sems, refs = refs[:10], refs[10:]
    places = ring_places(chips)
    barrier = greet(places[2:])
    ring = VectorRing(chips, lanes, places, parts, sum_ref, buffers, sems)
    ring.carry_vectors(*refs[:4], vector_ref, *refs[4:])
    ring.start_loads()
    total = vectors[0][...]
    for item in vectors[1:]:
        total = total + item[...]
    refs[0][...] = total.astype(jnp.bfloat16)
    pl.semaphore_wait(barrier, 3)
    ring.start_swaps()
    ring.vector_swap.start()
    ring.first()
    ring.run(0, 2 * (chips - 1))
    ring.settle()


def ring_sum(parts, vectors, devices):
    total_rows, columns = parts[0].shape
    count = len(parts)
    chips, lanes, block, buffers, sems = ring_plan(total_rows, columns, devices, count)
    bf = jnp.bfloat16
    dma = pltpu.SemaphoreType.DMA
    any_spec = pl.BlockSpec(memory_space=pl.ANY)
    vmem_spec = pl.BlockSpec(memory_space=pltpu.VMEM)
    vector_shape = vectors[0].shape
    return pl.pallas_call(
        functools.partial(ring_sum_kernel, chips, lanes, count),
        out_shape=[
            jax.ShapeDtypeStruct((2,) + block, bf),
            jax.ShapeDtypeStruct(vector_shape, bf),
        ],
        in_specs=[any_spec] * count + [vmem_spec] * count,
        out_specs=[any_spec] * 2,
        scratch_shapes=buffers
        + sems
        + [pltpu.VMEM(vector_shape, bf)]
        + [pltpu.VMEM((TILE, columns), bf)] * 3
        + [dma((4,)), dma((4,)), dma((1,))],
        compiler_params=pltpu.CompilerParams(
            collective_id=1, has_side_effects=True, vmem_limit_bytes=VMEM_BYTES
        ),
    )(*[item.reshape((2,) + block) for item in parts], *vectors)


BACK_GROUPS = ((N.dy, N.wd, N.normed_hidden), (N.spread, N.slope, N.wu, N.residual),
               (N.wo, N.attended, N.projected, N.log_total), (N.wq, N.x))
REST_LEFT = (N.normed_ffn, N.normed_mix, N.normed_in)
REST_RIGHT = (N.d_down, N.d_pre, N.d_branch, N.d_proj)
TICKS = 14


def tail_kernel(chips, lanes, slot, buffers, lengths_ref, assign_ref, *refs):
    back_names = sum(BACK_GROUPS, ())
    sources = dict(zip(back_names, refs))
    sources[N.x] = sources[N.x].at[slot]
    refs = refs[len(back_names) :]
    vectors, refs = refs[:4], refs[4:]
    rest_names = REST_LEFT + REST_RIGHT + (N.sums,)
    rest_sources, refs = dict(zip(rest_names, refs)), refs[len(rest_names) :]
    base_sums, down_base, rest_base, refs = refs[0], refs[1], refs[2], refs[4:]
    dx_out, sum_refs, vector_out, refs = refs[0], refs[1:4], refs[4], refs[5:]
    held = dict(zip(buffers, refs))
    refs = refs[len(buffers) :]
    pools, refs = refs[:2], refs[2:]
    ring_buffers, refs = (refs[:4], refs[4:8]), refs[8:]
    stage, turned, refs = refs[0], refs[1], refs[2:]
    vector_buffers, refs = refs[:4], refs[4:]
    ring_sems, refs = (refs[:10], refs[10:20], refs[20:30]), refs[30:]
    vector_sems, refs = refs[:3], refs[3:]
    back_sem, rest_sem, base_sem, dx_sem, free_sem = refs
    rows, width = held[N.dy].shape
    hidden = held[N.wide_scratch].shape[1]
    wide = hidden // width
    half_blocks = wide // 2
    each = width // stage.shape[2]
    spent, scratch = held[N.normed_hidden], held[N.wide_scratch]
    held[N.d_down] = held[N.dy]
    held[N.d_pre] = held[N.slope]
    held[N.d_proj] = held[N.projected]
    held[N.d_attended] = spent.at[:, 0:width]
    held[N.dx] = spent.at[:, width : 2 * width]
    held[N.d_branch] = spent.at[:, 2 * width : 3 * width]
    held[N.d_residual] = scratch.at[:, 0:width]
    held[N.bias_back] = scratch.at[:, width : width + rows]

    places = ring_places(chips)
    place, core, onward, backward, twin = places
    barrier = greet(places[2:])
    late_buffers = [pool.at[pl.ds(half * chips, chips)] for pool in pools for half in range(2)]
    first_ring = Ring(chips, lanes, places, (), sum_refs[0], ring_buffers[0], ring_sems[0])
    second_ring = Ring(chips, lanes, places, (), sum_refs[1], ring_buffers[1], ring_sems[1])
    third_ring = VectorRing(chips, lanes, places, (), sum_refs[2], late_buffers, ring_sems[2])
    third_ring.carry_vectors(*vector_buffers, vector_out, *vector_sems)
    on_lower = lax.axis_index("pipe") == 0

    def base_loads(ring, at, base_ref, first):
        own = first * each + core * half_blocks * each
        other = first * each + (1 - core) * half_blocks * each
        count = half_blocks * each
        copies = [
            pltpu.make_async_copy(
                base_ref.at[pl.ds(own, count)], ring.held.at[pl.ds(0, count)], base_sem.at[at, 0]
            )
        ]
        for block in range(half_blocks):
            copies.append(
                pltpu.make_async_copy(
                    base_ref.at[pl.ds(other + block * each, each)],
                    stage.at[block],
                    base_sem.at[at, 1 + block],
                )
            )
        return copies

    def block_swap(ring, block):
        return ring.remote(
            stage.at[block],
            ring.from_core[0].at[pl.ds(block * each, each)],
            ring.core_send.at[0, block],
            ring.core_recv.at[0, block],
            twin,
        )

    def add_block(ring, index, right):
        half, block = index // half_blocks, index % half_blocks
        chunks = slice(block * each, (block + 1) * each)
        product = dot_nn(turned[...], right).reshape((each,) + stage.shape[2:])

        @pl.when(core == half)
        def _():
            total = ring.held[chunks].astype(jnp.float32) + product
            ring.held[chunks] = total.astype(jnp.bfloat16)

        @pl.when(core != half)
        def _():
            total = stage[block].astype(jnp.float32) + product
            stage[block] = total.astype(jnp.bfloat16)
            block_swap(ring, block).start()

    def begin(ring):
        for block in range(half_blocks):
            block_swap(ring, block).wait_recv()
        ring.first()

    loads = {}
    for at, name in enumerate(back_names):
        copies = [(sources[name], held.get(name))]
        if name == N.wd:
            copies = [(sources[name], pools[0].at[pl.ds(0, wide * each)])]
        if name == N.wu:
            copies = []
            for block in range(wide):
                cols = pl.ds(block * width, width)
                target = pools[1].at[pl.ds(block * each, each)]
                copies.append((sources[name].at[:, :, cols], target))
        loads[name] = [
            pltpu.make_async_copy(source, target, back_sem.at[at, piece])
            for piece, (source, target) in enumerate(copies)
        ]
    rest_loads = {
        name: pltpu.make_async_copy(rest_sources[name], held[name], rest_sem.at[at])
        for at, name in enumerate(rest_names)
    }
    first_base = base_loads(first_ring, 0, down_base, 0)
    second_base = base_loads(second_ring, 1, rest_base, 4)
    third_base = base_loads(third_ring, 2, rest_base, 0)
    incoming, features = loads[N.dy][0], loads[N.normed_hidden][0]

    @pl.when(on_lower)
    def _():
        incoming.start()
        features.start()

    @pl.when(jnp.logical_not(on_lower))
    def _():
        pltpu.make_async_copy(rest_sources[N.d_down], held[N.dy], back_sem.at[0, 0]).start()
        features.start()

    for item in first_base:
        item.start()

    @pl.when(on_lower)
    def _():
        for name in back_names:
            if name not in (N.dy, N.normed_hidden):
                for item in loads[name]:
                    item.start()

    @pl.when(jnp.logical_not(on_lower))
    def _():
        for name in (N.d_pre, N.d_proj, N.sums):
            rest_loads[name].start()

    for name in REST_LEFT:
        rest_loads[name].start()
    second_base[0].start()

    def refill_stage(before, base):
        for block in range(half_blocks):
            for half in range(2):

                @pl.when(core != half)
                def _():
                    block_swap(before, block).wait_send()

            base[1 + block].start()

    pl.semaphore_wait(barrier, 3)
    incoming.wait()
    features.wait()
    for item in first_base:
        item.wait()
    for block in range(wide):
        cols = slice(block * width, (block + 1) * width)
        turned[...] = held[N.normed_hidden][:, cols].T
        add_block(first_ring, block, held[N.dy][...])
    begin(first_ring)

    steps = 2 * (chips - 1)
    rings = (first_ring, second_ring, third_ring)

    def tick(which, done):
        at = done[which]
        if at < TICKS:
            rings[which].run(at * steps // TICKS, (at + 1) * steps // TICKS)
            done[which] += 1

    def up_grads(done):
        rest_loads[N.normed_ffn].wait()
        turned[...] = held[N.normed_ffn][...].T
        for item in second_base:
            item.wait()
        for block in range(wide):
            cols = slice(block * width, (block + 1) * width)
            add_block(second_ring, block, held[N.d_pre][:, cols])
            if block == half_blocks - 1:
                tick(0, done)
        tick(0, done)
        begin(second_ring)

    def free_pools():
        for other in (onward, backward, twin):
            pl.semaphore_signal(free_sem, inc=1, device_id=other, device_id_type=MESH_IDS)

    order = (0, 1, 0, 1, 0, 1)
    start = [0, 0, 0]

    @pl.when(on_lower)
    def _():
        waited = {N.dy, N.normed_hidden}
        done = list(start)
        count = []

        def ready(name):
            for group in BACK_GROUPS:
                if name in group and name not in waited:
                    for item in group:
                        if item not in waited:
                            for piece in loads[item]:
                                piece.wait()
                    waited.update(group)

        def emit(name):
            if name == N.dx:
                pltpu.make_async_copy(held[N.dx], dx_out, dx_sem.at[0]).start()

        def one_tick():
            if len(count) == 0:
                refill_stage(first_ring, second_base)
                tick(0, done)
            else:
                if len(count) == 1:
                    free_pools()
                tick(order[len(count) - 1], done)
            count.append(0)

        def middle():
            tick(0, done)
            up_grads(done)

        length = slot_length(lengths_ref, assign_ref, slot)
        backward_body(
            held, vectors, length, False, ready, emit, one_tick, pools=pools, middle=middle
        )
        tick(order[-1], done)

    @pl.when(jnp.logical_not(on_lower))
    def _():
        done = list(start)
        free_pools()
        refill_stage(first_ring, second_base)
        rest_loads[N.d_branch].start()
        for name in (N.d_pre, N.d_proj, N.sums, N.d_branch):
            rest_loads[name].wait()
        tick(0, done)
        tick(0, done)
        up_grads(done)
        for which in order:
            tick(which, done)

    done = [4 + order.count(0), order.count(1), 0]
    for name in REST_LEFT[1:]:
        rest_loads[name].wait()
    vector_buffers[0][...] = (base_sums[...] + held[N.sums][...]).astype(jnp.bfloat16)

    pl.semaphore_wait(free_sem, 3)
    third_ring.vector_swap.start()
    third_base[0].start()
    refill_stage(second_ring, third_base)
    turned[...] = held[N.normed_in][...].T
    for item in third_base:
        item.wait()
    for block in range(4):
        if block == 3:
            turned[...] = held[N.normed_mix][...].T
        right = held[N.d_branch][...] if block == 3 else None
        if right is None:
            right = held[N.d_proj][:, block * width : (block + 1) * width]
        add_block(third_ring, block, right)
        if block % 2:
            tick(0, done)
            tick(1, done)
    begin(third_ring)
    left = [
        ((at + 1) / (TICKS - done[which]), which)
        for which in range(3)
        for at in range(TICKS - done[which])
    ]
    for share, which in sorted(left):
        tick(which, done)
    for ring in rings:
        ring.settle()
    for block in range(half_blocks):
        block_swap(third_ring, block).wait_send()

    @pl.when(on_lower)
    def _():
        pltpu.make_async_copy(held[N.dx], dx_out, dx_sem.at[0]).wait()


def tail_call(slot, sizes, given, vectors, kept, grads, base_sums, bases, devices):
    rows, width = given[N.dy].shape
    hidden = given[N.wu].shape[1]
    wide = hidden // width
    shapes = buffer_shapes(rows, width, hidden)
    chunk = chunk_rows(width, hidden, devices)
    chips, lanes, block, ring_buffers, ring_sems = ring_plan(chunk * devices, width, devices, 1)
    back_names = sum(BACK_GROUPS, ())
    rest_names = REST_LEFT + REST_RIGHT + (N.sums,)
    given = dict(given)
    given[N.wd] = given[N.wd].reshape(hidden // chunk, chunk, width)
    given[N.wu] = given[N.wu].reshape(width // chunk, chunk, hidden)
    buffers = tuple(name for name in back_names if name not in (N.wd, N.wu)) + REST_LEFT
    buffers += (N.sums, N.wide_scratch, N.delta)
    any_spec = pl.BlockSpec(memory_space=pl.ANY)
    vmem_spec = pl.BlockSpec(memory_space=pltpu.VMEM)
    smem_spec = pl.BlockSpec(memory_space=pltpu.SMEM)
    bf = jnp.bfloat16
    args = list(sizes) + [given[name] for name in back_names] + list(vectors)
    args += [kept[name] for name in REST_LEFT] + [grads[name] for name in REST_RIGHT + (N.sums,)]
    args += [base_sums] + [item.reshape(-1, chunk, width) for item in bases] + [grads[N.dx]]
    in_specs = [smem_spec] * 2 + [any_spec] * len(back_names) + [vmem_spec] * 4
    in_specs += [any_spec] * len(rest_names) + [vmem_spec] + [any_spec] * 3
    sum_shape = jax.ShapeDtypeStruct((2,) + block, bf)
    out_shape = [jax.ShapeDtypeStruct((rows, width), bf)] + [sum_shape] * 3
    out_shape.append(jax.ShapeDtypeStruct((SUM_ROWS, width), bf))
    dma = pltpu.SemaphoreType.DMA
    pool = pltpu.VMEM((2 * chips,) + block[1:], bf)
    return pl.pallas_call(
        functools.partial(tail_kernel, chips, lanes, slot, buffers),
        out_shape=out_shape,
        in_specs=in_specs,
        out_specs=[any_spec] * len(out_shape),
        input_output_aliases={len(args) - 1: 0},
        scratch_shapes=[pltpu.VMEM(*shapes[name]) for name in buffers]
        + [pool] * 2
        + ring_buffers * 2
        + [pltpu.VMEM((wide // 2, width // chunk, chunk, width), bf), pltpu.VMEM((width, rows), bf)]
        + [pltpu.VMEM((SUM_ROWS, width), bf)]
        + [pltpu.VMEM((TILE, width), bf)] * 3
        + ring_sems * 3
        + [dma((4,)), dma((4,)), dma((1,))]
        + [dma((len(back_names), wide)), dma((len(rest_names),)), dma((3, 1 + wide // 2)), dma((1,))]
        + [pltpu.SemaphoreType.REGULAR],
        compiler_params=pltpu.CompilerParams(
            collective_id=0, has_side_effects=True, vmem_limit_bytes=TAIL_VMEM_BYTES
        ),
    )(*args)


def finish_kernel(steps, count, down_hbm, up_hbm, rest_hbm, vectors, *refs):
    moved, refs = refs[: 2 * count], refs[2 * count :]
    outs, refs = refs[:4], refs[4:]
    gains, shifts, hidden_gains, hidden_shifts = refs[:4]
    stacked, refs = refs[4:6], refs[6:]
    narrow, broad, passing, in_sem, out_sem, arrive_sem, leave_sem = refs
    width = rest_hbm.shape[1]
    arrivals, departures = [], []
    for at, source in enumerate(moved):
        target = stacked[at // count].at[at % count]
        arrivals.append(pltpu.make_async_copy(source, passing.at[at], arrive_sem.at[at]))
        departures.append(pltpu.make_async_copy(passing.at[at], target, leave_sem.at[at]))

    def load(step):
        which, first, row, column = steps[step]
        source = (rest_hbm, rest_hbm, up_hbm, down_hbm)[which].at[pl.ds(first, width)]
        return pltpu.make_async_copy(source, narrow.at[step % DEPTH], in_sem.at[step % DEPTH])

    def store(step):
        which, first, row, column = steps[step]
        target = outs[which].at[pl.ds(row, width), pl.ds(column, width)]
        return pltpu.make_async_copy(broad.at[step % DEPTH], target, out_sem.at[step % DEPTH])

    for step in range(DEPTH):
        load(step).start()
    for item in arrivals:
        item.start()
    values = vectors[...].astype(jnp.float32)
    for row in range(3):
        gains[row] = values[row : row + 1]
    for row in range(7):
        shifts[row] = values[3 + row : 4 + row]
    wide = hidden_gains.shape[1] // width
    for block in range(wide):
        cols = slice(block * width, (block + 1) * width)
        hidden_gains[:, cols] = values[10 + block : 11 + block]
        for row in range(2):
            first = 10 + (row + 1) * wide + block
            hidden_shifts[row : row + 1, cols] = values[first : first + 1]
    for step in range(len(steps)):
        load(step).wait()
        if step >= DEPTH:
            store(step - DEPTH).wait()
        broad[step % DEPTH] = narrow[step % DEPTH].astype(jnp.float32)
        store(step).start()
        if step + DEPTH < len(steps):
            load(step + DEPTH).start()
        if step == DEPTH:
            for arrival, departure in zip(arrivals, departures):
                arrival.wait()
                departure.start()
    for step in range(len(steps) - DEPTH, len(steps)):
        store(step).wait()
    for item in departures:
        item.wait()


def finish(down, up, rest, vectors, slots_out, slots_grad, hidden):
    width = rest.shape[1]
    wide = hidden // width
    count = len(slots_out)
    half_rows = down.shape[0] // 2
    firsts = [block_row(block, width, hidden, half_rows) for block in range(wide)]
    steps = [(3, firsts[block], block * width, 0) for block in range(wide)]
    steps += [(2, firsts[block], 0, block * width) for block in range(wide)]
    steps += [(0, firsts[block], 0, block * width) for block in range(3)]
    steps.append((1, firsts[3], 0, 0))
    f = jnp.float32
    shapes = [(width, 3 * width), (width, width), (width, hidden), (hidden, width)]
    shapes += [(3, 1, width), (7, 1, width), (1, hidden), (2, hidden)]
    any_spec = pl.BlockSpec(memory_space=pl.ANY)
    vmem_spec = pl.BlockSpec(memory_space=pltpu.VMEM)
    out_shape = [jax.ShapeDtypeStruct(shape, f) for shape in shapes]
    pile = jax.ShapeDtypeStruct((count,) + slots_out[0].shape, slots_out[0].dtype)
    return pl.pallas_call(
        functools.partial(finish_kernel, tuple(steps), count),
        out_shape=out_shape + [pile, pile],
        in_specs=[any_spec] * 3 + [vmem_spec] + [any_spec] * (2 * count),
        out_specs=[any_spec] * 4 + [vmem_spec] * 4 + [any_spec] * 2,
        scratch_shapes=[
            pltpu.VMEM((DEPTH, width, width), jnp.bfloat16),
            pltpu.VMEM((DEPTH, width, width), f),
            pltpu.VMEM((2 * count,) + slots_out[0].shape, slots_out[0].dtype),
            pltpu.SemaphoreType.DMA((DEPTH,)),
            pltpu.SemaphoreType.DMA((DEPTH,)),
            pltpu.SemaphoreType.DMA((2 * count,)),
            pltpu.SemaphoreType.DMA((2 * count,)),
        ],
        compiler_params=pltpu.CompilerParams(vmem_limit_bytes=VMEM_BYTES),
    )(down, up, rest, vectors, *slots_out, *slots_grad)


def passed_along(block, axis, distance):
    devices = range(lax.axis_size(axis))
    route = [(i - distance, i) for i in devices if i - distance in devices]
    return lax.ppermute(block, axis, route)


def shards(
    inputs,
    cotangent,
    lengths,
    assign,
    query_key_value,
    out_weight,
    up_weight,
    down_weight,
    model_gains,
    model_shifts,
    hidden_gains,
    hidden_shifts,
):
    micro_count = inputs.shape[0]
    hidden = up_weight.shape[2]
    slots = range(micro_count)
    weights = {
        N.wq: query_key_value[0],
        N.wo: out_weight[0],
        N.wu: up_weight[0],
        N.wd: down_weight[0],
    }
    by_row = [jnp.transpose(item, (1, 0, 2)) for item in (model_gains, model_shifts)]
    vectors = (*by_row, hidden_gains, hidden_shifts)

    sizes = (lengths, assign)

    def run(steps, plane, slot, given, previous, after=()):
        return layer_call(
            steps, plane, slot, sizes, {**weights, **given}, vectors, previous, after
        )

    lower, upper = [], []
    for slot in slots:
        after = [lower[-1][N.spread]] if lower else []
        lower.append(run((N.forward,), 0, slot, {N.x: inputs}, {}, after))
    middle = [passed_along(lower[slot][N.y], "pipe", 1) for slot in slots]
    for slot in slots:
        after = [upper[-1][N.sums]] if upper else []
        given = {N.x: middle[slot], N.dy: cotangent}
        upper.append(run((N.forward, N.backward), 1, slot, given, lower[slot], after))
    returned = [passed_along(upper[slot][N.dx], "pipe", -1) for slot in slots]
    kept = [{**lower[slot], **upper[slot]} for slot in slots]
    devices = lax.axis_size("batch")
    first, final = slots
    given = {**kept[first], N.x: inputs, N.dy: returned[first]}
    first_grads = run((N.backward,), 0, first, given, kept[first])
    base_down, base_rest = weight_grads(kept[first], first_grads)
    width = inputs.shape[2]
    half_rows = chunk_rows(width, hidden, devices) * (devices // 2)
    given = {**kept[final], N.x: inputs, N.dy: returned[final]}
    if 2 * half_rows == hidden:
        dx, *sums, vector_sum = tail_call(
            final,
            sizes,
            {**weights, **given},
            vectors,
            kept[final],
            upper[final],
            first_grads[N.sums],
            (base_down, base_rest),
            devices,
        )
    else:
        final_grads = run((N.backward,), 0, final, given, kept[final])
        dx = final_grads[N.dx]
        last_down, last_rest = weight_grads(kept[final], final_grads)
        parts = []
        for pair in ((base_down, base_rest), (last_down, last_rest)):
            packed = jnp.concatenate(pair, axis=0)
            missing = -packed.shape[0] % (TILE * devices)
            parts.append(jnp.pad(packed, ((0, missing), (0, 0))))
        packed, vector_sum = ring_sum(parts, [first_grads[N.sums], final_grads[N.sums]], devices)
        packed = packed.reshape(-1, width)
        ends = (hidden, hidden + 4 * width, 2 * hidden + 4 * width)
        sums = (packed[: ends[0]], packed[ends[1] : ends[2]], packed[ends[0] : ends[1]])
    outs = finish(
        *[item.reshape(-1, width) for item in sums],
        vector_sum,
        [kept[slot][N.y] for slot in slots],
        [first_grads[N.dx], dx],
        hidden,
    )
    by_row = [jnp.transpose(item, (1, 0, 2)) for item in outs[4:6]]
    return (*[item[None] for item in outs[8:] + outs[:4]], *by_row, outs[6], outs[7][None])


def solution(mesh):
    return jax.shard_map(
        shards,
        mesh=mesh,
        in_specs=(
            P(None, "batch", None),
            P(None, "batch", None),
            P("batch"),
            P("batch"),
            P("pipe", None, None),
            P("pipe", None, None),
            P("pipe", None, None),
            P("pipe", None, None),
            P("pipe", None, None),
            P("pipe", None, None),
            P("pipe", None),
            P("pipe", None, None),
        ),
        out_specs=(
            P("pipe", None, "batch", None),
            P("pipe", None, "batch", None),
            P("pipe", None, None),
            P("pipe", None, None),
            P("pipe", None, None),
            P("pipe", None, None),
            P("pipe", None, None),
            P("pipe", None, None),
            P("pipe", None),
            P("pipe", None, None),
        ),
        check_vma=False,
    )
```

```python
import functools
import types

import jax
import jax.numpy as jnp
from jax import lax
from jax.experimental import pallas as pl
from jax.experimental.pallas import tpu as pltpu
from jax.sharding import PartitionSpec as P

HEAD = 64
PAIR = 2 * HEAD
EPSILON = 1e-05
SCALE = 0.125
HIDDEN_NEG = -1e30
CHUNK = 512
SUM_ROWS = 32
DEPTH = 3
HEAD_ROWS = 16

TILE = 16
VMEM_BYTES = 60 * 1024 * 1024
TAIL_VMEM_BYTES = 63 * 1024 * 1024
MESH_IDS = pl.DeviceIdType.MESH


def named(**given):
    return types.SimpleNamespace(**{name: name for name in given})


N = named(
    x=0,
    dy=0,
    y=0,
    dx=0,
    wq=0,
    wo=0,
    wu=0,
    wd=0,
    normed_in=0,
    projected=0,
    log_total=0,
    attended=0,
    normed_mix=0,
    residual=0,
    normed_ffn=0,
    normed_hidden=0,
    slope=0,
    spread=0,
    d_down=0,
    d_pre=0,
    d_branch=0,
    d_proj=0,
    sums=0,
    wide_scratch=0,
    d_residual=0,
    d_attended=0,
    delta=0,
    bias=0,
    bias_back=0,
    forward=0,
    backward=0,
)


def dot_nn(left, right):
    return jnp.dot(left, right, preferred_element_type=jnp.float32)


def dot_nt(left, right):
    return lax.dot_general(
        left, right, (((1,), (1,)), ((), ())), preferred_element_type=jnp.float32
    )


def standardize(values_in):
    centred = values_in - jnp.mean(values_in, axis=-1, keepdims=True)
    scale = lax.rsqrt(jnp.mean(centred * centred, axis=-1, keepdims=True) + EPSILON)
    return centred * scale, scale


def unit_backward(grad, unit, scale, gain):
    scaled = grad * gain
    first = jnp.mean(scaled, axis=-1, keepdims=True)
    second = jnp.mean(scaled * unit, axis=-1, keepdims=True)
    return (
        scale * (scaled - first - unit * second),
        jnp.sum(grad * unit, axis=0, keepdims=True),
        jnp.sum(grad, axis=0, keepdims=True),
    )


def column_sum(values):
    return jnp.sum(values.astype(jnp.float32), axis=0, keepdims=True)


def hiding_bias(rows, length, query_dim):
    query = lax.broadcasted_iota(jnp.int32, (rows, rows), query_dim)
    key = lax.broadcasted_iota(jnp.int32, (rows, rows), 1 - query_dim)
    visible = (key <= query) & ((key < length) | (key == query))
    return jnp.where(visible, 0.0, HIDDEN_NEG)


def own_lanes(values, which):
    lane = lax.broadcasted_iota(jnp.int32, values.shape, 1)
    mine = (lane >= HEAD) if which else (lane < HEAD)
    return jnp.where(mine, values, jnp.zeros_like(values))


def attend_forward(projected, attended, log_total, bias):
    rows, width = attended.shape
    half = rows // 2
    lane = lax.broadcasted_iota(jnp.int32, (half, PAIR), 1)

    def one_pair(pair, totals):
        first = pl.multiple_of(pair * PAIR, PAIR)
        items = []
        for block in range(2):
            at = slice(block * half, (block + 1) * half)
            reach = (block + 1) * half
            q = projected[at, pl.ds(first, PAIR)] * jnp.bfloat16(SCALE)
            k = projected[0:reach, pl.ds(width + first, PAIR)]
            v = projected[0:reach, pl.ds(2 * width + first, PAIR)]
            items += [(at, reach, own_lanes(q, which), k, v) for which in range(2)]
        scores = [dot_nt(q, k) + bias[at, 0:reach] for at, reach, q, k, v in items]
        softened = []
        for item in scores:
            top = jnp.max(item, axis=-1, keepdims=True)
            exps = jnp.exp(item - top)
            softened.append((exps, jnp.sum(exps, axis=-1, keepdims=True), top))
        mixed = [
            dot_nn(exps.astype(jnp.bfloat16), item[4]) * (1.0 / total)
            for item, (exps, total, top) in zip(items, softened)
        ]
        new_totals = []
        for block in range(2):
            at = items[2 * block][0]
            attended[at, pl.ds(first, PAIR)] = jnp.where(
                lane < HEAD, mixed[2 * block], mixed[2 * block + 1]
            )
            logs = totals[block]
            for which in range(2):
                exps, total, top = softened[2 * block + which]
                logs = jnp.where(lane == 2 * pair + which, top + jnp.log(total), logs)
            new_totals.append(logs)
        return tuple(new_totals)

    zero = jnp.zeros((half, PAIR), jnp.float32)
    totals = lax.fori_loop(0, width // PAIR, one_pair, (zero, zero), unroll=2)
    for block in range(2):
        log_total[:, block * half : (block + 1) * half] = totals[block].T[0:HEAD_ROWS]


def attend_backward(projected, d_attended, log_total, delta, bias, d_proj, tick):
    rows, width = d_attended.shape
    half = rows // 2

    def one_pair(pair, carry):
        first = pl.multiple_of(pair * PAIR, PAIR)
        k_all = projected[:, pl.ds(width + first, PAIR)]
        v_all = projected[:, pl.ds(2 * width + first, PAIR)]
        k_turned = k_all.T
        items = []
        for block in range(2):
            at = slice(block * half, (block + 1) * half)
            q = projected[at, pl.ds(first, PAIR)] * jnp.bfloat16(SCALE)
            grad = d_attended[at, pl.ds(first, PAIR)]
            for which in range(2):
                items.append((block, which, at, own_lanes(q, which), own_lanes(grad, which)))
        raw = []
        for block, which, at, q, grad in items:
            reach = (block + 1) * half
            raw.append((dot_nt(k_all[0:reach], q), dot_nt(v_all[0:reach], grad)))
        shaped = []
        for (block, which, at, q, grad), (scores, d_probs) in zip(items, raw):
            reach = (block + 1) * half
            head = pl.ds(2 * pair + which, 1)
            probs = jnp.exp(scores + bias[0:reach, at] - log_total[head, at])
            d_scores = (probs * (d_probs - delta[head, at])).astype(jnp.bfloat16)
            shaped.append((probs.astype(jnp.bfloat16), d_scores))
        dk = [None, None]
        dv = [None, None]
        dq = []
        for (block, which, at, q, grad), (probs, d_scores) in zip(items, shaped):
            reach = (block + 1) * half
            more_v = dot_nn(probs, grad)
            more_k = dot_nn(d_scores, q)
            dq.append(dot_nn(k_turned[which * HEAD : (which + 1) * HEAD, 0:reach], d_scores))
            for part in range(block + 1):
                piece = slice(part * half, (part + 1) * half)
                dv[part] = more_v[piece] if dv[part] is None else dv[part] + more_v[piece]
                dk[part] = more_k[piece] if dk[part] is None else dk[part] + more_k[piece]
        for block in range(2):
            at = slice(block * half, (block + 1) * half)
            turned = jnp.concatenate(dq[2 * block : 2 * block + 2], axis=0) * SCALE
            d_proj[at, pl.ds(first, PAIR)] = turned.T.astype(jnp.bfloat16)
            d_proj[at, pl.ds(width + first, PAIR)] = dk[block].astype(jnp.bfloat16)
            d_proj[at, pl.ds(2 * width + first, PAIR)] = dv[block].astype(jnp.bfloat16)
        return carry

    if tick is None:
        lax.fori_loop(0, width // PAIR, one_pair, 0, unroll=2)
    else:
        for first in range(0, width // PAIR, 2):
            lax.fori_loop(first, min(first + 2, width // PAIR), one_pair, 0, unroll=True)
            tick()


KEPT = (N.normed_in, N.projected, N.log_total, N.attended, N.normed_mix, N.residual,
        N.normed_ffn, N.normed_hidden, N.slope, N.spread)
GRADS = (N.d_down, N.d_pre, N.d_branch, N.d_proj, N.sums)


def buffer_shapes(rows, width, hidden):
    bf, f = jnp.bfloat16, jnp.float32
    return {
        N.x: ((rows, width), bf),
        N.dy: ((rows, width), bf),
        N.y: ((rows, width), bf),
        N.dx: ((rows, width), bf),
        N.wq: ((width, 3 * width), bf),
        N.wo: ((width, width), bf),
        N.wu: ((width, hidden), bf),
        N.wd: ((hidden, width), bf),
        N.normed_in: ((rows, width), bf),
        N.projected: ((rows, 3 * width), bf),
        N.log_total: ((HEAD_ROWS, rows), f),
        N.attended: ((rows, width), f),
        N.normed_mix: ((rows, width), bf),
        N.residual: ((rows, width), f),
        N.normed_ffn: ((rows, width), bf),
        N.normed_hidden: ((rows, hidden), bf),
        N.slope: ((rows, hidden), bf),
        N.spread: ((rows, PAIR), f),
        N.d_down: ((rows, width), bf),
        N.d_pre: ((rows, hidden), bf),
        N.d_branch: ((rows, width), bf),
        N.d_proj: ((rows, 3 * width), bf),
        N.sums: ((SUM_ROWS, width), f),
        N.wide_scratch: ((rows, hidden), f),
        N.d_residual: ((rows, width), f),
        N.d_attended: ((rows, width), bf),
        N.delta: ((HEAD_ROWS, rows), f),
        N.bias: ((rows, rows), f),
        N.bias_back: ((rows, rows), f),
    }


def forward_body(held, vectors, length, ready, emit):
    gm, sm, gh, sh = vectors
    sh = sh.at[0]
    bf = jnp.bfloat16
    rows, width = held[N.x].shape
    hidden = held[N.wu].shape[1]
    wide_scratch = held[N.wide_scratch]
    held[N.bias][...] = hiding_bias(rows, length, 0)
    ready(N.x)
    unit, unused = standardize(held[N.x][...].astype(jnp.float32))
    held[N.normed_in][...] = (unit * gm[0] + sm[0]).astype(bf)
    emit(N.normed_in)
    for block in range(3):
        cols = slice(block * width, (block + 1) * width)
        ready(N.wq)
        out = dot_nn(held[N.normed_in][...], held[N.wq][:, cols])
        if block != 1:
            out = out + sm[1 + block // 2]
        held[N.projected][:, cols] = out.astype(bf)
    emit(N.projected)
    attend_forward(held[N.projected], held[N.attended], held[N.log_total], held[N.bias])
    emit(N.log_total)
    emit(N.attended)

    unit, unused = standardize(held[N.attended][...])
    held[N.normed_mix][...] = (unit * gm[1] + sm[3]).astype(bf)
    emit(N.normed_mix)
    ready(N.wo)
    residual = held[N.x][...].astype(jnp.float32) + sm[4]
    residual = residual + dot_nn(held[N.normed_mix][...], held[N.wo][...])
    held[N.residual][...] = residual
    emit(N.residual)
    unit, unused = standardize(residual)
    held[N.normed_ffn][...] = (unit * gm[2] + sm[5]).astype(bf)
    emit(N.normed_ffn)
    ready(N.wu)
    total = jnp.zeros((rows, 1), jnp.float32)
    for first in range(0, hidden, CHUNK):
        cols = slice(first, first + CHUNK)
        pre = dot_nn(held[N.normed_ffn][...], held[N.wu][:, cols]) + sh[0:1, cols]
        share = 0.5 + 0.5 * lax.erf(pre * 0.7071067811865476)
        density = 0.3989422804014327 * jnp.exp(-0.5 * pre * pre)
        act = pre * share
        held[N.slope][:, cols] = (share + pre * density).astype(bf)
        wide_scratch[:, cols] = act
        total = total + jnp.sum(act, axis=-1, keepdims=True)
    emit(N.slope)
    mean = total * (1.0 / hidden)
    square = jnp.zeros((rows, 1), jnp.float32)
    for first in range(0, hidden, CHUNK):
        centred = wide_scratch[:, first : first + CHUNK] - mean
        square = square + jnp.sum(centred * centred, axis=-1, keepdims=True)
    scale = lax.rsqrt(square * (1.0 / hidden) + EPSILON)
    held[N.spread][...] = jnp.broadcast_to(scale, (rows, PAIR))
    emit(N.spread)
    for first in range(0, hidden, CHUNK):
        cols = slice(first, first + CHUNK)
        unit = (wide_scratch[:, cols] - mean) * scale
        held[N.normed_hidden][:, cols] = (unit * gh[0:1, cols] + sh[1:2, cols]).astype(bf)
    emit(N.normed_hidden)
    ready(N.wd)
    out = held[N.residual][...] + dot_nn(held[N.normed_hidden][...], held[N.wd][...])
    held[N.y][...] = (out + sm[6]).astype(bf)
    emit(N.y)


def pool_block(pool, block, width):
    each = width // pool.shape[1]
    return pool[block * each : (block + 1) * each].reshape(width, width)


def backward_body(held, vectors, length, masked, ready, emit, tick=None, pools=None, middle=None):
    gm, sm, gh, sh = vectors
    sh = sh.at[0]
    bf = jnp.bfloat16
    rows, width = held[N.x].shape
    hidden = held[N.wide_scratch].shape[1]
    wide = hidden // width
    wide_scratch, sums = held[N.wide_scratch], held[N.sums]
    sums[...] = jnp.zeros_like(sums)
    if pools is None:
        held[N.bias_back][...] = hiding_bias(rows, length, 1)
    ready(N.dy)
    d_down = held[N.dy][...]
    if masked:
        live = lax.broadcasted_iota(jnp.int32, (rows, 1), 0) < length
        d_down = jnp.where(live, d_down.astype(jnp.float32), 0.0).astype(bf)
    if tick is None:
        held[N.d_down][...] = d_down
    emit(N.d_down)
    sums[9:10, :] = column_sum(d_down)

    first_total = jnp.zeros((rows, 1), jnp.float32)
    second_total = jnp.zeros((rows, 1), jnp.float32)
    for block in range(wide):
        cols = slice(block * width, (block + 1) * width)
        ready(N.wd)
        ready(N.normed_hidden)
        weight = held[N.wd][cols, :] if pools is None else pool_block(pools[0], block, width)
        grad = dot_nt(held[N.d_down][...], weight)
        normed = held[N.normed_hidden][:, cols].astype(jnp.float32)
        unit = (normed - sh[1:2, cols]) * (1.0 / gh[0:1, cols])
        sums[10 + block : 11 + block, :] = jnp.sum(grad * unit, axis=0, keepdims=True)
        sums[18 + block : 19 + block, :] = jnp.sum(grad, axis=0, keepdims=True)
        scaled = grad * gh[0:1, cols]
        wide_scratch[:, cols] = scaled
        first_total = first_total + jnp.sum(scaled, axis=-1, keepdims=True)
        second_total = second_total + jnp.sum(scaled * unit, axis=-1, keepdims=True)
        if tick is not None and block == wide // 2 - 1:
            tick()
    first_mean = first_total * (1.0 / hidden)
    second_mean = second_total * (1.0 / hidden)
    ready(N.spread)
    ready(N.slope)
    scale = held[N.spread][:, 0:1]
    for block in range(wide):
        cols = slice(block * width, (block + 1) * width)
        normed = held[N.normed_hidden][:, cols].astype(jnp.float32)
        unit = (normed - sh[1:2, cols]) * (1.0 / gh[0:1, cols])
        d_act = scale * (wide_scratch[:, cols] - first_mean - unit * second_mean)
        d_pre = (d_act * held[N.slope][:, cols].astype(jnp.float32)).astype(bf)
        held[N.d_pre][:, cols] = d_pre
        sums[14 + block : 15 + block, :] = column_sum(d_pre)
    emit(N.d_pre)
    if middle is not None:
        middle()

    ready(N.wu)
    if pools is None:
        d_ffn = dot_nt(held[N.d_pre][...], held[N.wu][...])
    else:
        d_ffn = jnp.zeros((rows, width), jnp.float32)
        for block in range(wide):
            cols = slice(block * width, (block + 1) * width)
            d_ffn = d_ffn + dot_nt(held[N.d_pre][:, cols], pool_block(pools[1], block, width))
    ready(N.residual)
    unit, scale = standardize(held[N.residual][...])
    through, gain_sum, shift_sum = unit_backward(d_ffn, unit, scale, gm[2])
    sums[2:3, :] = gain_sum
    sums[8:9, :] = shift_sum
    through = through + held[N.d_down][...].astype(jnp.float32)
    held[N.d_residual][...] = through
    held[N.d_branch][...] = through.astype(bf)
    emit(N.d_branch)
    sums[7:8, :] = column_sum(held[N.d_branch][...])
    if tick is not None:
        tick()

    ready(N.wo)
    d_mix = dot_nt(held[N.d_branch][...], held[N.wo][...])
    ready(N.attended)
    attended = held[N.attended][...]
    unit, scale = standardize(attended)
    through, gain_sum, shift_sum = unit_backward(d_mix, unit, scale, gm[1])
    sums[1:2, :] = gain_sum
    sums[6:7, :] = shift_sum
    held[N.d_attended][...] = through.astype(bf)
    product = held[N.d_attended][...].astype(jnp.float32) * attended
    upper = product.astype(bf)
    lower = (product - upper.astype(jnp.float32)).astype(bf)
    head_row = lax.broadcasted_iota(jnp.int32, (HEAD_ROWS, width), 0)
    head_col = lax.broadcasted_iota(jnp.int32, (HEAD_ROWS, width), 1) // HEAD
    chooser = jnp.where(head_row == head_col, 1.0, 0.0).astype(bf)
    held[N.delta][...] = dot_nt(chooser, upper) + dot_nt(chooser, lower)
    if tick is not None:
        tick()

    ready(N.projected)
    ready(N.log_total)
    if pools is not None:
        held[N.bias_back][...] = hiding_bias(rows, length, 1)
    attend_backward(
        held[N.projected], held[N.d_attended], held[N.log_total], held[N.delta],
        held[N.bias_back], held[N.d_proj], tick,
    )
    emit(N.d_proj)
    ready(N.wq)
    d_norm = dot_nt(held[N.d_proj][...], held[N.wq][...])
    sums[4:5, :] = column_sum(held[N.d_proj][:, 0:width])
    sums[5:6, :] = column_sum(held[N.d_proj][:, 2 * width :])
    ready(N.x)
    unit, scale = standardize(held[N.x][...].astype(jnp.float32))
    through, gain_sum, shift_sum = unit_backward(d_norm, unit, scale, gm[0])
    sums[0:1, :] = gain_sum
    sums[3:4, :] = shift_sum
    held[N.dx][...] = (through + held[N.d_residual][...]).astype(bf)
    emit(N.dx)
    emit(N.sums)


def slot_length(lengths_ref, assign_ref, slot):
    total = jnp.int32(0)
    for at in range(lengths_ref.shape[0]):
        total = total + jnp.where(assign_ref[at] == slot, lengths_ref[at], 0)
    return total


def layer_kernel(
    steps, plane, slot, groups, stacked, out_names, unread, buffers, lengths_ref, assign_ref, *refs
):
    in_names = sum(groups, ())
    sources = dict(zip(in_names, refs))
    for name in stacked:
        sources[name] = sources[name].at[slot]
    vectors = refs[len(in_names) : len(in_names) + 4]
    refs = refs[len(in_names) + 4 + unread :]
    targets = dict(zip(out_names, refs))
    refs = refs[len(out_names) :]
    held = dict(zip(buffers, refs))
    in_sem, out_sem = refs[len(buffers) :]

    @pl.when(lax.axis_index("pipe") == plane)
    def _():
        loads = {
            name: pltpu.make_async_copy(sources[name], held[name], in_sem.at[at])
            for at, name in enumerate(in_names)
        }
        stores = {
            name: pltpu.make_async_copy(held[name], targets[name], out_sem.at[at])
            for at, name in enumerate(out_names)
        }
        for name in in_names:
            loads[name].start()
        waited = set()

        def ready(name):
            for group in groups:
                if name in group and name not in waited:
                    waited.update(group)
                    for item in group:
                        loads[item].wait()

        def emit(name):
            if name in stores:
                stores[name].start()

        length = slot_length(lengths_ref, assign_ref, slot)
        if N.forward in steps:
            forward_body(held, vectors, length, ready, emit)
        if N.backward in steps:
            backward_body(held, vectors, length, N.forward in steps, ready, emit)
        for name in out_names:
            stores[name].wait()


FORWARD_ONLY = (N.projected, N.log_total, N.attended, N.residual, N.slope, N.spread)


def layer_call(steps, plane, slot, sizes, given, vectors, previous, after=()):
    stacked = tuple(name for name in (N.x, N.dy) if name in given and given[name].ndim == 3)
    rows, width = given[N.x].shape[-2:]
    hidden = given[N.wu].shape[1]
    shapes = buffer_shapes(rows, width, hidden)
    if steps == (N.forward,):
        groups = ((N.x, N.wq), (N.wo, N.wu, N.wd))
        out_names = (N.y,) + KEPT
        spare = (N.wide_scratch, N.bias)
    elif steps == (N.backward,):
        groups = ((N.dy, N.wd, N.normed_hidden), (N.spread, N.slope, N.wu, N.residual),
                  (N.wo, N.attended, N.projected, N.log_total), (N.wq, N.x))
        out_names = (N.dx,) + GRADS
        spare = (N.wide_scratch, N.bias_back, N.d_residual, N.d_attended, N.delta)
    else:
        groups = ((N.x, N.wq), (N.wo, N.wu), (N.wd, N.dy))
        out_names = (N.y,) + tuple(name for name in KEPT if name not in FORWARD_ONLY)
        out_names += (N.dx,) + GRADS
        spare = (N.wide_scratch, N.bias, N.bias_back, N.d_residual, N.d_attended, N.delta)
        spare += FORWARD_ONLY
    in_names = sum(groups, ())
    buffers = in_names + tuple(name for name in out_names if name not in in_names) + spare
    any_spec = pl.BlockSpec(memory_space=pl.ANY)
    vmem_spec = pl.BlockSpec(memory_space=pltpu.VMEM)
    smem_spec = pl.BlockSpec(memory_space=pltpu.SMEM)
    in_specs = [smem_spec] * 2 + [any_spec] * len(in_names) + [vmem_spec] * 4
    args = list(sizes) + [given[name] for name in in_names] + list(vectors)
    shared = [name for name in out_names if name in previous]
    aliases = {len(args) + at: out_names.index(name) for at, name in enumerate(shared)}
    in_specs += [any_spec] * len(shared)
    args += [previous[name] for name in shared]
    in_specs += [any_spec] * len(after)
    args += list(after)
    scratch = [pltpu.VMEM(*shapes[name]) for name in buffers]
    scratch.append(pltpu.SemaphoreType.DMA((len(in_names),)))
    scratch.append(pltpu.SemaphoreType.DMA((len(out_names),)))
    outs = pl.pallas_call(
        functools.partial(
            layer_kernel, steps, plane, slot, groups, stacked, out_names, len(shared + list(after)), buffers
        ),
        out_shape=[jax.ShapeDtypeStruct(*shapes[name]) for name in out_names],
        in_specs=in_specs,
        out_specs=[any_spec] * len(out_names),
        input_output_aliases=aliases,
        scratch_shapes=scratch,
        compiler_params=pltpu.CompilerParams(vmem_limit_bytes=VMEM_BYTES),
        cost_estimate=pl.CostEstimate(
            flops=len(steps) * 2 * rows * width * (4 * width + 2 * hidden),
            bytes_accessed=40_000_000,
            transcendentals=0,
        ),
    )(*args)
    return dict(zip(out_names, outs))


LEFT = (N.normed_hidden, N.normed_ffn, N.normed_mix, N.normed_in)
RIGHT = (N.d_down, N.d_pre, N.d_branch, N.d_proj)


def chunk_rows(width, hidden, devices):
    chips = devices // 2
    return -(-(hidden // 2) // (chips * TILE)) * TILE


def block_row(block, width, hidden, half_rows):
    each = hidden // width // 2
    return (block // each) * half_rows + (block % each) * width


def weight_grad_kernel(*refs):
    parts = len(LEFT)
    sources, refs = refs[: 2 * parts], refs[2 * parts :]
    targets, scratch = refs[:2], refs[2:]
    left, right = scratch[0:parts], scratch[parts : 2 * parts]
    out_s = scratch[2 * parts : 2 * parts + 2]
    turned, in_sem, out_sem = scratch[2 * parts + 2 :]
    width = left[3].shape[1]
    wide = left[0].shape[1] // width
    loads = [
        pltpu.make_async_copy(source, target, in_sem.at[at])
        for at, (source, target) in enumerate(zip(sources, left + right))
    ]
    for part in range(parts):
        loads[part].start()
        loads[parts + part].start()
    starts = (0, 4, 3, 0)
    stores = []

    def store(which, first, count):
        at = pl.ds(first, count)
        stores.append(
            pltpu.make_async_copy(
                out_s[which].at[at], targets[which].at[at], out_sem.at[len(stores)]
            )
        )
        stores[-1].start()

    for part in range(parts):
        loads[part].wait()
        loads[parts + part].wait()
        first = starts[part] * width
        if part == 0:

            def one(block, carry):
                at = pl.ds(pl.multiple_of(block * width, width), width)
                turned[...] = left[part][:, at].T
                out_s[0][at, :] = dot_nn(turned[...], right[part][...]).astype(jnp.bfloat16)
                return carry

            lax.fori_loop(0, wide, one, 0)
            store(0, 0, out_s[0].shape[0])
        else:
            turned[...] = left[part][...].T
            blocks = right[part].shape[1] // width

            def one(block, carry):
                cols = pl.ds(pl.multiple_of(block * width, width), width)
                at = pl.ds(pl.multiple_of(first + block * width, width), width)
                out_s[1][at, :] = dot_nn(turned[...], right[part][:, cols]).astype(jnp.bfloat16)
                return carry

            lax.fori_loop(0, blocks, one, 0)
            store(1, first, blocks * width)
    for item in stores:
        item.wait()


def weight_grads(kept, grads):
    args = [kept[name] for name in LEFT] + [grads[name] for name in RIGHT]
    rows, width = kept[N.normed_in].shape
    hidden = kept[N.normed_hidden].shape[1]
    bf = jnp.bfloat16
    shapes = [(hidden, width), (4 * width + hidden, width)]
    any_spec = pl.BlockSpec(memory_space=pl.ANY)
    scratch = [pltpu.VMEM(item.shape, bf) for item in args]
    scratch += [pltpu.VMEM(shape, bf) for shape in shapes]
    scratch += [
        pltpu.VMEM((width, rows), bf),
        pltpu.SemaphoreType.DMA((len(args),)),
        pltpu.SemaphoreType.DMA((5,)),
    ]
    return pl.pallas_call(
        weight_grad_kernel,
        out_shape=[jax.ShapeDtypeStruct(shape, bf) for shape in shapes],
        in_specs=[any_spec] * len(args),
        out_specs=[any_spec] * 2,
        scratch_shapes=scratch,
        compiler_params=pltpu.CompilerParams(vmem_limit_bytes=VMEM_BYTES),
        cost_estimate=pl.CostEstimate(
            flops=2 * rows * width * (4 * width + 2 * hidden),
            bytes_accessed=30_000_000,
            transcendentals=0,
        ),
    )(*args)


def ring_places(chips):
    line_len = chips // 2
    pipe = lax.axis_index("pipe")
    batch = lax.axis_index("batch")
    core = batch % 2
    side = (batch // 2) % 2
    line = batch // 4
    place = line * (1 - side) + (chips - 1 - line) * side

    def chip_at(spot):
        far = spot // line_len
        along = spot * (1 - far) + (chips - 1 - spot) * far
        return (pipe, (along * 2 + far) * 2 + core)

    onward = chip_at((place + 1) % chips)
    backward = chip_at((place + chips - 1) % chips)
    twin = (pipe, batch + 1 - 2 * core)
    return place, core, onward, backward, twin


def greet(devices):
    barrier = pltpu.get_barrier_semaphore()
    for other in devices:
        pl.semaphore_signal(barrier, inc=1, device_id=other, device_id_type=MESH_IDS)
    return barrier


class Ring:
    def __init__(self, chips, lanes, places, parts, sum_ref, buffers, sems):
        self.chips, self.lanes, self.parts, self.sum_ref = chips, lanes, parts, sum_ref
        self.place, self.core, self.onward, self.backward, self.twin = places
        count = max(len(parts), 1)
        self.own, self.from_core = buffers[:count], buffers[count : 2 * count]
        self.arriving, self.final = buffers[2 * count :]
        self.held = self.own[0]
        (self.load_sem, self.core_send, self.core_recv, self.ring_send, self.ring_recv,
         self.spread_send, self.spread_recv, self.cross_send, self.cross_recv,
         self.store_sem) = sems

    def chunk_of(self, rank):
        half_up = (rank + 1) // 2
        sign = 1 - 2 * (rank % 2)
        return (self.place + self.chips + sign * half_up) % self.chips

    def load(self, rank, which):
        chunk = self.chunk_of(rank)
        return pltpu.make_async_copy(
            self.parts[which].at[self.core, chunk],
            self.own[which].at[chunk],
            self.load_sem.at[which, rank],
        )

    def remote(self, source, target, send_sem, recv_sem, device):
        return pltpu.make_async_remote_copy(
            src_ref=source,
            dst_ref=target,
            send_sem=send_sem,
            recv_sem=recv_sem,
            device_id=device,
            device_id_type=MESH_IDS,
        )

    def swap(self, rank, which):
        chunk = self.chunk_of(rank)
        return self.remote(
            self.parts[which].at[1 - self.core, chunk],
            self.from_core[which].at[chunk],
            self.core_send.at[which, rank],
            self.core_recv.at[which, rank],
            self.twin,
        )

    def start_loads(self):
        for rank in range(self.chips):
            for which in range(len(self.parts)):
                self.load(rank, which).start()

    def start_swaps(self):
        for rank in range(self.chips):
            for which in range(len(self.parts)):
                self.swap(rank, which).start()

    def add_rows(self, chunk, first, count, sources):
        def one(index, carry):
            rows = pl.ds(pl.multiple_of(first + index * TILE, TILE), TILE)
            total = self.held[chunk, rows, :].astype(jnp.float32)
            for source in sources:
                total = total + source[rows, :].astype(jnp.float32)
            self.held[chunk, rows, :] = total.astype(jnp.bfloat16)
            return carry

        lax.fori_loop(0, count // TILE, one, 0)

    def prepare(self, rank):
        chunk = self.chunk_of(rank)
        for which in range(len(self.parts)):
            self.load(rank, which).wait()
            self.swap(rank, which).wait_recv()
        sources = [item.at[chunk] for item in self.own[1:] + self.from_core]
        self.add_rows(chunk, 0, self.held.shape[1], sources)

    def neighbour(self, lane):
        return self.onward if self.lanes[lane][0] > 0 else self.backward

    def ring_chunk(self, lane, step):
        return (self.place + (self.chips - 1) * self.chips - self.lanes[lane][0] * step) % self.chips

    def ring_copy(self, lane, step):
        sign, first, count = self.lanes[lane]
        rows = pl.ds(first, count)
        return self.remote(
            self.held.at[self.ring_chunk(lane, step), rows],
            self.arriving.at[step, rows],
            self.ring_send.at[lane, step],
            self.ring_recv.at[lane, step],
            self.neighbour(lane),
        )

    def take(self, lane, step):
        sign, first, count = self.lanes[lane]
        self.ring_copy(lane, step - 1).wait_recv()
        chunk = self.ring_chunk(lane, step)
        self.add_rows(chunk, first, count, [self.arriving.at[step - 1]])

    def first(self):
        self.prepare(0)
        for lane in range(len(self.lanes)):
            self.ring_copy(lane, 0).start()

    def reduce_step(self, step):
        for rank in (2 * step - 1, 2 * step):

            @pl.when(rank < self.chips)
            def _():
                self.prepare(rank)

        for lane in range(len(self.lanes)):
            self.take(lane, step)
            self.ring_copy(lane, step).start()

    def spread_parts(self, lane, step):
        sign, first, count = self.lanes[lane]
        chunk = (self.place + (self.chips + 1) * self.chips + sign * (1 - step)) % self.chips
        return chunk, pl.ds(first, count)

    def spread_copy(self, lane, step, source):
        chunk, rows = self.spread_parts(lane, step)
        return self.remote(
            source.at[chunk, rows],
            self.final.at[chunk, rows],
            self.spread_send.at[lane, step],
            self.spread_recv.at[lane, step],
            self.neighbour(lane),
        )

    def cross_copy(self, lane, step, source):
        chunk, rows = self.spread_parts(lane, step)
        return self.remote(
            source.at[chunk, rows],
            self.sum_ref.at[self.core, chunk, rows],
            self.cross_send.at[lane, step],
            self.cross_recv.at[lane, step],
            self.twin,
        )

    def store_copy(self, lane, step, source):
        chunk, rows = self.spread_parts(lane, step)
        return pltpu.make_async_copy(
            source.at[chunk, rows],
            self.sum_ref.at[self.core, chunk, rows],
            self.store_sem.at[lane, step],
        )

    def turn(self):
        for lane in range(len(self.lanes)):
            self.take(lane, self.chips - 1)
            self.spread_copy(lane, 0, self.held).start()
            self.cross_copy(lane, 0, self.held).start()
            self.store_copy(lane, 0, self.held).start()

    def spread_step(self, step):
        for lane in range(len(self.lanes)):
            self.spread_copy(lane, step - 1, self.final).wait_recv()
            self.spread_copy(lane, step, self.final).start()
            self.cross_copy(lane, step, self.final).start()
            self.store_copy(lane, step, self.final).start()

    def last(self):
        for lane in range(len(self.lanes)):
            self.spread_copy(lane, self.chips - 2, self.final).wait_recv()
            self.cross_copy(lane, self.chips - 1, self.final).start()
            self.store_copy(lane, self.chips - 1, self.final).start()

    def run(self, begin, end):
        chips = self.chips

        def loop(low, high, step_of):
            def one(step, carry):
                step_of(step)
                return carry

            if low < high:
                lax.fori_loop(low, high, one, 0)

        loop(begin + 1, min(end, chips - 2) + 1, self.reduce_step)
        if begin <= chips - 2 < end:
            self.turn()
        loop(max(begin - chips + 2, 1), min(end - chips + 1, chips - 2) + 1, self.spread_step)
        if end == 2 * (chips - 1):
            self.last()

    def settle(self):
        def swaps(rank, carry):
            for which in range(len(self.parts)):
                self.swap(rank, which).wait_send()
            return carry

        def steps(step, carry):
            for lane in range(len(self.lanes)):
                self.ring_copy(lane, step).wait_send()
                self.spread_copy(lane, step, self.final).wait_send()
            return carry

        def outs(step, carry):
            for lane in range(len(self.lanes)):
                self.cross_copy(lane, step, self.final).wait()
                self.store_copy(lane, step, self.final).wait()
            return carry

        if self.parts:
            lax.fori_loop(0, self.chips, swaps, 0)
        lax.fori_loop(0, self.chips - 1, steps, 0)
        lax.fori_loop(0, self.chips, outs, 0)


def ring_plan(total_rows, columns, devices, count):
    chips = devices // 2
    chunk_rows = total_rows // devices
    tiles = chunk_rows // TILE
    shares = [tiles // 4 + (1 if spot < tiles % 4 else 0) for spot in range(4)]
    lanes = []
    first = 0
    for sign, share in zip((1, -1, 1, -1), shares):
        if share:
            lanes.append((sign, first * TILE, share * TILE))
        first += share
    block = (chips, chunk_rows, columns)
    dma = pltpu.SemaphoreType.DMA
    buffers = [pltpu.VMEM(block, jnp.bfloat16)] * (2 * count + 2)
    sems = [dma((count, chips))] * 3 + [dma((len(lanes), chips))] * 7
    return chips, tuple(lanes), block, buffers, sems


class VectorRing(Ring):
    def carry_vectors(self, held, from_twin, arriving, final, sum_ref, send, recv, store):
        my_rows = pl.ds(pl.multiple_of(self.core * TILE, TILE), TILE)
        twin_rows = pl.ds(pl.multiple_of((1 - self.core) * TILE, TILE), TILE)
        self.vectors, self.from_twin, self.vector_in, self.vector_sum = held, from_twin, arriving, final
        self.my_rows = my_rows

        def copy(at, source, target, device):
            return self.remote(source, target, send.at[at], recv.at[at], device)

        self.vector_swap = copy(0, held.at[twin_rows], from_twin, self.twin)
        self.vector_ring = copy(1, held.at[my_rows], arriving, self.onward)
        self.vector_spread = copy(2, final, final, self.onward)
        self.vector_cross = copy(3, final, sum_ref.at[my_rows], self.twin)
        self.vector_out = pltpu.make_async_copy(final, sum_ref.at[my_rows], store.at[0])

    def add_vectors(self, source):
        self.vectors[self.my_rows, :] = (
            self.vectors[self.my_rows, :].astype(jnp.float32) + source[...].astype(jnp.float32)
        ).astype(jnp.bfloat16)

    def first(self):
        super().first()
        self.vector_swap.wait_recv()
        self.add_vectors(self.from_twin)

        @pl.when(self.place == 0)
        def _():
            self.vector_ring.start()

    def reduce_step(self, step):
        super().reduce_step(step)

        @pl.when(self.place == step)
        def _():
            self.vector_ring.wait_recv()
            self.add_vectors(self.vector_in)
            self.vector_ring.start()

    def turn(self):
        @pl.when(self.place == self.chips - 1)
        def _():
            self.vector_ring.wait_recv()
            self.add_vectors(self.vector_in)
            self.vector_sum[...] = self.vectors[self.my_rows, :]
            self.vector_spread.start()
            self.vector_cross.start()
            self.vector_out.start()

        super().turn()

    def pass_vectors(self, step, last):
        @pl.when((self.place + 1) % self.chips == step)
        def _():
            self.vector_spread.wait_recv()
            if not last:
                self.vector_spread.start()
            self.vector_cross.start()
            self.vector_out.start()

    def spread_step(self, step):
        super().spread_step(step)
        self.pass_vectors(step, False)

    def last(self):
        super().last()
        self.pass_vectors(self.chips - 1, True)

    def settle(self):
        super().settle()
        self.vector_swap.wait_send()
        self.vector_cross.wait()
        self.vector_out.wait()

        @pl.when(self.place != self.chips - 1)
        def _():
            self.vector_ring.wait_send()

        @pl.when(self.place != self.chips - 2)
        def _():
            self.vector_spread.wait_send()


def ring_sum_kernel(chips, lanes, count, *refs):
    parts, vectors = refs[:count], refs[count : 2 * count]
    sum_ref, vector_ref = refs[2 * count : 2 * count + 2]
    refs = refs[2 * count + 2 :]
    buffers, refs = refs[: 2 * count + 2], refs[2 * count + 2 :]
    sems, refs = refs[:10], refs[10:]
    places = ring_places(chips)
    barrier = greet(places[2:])
    ring = VectorRing(chips, lanes, places, parts, sum_ref, buffers, sems)
    ring.carry_vectors(*refs[:4], vector_ref, *refs[4:])
    ring.start_loads()
    total = vectors[0][...]
    for item in vectors[1:]:
        total = total + item[...]
    refs[0][...] = total.astype(jnp.bfloat16)
    pl.semaphore_wait(barrier, 3)
    ring.start_swaps()
    ring.vector_swap.start()
    ring.first()
    ring.run(0, 2 * (chips - 1))
    ring.settle()


def ring_sum(parts, vectors, devices):
    total_rows, columns = parts[0].shape
    count = len(parts)
    chips, lanes, block, buffers, sems = ring_plan(total_rows, columns, devices, count)
    bf = jnp.bfloat16
    dma = pltpu.SemaphoreType.DMA
    any_spec = pl.BlockSpec(memory_space=pl.ANY)
    vmem_spec = pl.BlockSpec(memory_space=pltpu.VMEM)
    vector_shape = vectors[0].shape
    return pl.pallas_call(
        functools.partial(ring_sum_kernel, chips, lanes, count),
        out_shape=[
            jax.ShapeDtypeStruct((2,) + block, bf),
            jax.ShapeDtypeStruct(vector_shape, bf),
        ],
        in_specs=[any_spec] * count + [vmem_spec] * count,
        out_specs=[any_spec] * 2,
        scratch_shapes=buffers
        + sems
        + [pltpu.VMEM(vector_shape, bf)]
        + [pltpu.VMEM((TILE, columns), bf)] * 3
        + [dma((4,)), dma((4,)), dma((1,))],
        compiler_params=pltpu.CompilerParams(
            collective_id=1, has_side_effects=True, vmem_limit_bytes=VMEM_BYTES
        ),
    )(*[item.reshape((2,) + block) for item in parts], *vectors)


BACK_GROUPS = ((N.dy, N.wd, N.normed_hidden), (N.spread, N.slope, N.wu, N.residual),
               (N.wo, N.attended, N.projected, N.log_total), (N.wq, N.x))
REST_LEFT = (N.normed_ffn, N.normed_mix, N.normed_in)
REST_RIGHT = (N.d_down, N.d_pre, N.d_branch, N.d_proj)
TICKS = 14


def tail_kernel(chips, lanes, slot, buffers, lengths_ref, assign_ref, *refs):
    back_names = sum(BACK_GROUPS, ())
    sources = dict(zip(back_names, refs))
    sources[N.x] = sources[N.x].at[slot]
    refs = refs[len(back_names) :]
    vectors, refs = refs[:4], refs[4:]
    rest_names = REST_LEFT + REST_RIGHT + (N.sums,)
    rest_sources, refs = dict(zip(rest_names, refs)), refs[len(rest_names) :]
    base_sums, down_base, rest_base, refs = refs[0], refs[1], refs[2], refs[4:]
    dx_out, sum_refs, vector_out, refs = refs[0], refs[1:4], refs[4], refs[5:]
    held = dict(zip(buffers, refs))
    refs = refs[len(buffers) :]
    pools, refs = refs[:2], refs[2:]
    ring_buffers, refs = (refs[:4], refs[4:8]), refs[8:]
    stage, turned, refs = refs[0], refs[1], refs[2:]
    vector_buffers, refs = refs[:4], refs[4:]
    ring_sems, refs = (refs[:10], refs[10:20], refs[20:30]), refs[30:]
    vector_sems, refs = refs[:3], refs[3:]
    back_sem, rest_sem, base_sem, dx_sem, free_sem = refs
    rows, width = held[N.dy].shape
    hidden = held[N.wide_scratch].shape[1]
    wide = hidden // width
    half_blocks = wide // 2
    each = width // stage.shape[2]
    spent, scratch = held[N.normed_hidden], held[N.wide_scratch]
    held[N.d_down] = held[N.dy]
    held[N.d_pre] = held[N.slope]
    held[N.d_proj] = held[N.projected]
    held[N.d_attended] = spent.at[:, 0:width]
    held[N.dx] = spent.at[:, width : 2 * width]
    held[N.d_branch] = spent.at[:, 2 * width : 3 * width]
    held[N.d_residual] = scratch.at[:, 0:width]
    held[N.bias_back] = scratch.at[:, width : width + rows]

    places = ring_places(chips)
    place, core, onward, backward, twin = places
    barrier = greet(places[2:])
    late_buffers = [pool.at[pl.ds(half * chips, chips)] for pool in pools for half in range(2)]
    first_ring = Ring(chips, lanes, places, (), sum_refs[0], ring_buffers[0], ring_sems[0])
    second_ring = Ring(chips, lanes, places, (), sum_refs[1], ring_buffers[1], ring_sems[1])
    third_ring = VectorRing(chips, lanes, places, (), sum_refs[2], late_buffers, ring_sems[2])
    third_ring.carry_vectors(*vector_buffers, vector_out, *vector_sems)
    on_lower = lax.axis_index("pipe") == 0

    def base_loads(ring, at, base_ref, first):
        own = first * each + core * half_blocks * each
        other = first * each + (1 - core) * half_blocks * each
        count = half_blocks * each
        copies = [
            pltpu.make_async_copy(
                base_ref.at[pl.ds(own, count)], ring.held.at[pl.ds(0, count)], base_sem.at[at, 0]
            )
        ]
        for block in range(half_blocks):
            copies.append(
                pltpu.make_async_copy(
                    base_ref.at[pl.ds(other + block * each, each)],
                    stage.at[block],
                    base_sem.at[at, 1 + block],
                )
            )
        return copies

    def block_swap(ring, block):
        return ring.remote(
            stage.at[block],
            ring.from_core[0].at[pl.ds(block * each, each)],
            ring.core_send.at[0, block],
            ring.core_recv.at[0, block],
            twin,
        )

    def add_block(ring, index, right):
        half, block = index // half_blocks, index % half_blocks
        chunks = slice(block * each, (block + 1) * each)
        product = dot_nn(turned[...], right).reshape((each,) + stage.shape[2:])

        @pl.when(core == half)
        def _():
            total = ring.held[chunks].astype(jnp.float32) + product
            ring.held[chunks] = total.astype(jnp.bfloat16)

        @pl.when(core != half)
        def _():
            total = stage[block].astype(jnp.float32) + product
            stage[block] = total.astype(jnp.bfloat16)
            block_swap(ring, block).start()

    def add_blocks(ring, product_of, between=None):
        for at in range(wide):
            block = at % half_blocks
            half = 1 - core if at < half_blocks else core
            first = pl.multiple_of((half * half_blocks + block) * width, width)
            product = product_of(pl.ds(first, width)).reshape((each,) + stage.shape[2:])
            if at < half_blocks:
                stage[block] = (stage[block].astype(jnp.float32) + product).astype(jnp.bfloat16)
                block_swap(ring, block).start()
            else:
                chunks = slice(block * each, (block + 1) * each)
                total = ring.held[chunks].astype(jnp.float32) + product
                ring.held[chunks] = total.astype(jnp.bfloat16)
            if at == half_blocks - 1 and between is not None:
                between()

    def begin(ring):
        for block in range(half_blocks):
            block_swap(ring, block).wait_recv()
        ring.first()

    loads = {}
    for at, name in enumerate(back_names):
        copies = [(sources[name], held.get(name))]
        if name == N.wd:
            copies = [(sources[name], pools[0].at[pl.ds(0, wide * each)])]
        if name == N.wu:
            copies = []
            for block in range(wide):
                cols = pl.ds(block * width, width)
                target = pools[1].at[pl.ds(block * each, each)]
                copies.append((sources[name].at[:, :, cols], target))
        loads[name] = [
            pltpu.make_async_copy(source, target, back_sem.at[at, piece])
            for piece, (source, target) in enumerate(copies)
        ]
    rest_loads = {
        name: pltpu.make_async_copy(rest_sources[name], held[name], rest_sem.at[at])
        for at, name in enumerate(rest_names)
    }
    first_base = base_loads(first_ring, 0, down_base, 0)
    second_base = base_loads(second_ring, 1, rest_base, 4)
    third_base = base_loads(third_ring, 2, rest_base, 0)
    incoming, features = loads[N.dy][0], loads[N.normed_hidden][0]

    @pl.when(on_lower)
    def _():
        incoming.start()
        features.start()

    @pl.when(jnp.logical_not(on_lower))
    def _():
        pltpu.make_async_copy(rest_sources[N.d_down], held[N.dy], back_sem.at[0, 0]).start()
        features.start()

    for item in first_base:
        item.start()

    @pl.when(on_lower)
    def _():
        for name in back_names:
            if name not in (N.dy, N.normed_hidden):
                for item in loads[name]:
                    item.start()

    @pl.when(jnp.logical_not(on_lower))
    def _():
        for name in (N.d_pre, N.d_proj, N.sums):
            rest_loads[name].start()

    for name in REST_LEFT:
        rest_loads[name].start()
    second_base[0].start()

    def refill_stage(before, base):
        for block in range(half_blocks):
            block_swap(before, block).wait_send()
            base[1 + block].start()

    pl.semaphore_wait(barrier, 3)
    incoming.wait()
    features.wait()
    for item in first_base:
        item.wait()

    def down_product(cols):
        turned[...] = held[N.normed_hidden][:, cols].T
        return dot_nn(turned[...], held[N.dy][...])

    add_blocks(first_ring, down_product)
    begin(first_ring)

    steps = 2 * (chips - 1)
    rings = (first_ring, second_ring, third_ring)

    def tick(which, done):
        at = done[which]
        if at < TICKS:
            rings[which].run(at * steps // TICKS, (at + 1) * steps // TICKS)
            done[which] += 1

    def up_grads(done):
        rest_loads[N.normed_ffn].wait()
        turned[...] = held[N.normed_ffn][...].T
        for item in second_base:
            item.wait()
        add_blocks(
            second_ring,
            lambda cols: dot_nn(turned[...], held[N.d_pre][:, cols]),
            lambda: tick(0, done),
        )
        tick(0, done)
        begin(second_ring)

    def free_pools():
        for other in (onward, backward, twin):
            pl.semaphore_signal(free_sem, inc=1, device_id=other, device_id_type=MESH_IDS)

    def load_third():
        third_base[0].start()
        refill_stage(second_ring, third_base)

    order = (0, 1, 0, 1, 0, 1)
    start = [0, 0, 0]

    @pl.when(on_lower)
    def _():
        waited = {N.dy, N.normed_hidden}
        done = list(start)
        count = []

        def ready(name):
            for group in BACK_GROUPS:
                if name in group and name not in waited:
                    for item in group:
                        if item not in waited:
                            for piece in loads[item]:
                                piece.wait()
                    waited.update(group)

        def emit(name):
            if name == N.dx:
                pltpu.make_async_copy(held[N.dx], dx_out, dx_sem.at[0]).start()

        def one_tick():
            if len(count) == 0:
                refill_stage(first_ring, second_base)
                tick(0, done)
            else:
                if len(count) == 1:
                    free_pools()
                    load_third()
                tick(order[len(count) - 1], done)
            count.append(0)

        def middle():
            tick(0, done)
            up_grads(done)

        length = slot_length(lengths_ref, assign_ref, slot)
        backward_body(
            held, vectors, length, False, ready, emit, one_tick, pools=pools, middle=middle
        )
        tick(order[-1], done)

    @pl.when(jnp.logical_not(on_lower))
    def _():
        done = list(start)
        free_pools()
        refill_stage(first_ring, second_base)
        rest_loads[N.d_branch].start()
        for name in (N.d_pre, N.d_proj, N.sums, N.d_branch):
            rest_loads[name].wait()
        tick(0, done)
        tick(0, done)
        up_grads(done)
        load_third()
        for which in order:
            tick(which, done)

    done = [4 + order.count(0), order.count(1), 0]
    for name in REST_LEFT[1:]:
        rest_loads[name].wait()
    vector_buffers[0][...] = (base_sums[...] + held[N.sums][...]).astype(jnp.bfloat16)

    pl.semaphore_wait(free_sem, 3)
    third_ring.vector_swap.start()
    turned[...] = held[N.normed_in][...].T
    for item in third_base:
        item.wait()
    for block in range(4):
        if block == 3:
            turned[...] = held[N.normed_mix][...].T
        right = held[N.d_branch][...] if block == 3 else None
        if right is None:
            right = held[N.d_proj][:, block * width : (block + 1) * width]
        add_block(third_ring, block, right)
        if block % 2:
            tick(0, done)
            tick(1, done)
    begin(third_ring)
    left = [
        ((at + 1) / (TICKS - done[which]), which)
        for which in range(3)
        for at in range(TICKS - done[which])
    ]
    for share, which in sorted(left):
        tick(which, done)
    for ring in rings:
        ring.settle()
    for block in range(half_blocks):
        block_swap(third_ring, block).wait_send()

    @pl.when(on_lower)
    def _():
        pltpu.make_async_copy(held[N.dx], dx_out, dx_sem.at[0]).wait()


def tail_call(slot, sizes, given, vectors, kept, grads, base_sums, bases, devices):
    rows, width = given[N.dy].shape
    hidden = given[N.wu].shape[1]
    wide = hidden // width
    shapes = buffer_shapes(rows, width, hidden)
    chunk = chunk_rows(width, hidden, devices)
    chips, lanes, block, ring_buffers, ring_sems = ring_plan(chunk * devices, width, devices, 1)
    back_names = sum(BACK_GROUPS, ())
    rest_names = REST_LEFT + REST_RIGHT + (N.sums,)
    given = dict(given)
    given[N.wd] = given[N.wd].reshape(hidden // chunk, chunk, width)
    given[N.wu] = given[N.wu].reshape(width // chunk, chunk, hidden)
    buffers = tuple(name for name in back_names if name not in (N.wd, N.wu)) + REST_LEFT
    buffers += (N.sums, N.wide_scratch, N.delta)
    any_spec = pl.BlockSpec(memory_space=pl.ANY)
    vmem_spec = pl.BlockSpec(memory_space=pltpu.VMEM)
    smem_spec = pl.BlockSpec(memory_space=pltpu.SMEM)
    bf = jnp.bfloat16
    args = list(sizes) + [given[name] for name in back_names] + list(vectors)
    args += [kept[name] for name in REST_LEFT] + [grads[name] for name in REST_RIGHT + (N.sums,)]
    args += [base_sums] + [item.reshape(-1, chunk, width) for item in bases] + [grads[N.dx]]
    in_specs = [smem_spec] * 2 + [any_spec] * len(back_names) + [vmem_spec] * 4
    in_specs += [any_spec] * len(rest_names) + [vmem_spec] + [any_spec] * 3
    sum_shape = jax.ShapeDtypeStruct((2,) + block, bf)
    out_shape = [jax.ShapeDtypeStruct((rows, width), bf)] + [sum_shape] * 3
    out_shape.append(jax.ShapeDtypeStruct((SUM_ROWS, width), bf))
    dma = pltpu.SemaphoreType.DMA
    pool = pltpu.VMEM((2 * chips,) + block[1:], bf)
    return pl.pallas_call(
        functools.partial(tail_kernel, chips, lanes, slot, buffers),
        out_shape=out_shape,
        in_specs=in_specs,
        out_specs=[any_spec] * len(out_shape),
        input_output_aliases={len(args) - 1: 0},
        scratch_shapes=[pltpu.VMEM(*shapes[name]) for name in buffers]
        + [pool] * 2
        + ring_buffers * 2
        + [pltpu.VMEM((wide // 2, width // chunk, chunk, width), bf), pltpu.VMEM((width, rows), bf)]
        + [pltpu.VMEM((SUM_ROWS, width), bf)]
        + [pltpu.VMEM((TILE, width), bf)] * 3
        + ring_sems * 3
        + [dma((4,)), dma((4,)), dma((1,))]
        + [dma((len(back_names), wide)), dma((len(rest_names),)), dma((3, 1 + wide // 2)), dma((1,))]
        + [pltpu.SemaphoreType.REGULAR],
        compiler_params=pltpu.CompilerParams(
            collective_id=0, has_side_effects=True, vmem_limit_bytes=TAIL_VMEM_BYTES
        ),
    )(*args)


def finish_kernel(steps, count, down_hbm, up_hbm, rest_hbm, vectors, *refs):
    moved, refs = refs[: 2 * count], refs[2 * count :]
    outs, refs = refs[:4], refs[4:]
    gains, shifts, hidden_gains, hidden_shifts = refs[:4]
    stacked, refs = refs[4:6], refs[6:]
    narrow, broad, passing, in_sem, out_sem, arrive_sem, leave_sem = refs
    width = rest_hbm.shape[1]
    arrivals, departures = [], []
    for at, source in enumerate(moved):
        target = stacked[at // count].at[at % count]
        arrivals.append(pltpu.make_async_copy(source, passing.at[at], arrive_sem.at[at]))
        departures.append(pltpu.make_async_copy(passing.at[at], target, leave_sem.at[at]))

    def load(step):
        which, first, row, column = steps[step]
        source = (rest_hbm, rest_hbm, up_hbm, down_hbm)[which].at[pl.ds(first, width)]
        return pltpu.make_async_copy(source, narrow.at[step % DEPTH], in_sem.at[step % DEPTH])

    def store(step):
        which, first, row, column = steps[step]
        target = outs[which].at[pl.ds(row, width), pl.ds(column, width)]
        return pltpu.make_async_copy(broad.at[step % DEPTH], target, out_sem.at[step % DEPTH])

    for step in range(DEPTH):
        load(step).start()
    for item in arrivals:
        item.start()
    values = vectors[...].astype(jnp.float32)
    for row in range(3):
        gains[row] = values[row : row + 1]
    for row in range(7):
        shifts[row] = values[3 + row : 4 + row]
    wide = hidden_gains.shape[1] // width
    for block in range(wide):
        cols = slice(block * width, (block + 1) * width)
        hidden_gains[:, cols] = values[10 + block : 11 + block]
        for row in range(2):
            first = 10 + (row + 1) * wide + block
            hidden_shifts[row : row + 1, cols] = values[first : first + 1]
    for step in range(len(steps)):
        load(step).wait()
        if step >= DEPTH:
            store(step - DEPTH).wait()
        broad[step % DEPTH] = narrow[step % DEPTH].astype(jnp.float32)
        store(step).start()
        if step + DEPTH < len(steps):
            load(step + DEPTH).start()
        if step == DEPTH:
            for arrival, departure in zip(arrivals, departures):
                arrival.wait()
                departure.start()
    for step in range(len(steps) - DEPTH, len(steps)):
        store(step).wait()
    for item in departures:
        item.wait()


def finish(down, up, rest, vectors, slots_out, slots_grad, hidden):
    width = rest.shape[1]
    wide = hidden // width
    count = len(slots_out)
    half_rows = down.shape[0] // 2
    firsts = [block_row(block, width, hidden, half_rows) for block in range(wide)]
    steps = [(3, firsts[block], block * width, 0) for block in range(wide)]
    steps += [(2, firsts[block], 0, block * width) for block in range(wide)]
    steps += [(0, firsts[block], 0, block * width) for block in range(3)]
    steps.append((1, firsts[3], 0, 0))
    f = jnp.float32
    shapes = [(width, 3 * width), (width, width), (width, hidden), (hidden, width)]
    shapes += [(3, 1, width), (7, 1, width), (1, hidden), (2, hidden)]
    any_spec = pl.BlockSpec(memory_space=pl.ANY)
    vmem_spec = pl.BlockSpec(memory_space=pltpu.VMEM)
    out_shape = [jax.ShapeDtypeStruct(shape, f) for shape in shapes]
    pile = jax.ShapeDtypeStruct((count,) + slots_out[0].shape, slots_out[0].dtype)
    return pl.pallas_call(
        functools.partial(finish_kernel, tuple(steps), count),
        out_shape=out_shape + [pile, pile],
        in_specs=[any_spec] * 3 + [vmem_spec] + [any_spec] * (2 * count),
        out_specs=[any_spec] * 4 + [vmem_spec] * 4 + [any_spec] * 2,
        scratch_shapes=[
            pltpu.VMEM((DEPTH, width, width), jnp.bfloat16),
            pltpu.VMEM((DEPTH, width, width), f),
            pltpu.VMEM((2 * count,) + slots_out[0].shape, slots_out[0].dtype),
            pltpu.SemaphoreType.DMA((DEPTH,)),
            pltpu.SemaphoreType.DMA((DEPTH,)),
            pltpu.SemaphoreType.DMA((2 * count,)),
            pltpu.SemaphoreType.DMA((2 * count,)),
        ],
        compiler_params=pltpu.CompilerParams(vmem_limit_bytes=VMEM_BYTES),
    )(down, up, rest, vectors, *slots_out, *slots_grad)


def passed_along(block, axis, distance):
    devices = range(lax.axis_size(axis))
    route = [(i - distance, i) for i in devices if i - distance in devices]
    return lax.ppermute(block, axis, route)


def shards(
    inputs,
    cotangent,
    lengths,
    assign,
    query_key_value,
    out_weight,
    up_weight,
    down_weight,
    model_gains,
    model_shifts,
    hidden_gains,
    hidden_shifts,
):
    micro_count = inputs.shape[0]
    hidden = up_weight.shape[2]
    slots = range(micro_count)
    weights = {
        N.wq: query_key_value[0],
        N.wo: out_weight[0],
        N.wu: up_weight[0],
        N.wd: down_weight[0],
    }
    by_row = [jnp.transpose(item, (1, 0, 2)) for item in (model_gains, model_shifts)]
    vectors = (*by_row, hidden_gains, hidden_shifts)

    sizes = (lengths, assign)

    def run(steps, plane, slot, given, previous, after=()):
        return layer_call(
            steps, plane, slot, sizes, {**weights, **given}, vectors, previous, after
        )

    lower, upper = [], []
    for slot in slots:
        after = [lower[-1][N.spread]] if lower else []
        lower.append(run((N.forward,), 0, slot, {N.x: inputs}, {}, after))
    middle = [passed_along(lower[slot][N.y], "pipe", 1) for slot in slots]
    for slot in slots:
        after = [upper[-1][N.sums]] if upper else []
        given = {N.x: middle[slot], N.dy: cotangent}
        upper.append(run((N.forward, N.backward), 1, slot, given, lower[slot], after))
    returned = [passed_along(upper[slot][N.dx], "pipe", -1) for slot in slots]
    kept = [{**lower[slot], **upper[slot]} for slot in slots]
    devices = lax.axis_size("batch")
    first, final = slots
    given = {**kept[first], N.x: inputs, N.dy: returned[first]}
    first_grads = run((N.backward,), 0, first, given, kept[first])
    base_down, base_rest = weight_grads(kept[first], first_grads)
    width = inputs.shape[2]
    half_rows = chunk_rows(width, hidden, devices) * (devices // 2)
    given = {**kept[final], N.x: inputs, N.dy: returned[final]}
    if 2 * half_rows == hidden:
        dx, *sums, vector_sum = tail_call(
            final,
            sizes,
            {**weights, **given},
            vectors,
            kept[final],
            upper[final],
            first_grads[N.sums],
            (base_down, base_rest),
            devices,
        )
    else:
        final_grads = run((N.backward,), 0, final, given, kept[final])
        dx = final_grads[N.dx]
        last_down, last_rest = weight_grads(kept[final], final_grads)
        parts = []
        for pair in ((base_down, base_rest), (last_down, last_rest)):
            packed = jnp.concatenate(pair, axis=0)
            missing = -packed.shape[0] % (TILE * devices)
            parts.append(jnp.pad(packed, ((0, missing), (0, 0))))
        packed, vector_sum = ring_sum(parts, [first_grads[N.sums], final_grads[N.sums]], devices)
        packed = packed.reshape(-1, width)
        ends = (hidden, hidden + 4 * width, 2 * hidden + 4 * width)
        sums = (packed[: ends[0]], packed[ends[1] : ends[2]], packed[ends[0] : ends[1]])
    outs = finish(
        *[item.reshape(-1, width) for item in sums],
        vector_sum,
        [kept[slot][N.y] for slot in slots],
        [first_grads[N.dx], dx],
        hidden,
    )
    by_row = [jnp.transpose(item, (1, 0, 2)) for item in outs[4:6]]
    return (*[item[None] for item in outs[8:] + outs[:4]], *by_row, outs[6], outs[7][None])


def solution(mesh):
    return jax.shard_map(
        shards,
        mesh=mesh,
        in_specs=(
            P(None, "batch", None),
            P(None, "batch", None),
            P("batch"),
            P("batch"),
            P("pipe", None, None),
            P("pipe", None, None),
            P("pipe", None, None),
            P("pipe", None, None),
            P("pipe", None, None),
            P("pipe", None, None),
            P("pipe", None),
            P("pipe", None, None),
        ),
        out_specs=(
            P("pipe", None, "batch", None),
            P("pipe", None, "batch", None),
            P("pipe", None, None),
            P("pipe", None, None),
            P("pipe", None, None),
            P("pipe", None, None),
            P("pipe", None, None),
            P("pipe", None, None),
            P("pipe", None),
            P("pipe", None, None),
        ),
        check_vma=False,
    )
```
